32 devices in a mesh: dp: 16 (over z, y, core), tensor: 2 (over x).
Axes of the slice: x: 2, y: 2, z: 4, core: 2. Of those that a mesh axis runs over, the one named last changes fastest.
Arguments:
- tokens: bfloat16 [18432, 1024], P(('dp', 'tensor')), may hold values from -6 to 6
- cotangent: bfloat16 [18432, 1024], P(('dp', 'tensor')), may hold values from -6 to 6
- lengths: int32 [16, 3], P('dp'), may hold values from 1 to 1024, 1152 in all within a row
- qkv_weight: float32 [1024, 3, 1024], P('dp', None, 'tensor'), may hold values from -0.1875 to 0.1875
- proj_weight: float32 [1024, 1024], P('tensor', 'dp'), may hold values from -1.5 to 1.5
- up_weight: float32 [1024, 4096], P('dp', 'tensor'), may hold values from -0.1875 to 0.1875
- down_weight: float32 [4096, 1024], P('tensor', 'dp'), may hold values from -0.09375 to 0.09375
- small_params: float32 [13, 1024], P(None, ('dp', 'tensor')), may hold values from -1.2 to 1.4
- qkv_first: float32 [1024, 3, 1024], P('dp', None, 'tensor'), may hold values from -48 to 48
- proj_first: float32 [1024, 1024], P('tensor', 'dp'), may hold values from -8 to 8
- up_first: float32 [1024, 4096], P('dp', 'tensor'), may hold values from -28 to 28
- down_first: float32 [4096, 1024], P('tensor', 'dp'), may hold values from -64 to 64
- small_first: float32 [13, 1024], P(None, ('dp', 'tensor')), may hold values from -96 to 96
- qkv_second: float32 [1024, 3, 1024], P('dp', None, 'tensor'), may hold values from 258.048 to 1013.76
- proj_second: float32 [1024, 1024], P('tensor', 'dp'), may hold values from 10.1376 to 40.5504
- up_second: float32 [1024, 4096], P('dp', 'tensor'), may hold values from 92.16 to 368.64
- down_second: float32 [4096, 1024], P('tensor', 'dp'), may hold values from 497.664 to 1990.656
- small_second: float32 [13, 1024], P(None, ('dp', 'tensor')), may hold values from 1013.76 to 4055.04
Outputs:
- block_out: bfloat16 [18432, 1024], P(('dp', 'tensor'))
- token_grad: float32 [18432, 1024], P(('dp', 'tensor'))
- qkv_first_new: float32 [1024, 3, 1024], P('dp', None, 'tensor')
- qkv_second_new: float32 [1024, 3, 1024], P('dp', None, 'tensor')
- qkv_weight_new: float32 [1024, 3, 1024], P('dp', None, 'tensor')
- proj_first_new: float32 [1024, 1024], P('tensor', 'dp')
- proj_second_new: float32 [1024, 1024], P('tensor', 'dp')
- proj_weight_new: float32 [1024, 1024], P('tensor', 'dp')
- up_first_new: float32 [1024, 4096], P('dp', 'tensor')
- up_second_new: float32 [1024, 4096], P('dp', 'tensor')
- up_weight_new: float32 [1024, 4096], P('dp', 'tensor')
- down_first_new: float32 [4096, 1024], P('tensor', 'dp')
- down_second_new: float32 [4096, 1024], P('tensor', 'dp')
- down_weight_new: float32 [4096, 1024], P('tensor', 'dp')
- small_first_new: float32 [13, 1024], P(None, ('dp', 'tensor'))
- small_second_new: float32 [13, 1024], P(None, ('dp', 'tensor'))
- small_params_new: float32 [13, 1024], P(None, ('dp', 'tensor'))
The draws below stay inside these ranges and needn't reach their ends.
Inputs may be any that keep to these rules, and one draw needn't show every extreme that they name: `lengths`: each row sums to 1152 and its largest entry is exactly 1024.
All inputs are finite; a program needn't handle non-finite values.
Results may differ from the reference program's by a relative error of at most 0.02.
Values may be sent and summed in bfloat16 or wider, within the bound.
No kernel may reach another device: no remote copies, remote signals or barrier semaphores. Data moves between devices by JAX's collectives and lax.ppermute only.
A program may use at most 192 MiB of HBM per device.

```python
import math
import jax
import jax.numpy as jnp
import numpy as np
from jax import lax

D = 1024
HEADS = 16
HD = 64
FF = 4096
ROT = 16
TOK_GRP = 1152
MAXLEN = 1024
STEP = 10
SEQS = 3
TOKENS = 18432
N_DP = 16


def draw_small_params(key, part):
    key = jax.random.fold_in(key, 7)
    biases = 0.3 * jax.random.normal(jax.random.fold_in(key, 1), (13, D), jnp.float32)
    biases = jnp.clip(biases, -1.2, 1.2)
    gains = jax.random.uniform(jax.random.fold_in(key, 2), (13, D), jnp.float32, 0.6, 1.4)
    row_id = jnp.arange(13)[:, None]
    return jnp.where((row_id == 0) | (row_id == 2), gains, biases)


def with_spikes(entries, own_key, source, target, shards_of, factor):
    owner, partner = [(jnp.arange(entries.shape[dim]) // (entries.shape[dim] // shards_of)).reshape([-1 if axis == dim else 1 for axis in range(entries.ndim)]) for dim in (source, target)]
    chosen = jax.random.permutation(own_key, shards_of)[partner]
    strong = (owner == chosen) | (owner == (partner + shards_of // 2) % shards_of)
    return jnp.where(strong, factor * entries, entries)


def level_of(own_key, extent, shards, smallest, high):
    level = 1.0
    for dim, blocks in shards:
        steps = jax.random.uniform(jax.random.fold_in(jax.random.fold_in(own_key, 6), dim), (blocks,), jnp.float32, smallest / len(shards), high / len(shards))
        level = level * jnp.repeat(jnp.exp(steps), extent[dim] // blocks).reshape((-1,) + (1,) * (len(extent) - 1 - dim))
    return level


def split_up(count, total, limit, skew):
    loads = [(1 << 20) // math.isqrt(standing ** skew) + 1 for standing in range(2, count + 1)]
    spare, counts = total - limit - (count - 1), [1] * (count - 1)
    while spare > 0:
        movable = [i for i in range(count - 1) if counts[i] < limit]
        mass, budget = sum([loads[i] for i in movable]), spare
        for i in movable:
            extra = min(limit - counts[i], max(1, budget * loads[i] // mass), spare)
            counts[i] = counts[i] + extra
            spare = spare - extra
    return np.array([limit] + counts)


def ragged_sizes(rng, count, total, reach, lean):
    if count == 2:
        one = jax.random.randint(rng, (), max(1, total - reach), min(reach, total - 1) + 1)
        return jnp.stack([one, total - one])
    tallies = jnp.asarray(split_up(count, total, reach, lean), jnp.int32)
    couples = (count - 1) // 2
    source_of, receiver = tallies[1:1 + 2 * couples:2], tallies[2:2 + 2 * couples:2]
    margin = jnp.minimum(source_of - 1, reach - receiver)
    passed = jax.random.randint(jax.random.fold_in(rng, 1), (couples,), 0, 1 << 20) % (margin + 1)
    tallies = tallies.at[1:1 + 2 * couples:2].set(source_of - passed).at[2:2 + 2 * couples:2].set(receiver + passed)
    return tallies[jax.random.permutation(jax.random.fold_in(rng, 2), count)]


def scatter_about(own_key, shape, deviation, reach, cuts=(), held_as=jnp.bfloat16):
    entries = jax.random.normal(own_key, shape, jnp.float32) * deviation
    if len(cuts) > 0:
        entries = level_of(own_key, shape, cuts, -0.22, 0.18) * entries
    return jnp.clip(entries, min=-reach, max=reach).astype(held_as)


def gaussian_with(key, shape, spread, limit, cuts, heavy, kind=jnp.bfloat16):
    result = spread * jax.random.normal(key, shape, jnp.float32)
    if cuts:
        result = result * level_of(key, shape, cuts, -0.22, 0.18)
    return jnp.clip(with_spikes(result, jax.random.fold_in(key, 3), *heavy), -limit, limit).astype(kind)


def setup_inputs(seed: int = 0) -> dict:
    key_list = jax.random.split(jax.random.key(seed), 19)
    return {
        "tokens": scatter_about(key_list[0], (TOKENS, D), 1.0, 6.0, ((0, 32),)),
        "cotangent": gaussian_with(key_list[1], (TOKENS, D), 1.0, 6.0, ((0, 32),), (0, 1, 32, 2.75)),
        "lengths": jax.vmap(lambda own: ragged_sizes(own, SEQS, TOK_GRP, MAXLEN, 2))(jax.random.split(key_list[2], N_DP)).reshape((N_DP, SEQS)).astype(jnp.int32),
        "qkv_weight": scatter_about(key_list[3], (D, 3, D), D ** -0.5, 0.1875, ((0, 16), (2, 2)), jnp.float32),
        "proj_weight": scatter_about(key_list[4], (D, D), (D // 64) ** -0.5, 1.5, ((0, 2), (1, 16)), jnp.float32),
        "up_weight": scatter_about(key_list[5], (D, FF), D ** -0.5, 0.1875, ((0, 16), (1, 2)), jnp.float32),
        "down_weight": scatter_about(key_list[6], (FF, D), FF ** -0.5, 0.09375, ((0, 2), (1, 16)), jnp.float32),
        "small_params": draw_small_params(jax.random.fold_in(key_list[18], 71), 0),
        "qkv_first": scatter_about(key_list[8], (D, 3, D), (0.055 * TOKENS ** 0.5), 48.0, ((0, 16), (2, 2)), jnp.float32),
        "proj_first": scatter_about(key_list[9], (D, D), (0.011 * TOKENS ** 0.5), 8.0, ((0, 2), (1, 16)), jnp.float32),
        "up_first": scatter_about(key_list[10], (D, FF), (0.033 * TOKENS ** 0.5), 28.0, ((0, 16), (1, 2)), jnp.float32),
        "down_first": scatter_about(key_list[11], (FF, D), (0.077 * TOKENS ** 0.5), 64.0, ((0, 2), (1, 16)), jnp.float32),
        "small_first": scatter_about(key_list[12], (13, D), (0.11 * TOKENS ** 0.5), 96.0, ((1, 32),), jnp.float32),
        "qkv_second": jnp.clip(jnp.exp(math.log(1013.76) - 1.36827585 * jax.random.uniform(key_list[13], (D, 3, D), jnp.float32) ** level_of(key_list[13], (D, 3, D), ((0, 16), (2, 2)), -0.2, 0.2)), 258.048, 1013.76),
        "proj_second": jnp.clip(jnp.exp(math.log(40.5504) - 1.3862944 * jax.random.uniform(key_list[14], (D, D), jnp.float32) ** level_of(key_list[14], (D, D), ((0, 2), (1, 16)), -0.2, 0.2)), 10.1376, 40.5504),
        "up_second": jnp.clip(jnp.exp(math.log(368.64) - 1.3862944 * jax.random.uniform(key_list[15], (D, FF), jnp.float32) ** level_of(key_list[15], (D, FF), ((0, 16), (1, 2)), -0.2, 0.2)), 92.16, 368.64),
        "down_second": jnp.clip(jnp.exp(math.log(1990.656) - 1.3862944 * jax.random.uniform(key_list[16], (FF, D), jnp.float32) ** level_of(key_list[16], (FF, D), ((0, 2), (1, 16)), -0.2, 0.2)), 497.664, 1990.656),
        "small_second": jnp.clip(jnp.exp(math.log(4055.04) - 1.3862944 * jax.random.uniform(key_list[17], (13, D), jnp.float32) ** level_of(key_list[17], (13, D), ((1, 32),), -0.2, 0.2)), 1013.76, 4055.04),
    }


EPS_NORM = 1e-05
BETA_ONE = 0.9
BETA_TWO = 0.95
EPS_ADAM = 1e-08
DECAY = 0.01
SMALL_RATE = 0.3
PRECISE = lax.Precision.HIGHEST

@jax.custom_vjp
def reduced_precision(v):
    return lax.optimization_barrier(v.astype(jnp.bfloat16)).astype(jnp.float32)

@jax.custom_vjp
def low_back(v):
    return v

def low_keep(v):
    return (reduced_precision(v), None)

def low_pass(kept, grad):
    return (grad,)

def back_keep(v):
    return (v, None)

def back_low(kept, grad):
    return (reduced_precision(grad),)
reduced_precision.defvjp(low_keep, low_pass)
low_back.defvjp(back_keep, back_low)

def layout(lengths_row, row_count):
    starts = jnp.cumsum(lengths_row) - lengths_row
    row_index = jnp.arange(row_count, dtype=jnp.int32)
    member = (row_index[:, None] >= starts[None, :]).astype(jnp.int32)
    sequence = lax.optimization_barrier(jnp.sum(member, axis=1)) - 1
    onehot = (sequence[:, None] == jnp.arange(lengths_row.shape[0], dtype=jnp.int32)[None, :]).astype(jnp.int32)
    position = row_index - lax.optimization_barrier(jnp.sum(onehot * starts[None, :], axis=1))
    return (sequence, position)

def rotary_tables(position, rot_dims):
    half_rot = rot_dims // 2
    frequency = 10000.0 ** (-(2.0 * jnp.arange(half_rot, dtype=jnp.float32)) / rot_dims)
    angles = position.astype(jnp.float32)[:, None] * frequency[None, :]
    angles = jnp.concatenate([angles, angles], axis=1)
    return (jnp.cos(angles), jnp.sin(angles))

def rotate(tensor, cosine, sine_table):
    rot_dims = cosine.shape[1]
    half_rot = rot_dims // 2
    rotated = tensor[..., :rot_dims]
    turned = jnp.concatenate([-rotated[..., half_rot:], rotated[..., :half_rot]], axis=-1)
    rotated = rotated * cosine[:, None, :] + turned * sine_table[:, None, :]
    return jnp.concatenate([rotated, tensor[..., rot_dims:]], axis=-1)

def apply_layer_norm(layer_inputs):
    average = lax.optimization_barrier(jnp.mean(layer_inputs, axis=-1, keepdims=True))
    centred = layer_inputs - average
    variance = lax.optimization_barrier(jnp.mean(centred * centred, axis=-1, keepdims=True))
    inverse_deviation = lax.rsqrt(variance + EPS_NORM)
    return (centred * inverse_deviation, inverse_deviation)

def group_forward(layer_inputs, lengths_row, qkv_weight, proj_weight, up_weight, down_weight, small_parameters):
    row_count = layer_inputs.shape[0]
    sequence, position = layout(lengths_row, row_count)
    cosine, sine_table = rotary_tables(position, ROT)
    centered_whitened, inverse_deviation = apply_layer_norm(layer_inputs)
    attention_normed_rows = reduced_precision(centered_whitened * small_parameters[0] + small_parameters[1])
    feedforward_normed_rows = reduced_precision(centered_whitened * small_parameters[2] + small_parameters[3])
    qkv_pre = jnp.dot(attention_normed_rows, reduced_precision(qkv_weight).reshape(D, 3 * D), precision=PRECISE) + small_parameters[4:7].reshape(3 * D)
    qkv_pre = low_back(qkv_pre).reshape(row_count, 3, HEADS, HD)
    queries = reduced_precision(rotate(qkv_pre[:, 0], cosine, sine_table))
    key_rows = reduced_precision(rotate(qkv_pre[:, 1], cosine, sine_table))
    value_rows = reduced_precision(qkv_pre[:, 2])
    row_index = jnp.arange(row_count, dtype=jnp.int32)
    allowed = (sequence[:, None] == sequence[None, :]) & (row_index[None, :] <= row_index[:, None])

    def one_head(pieces):
        query_head, key_head, value_head = pieces
        scores = low_back(jnp.dot(query_head, key_head.T, precision=PRECISE) * HD ** (-0.5))
        scores = jnp.where(allowed, scores, -1e+30)
        probs = reduced_precision(jax.nn.softmax(scores, axis=-1))
        return jnp.dot(probs, value_head, precision=PRECISE)
    head_out = lax.map(jax.checkpoint(one_head), (queries.transpose(1, 0, 2), key_rows.transpose(1, 0, 2), value_rows.transpose(1, 0, 2)))
    attended = reduced_precision(low_back(head_out.transpose(1, 0, 2).reshape(row_count, D)))
    hidden_pre = low_back(jnp.dot(feedforward_normed_rows, reduced_precision(up_weight), precision=PRECISE) + small_parameters[8:12].reshape(FF))
    hidden = reduced_precision(jax.nn.gelu(hidden_pre, approximate=False))
    attn_branch = jnp.dot(attended, reduced_precision(proj_weight), precision=PRECISE) + small_parameters[7]
    mlp_branch = jnp.dot(hidden, reduced_precision(down_weight), precision=PRECISE) + small_parameters[12]
    return layer_inputs + attn_branch + mlp_branch

def adamw(weight, moment, second, gradient, step_rate, decay_rate):
    moment = BETA_ONE * moment + (1.0 - BETA_ONE) * gradient
    second = BETA_TWO * second + (1.0 - BETA_TWO) * gradient * gradient
    moment_hat = moment / (1.0 - BETA_ONE ** STEP)
    second_hat = second / (1.0 - BETA_TWO ** STEP)
    weight = weight - step_rate * (moment_hat / (jnp.sqrt(second_hat) + EPS_ADAM) + decay_rate * weight)
    return (moment, second, weight)

def reference(tokens, cotangent, lengths, qkv_weight, proj_weight, up_weight, down_weight, small_params, qkv_first, proj_first, up_first, down_first, small_first, qkv_second, proj_second, up_second, down_second, small_second):
    layer_inputs = tokens.astype(jnp.float32).reshape(N_DP, TOK_GRP, D)

    def forward(layer_inputs, qkv_w, proj_w, up_w, down_w, small_parameters):

        def one_group(pieces):
            return group_forward(pieces[0], pieces[1], qkv_w, proj_w, up_w, down_w, small_parameters)
        return lax.map(jax.checkpoint(one_group), (layer_inputs, lengths))
    outputs, pullback = jax.vjp(forward, layer_inputs, qkv_weight, proj_weight, up_weight, down_weight, small_params)
    gradients = pullback(cotangent.astype(jnp.float32).reshape(N_DP, TOK_GRP, D))
    block_out = outputs.reshape(TOKENS, D).astype(jnp.bfloat16)
    token_grad = gradients[0].reshape(TOKENS, D)
    qkv_new = adamw(qkv_weight, qkv_first, qkv_second, gradients[1], D ** (-0.5), DECAY)
    proj_new = adamw(proj_weight, proj_first, proj_second, gradients[2], (D // 64) ** (-0.5), DECAY)
    up_new = adamw(up_weight, up_first, up_second, gradients[3], D ** (-0.5), DECAY)
    down_new = adamw(down_weight, down_first, down_second, gradients[4], FF ** (-0.5), DECAY)
    small_new = adamw(small_params, small_first, small_second, gradients[5], SMALL_RATE, 0.0)
    return (block_out, token_grad, qkv_new[0], qkv_new[1], qkv_new[2], proj_new[0], proj_new[1], proj_new[2], up_new[0], up_new[1], up_new[2], down_new[0], down_new[1], down_new[2], small_new[0], small_new[1], small_new[2])
```

```python
import functools
import math

import jax
import jax.numpy as jnp
from jax import lax
from jax.experimental import pallas as pl
from jax.experimental.pallas import tpu as pltpu
from jax.sharding import PartitionSpec as P

D = 1024
HD = 64
FF = 4096
ROT = 16
STEP = 10

EPS_NORM = 1e-05
BETA_ONE = 0.9
BETA_TWO = 0.95
EPS_ADAM = 1e-08
DECAY = 0.01
SMALL_RATE = 0.3
BFLOAT = jnp.bfloat16
FLOAT = jnp.float32
ROOT_HALF = 1.0 / math.sqrt(2.0)
INV_ROOT_TAU = 1.0 / math.sqrt(2.0 * math.pi)
PAIR = 2 * HD
QB = 128
MASKED = -1e30


def layout(lengths_row, row_count):
    starts = jnp.cumsum(lengths_row) - lengths_row
    row_index = jnp.arange(row_count, dtype=jnp.int32)
    own_start = jnp.max(
        jnp.where(row_index[:, None] >= starts[None, :], starts[None, :], 0), axis=1
    )
    return own_start, row_index - own_start


def rotary_tables(position):
    half = ROT // 2
    lane = jnp.arange(PAIR, dtype=jnp.int32) % HD
    frequency = 10000.0 ** (-(2.0 * jnp.arange(half, dtype=FLOAT)) / ROT)
    angles = position.astype(FLOAT)[:, None] * frequency[None, :]
    cos = jnp.tile(jnp.cos(angles), (1, PAIR // half))
    sin = jnp.tile(jnp.sin(angles), (1, PAIR // half))
    keep = jnp.where(lane[None] < ROT, cos, 1.0)
    from_left = jnp.where((lane[None] >= half) & (lane[None] < ROT), sin, 0.0)
    from_right = jnp.where(lane[None] < half, -sin, 0.0)
    return keep, from_left, from_right


def attention_kernel(
    pre_ref, grad_ref, keep_ref, left_ref, right_ref, start_ref,
    att_ref, dpre_ref,
    q2_ref, g2_ref, k_ref, kt_ref, v_ref, vt_ref, dk_ref, dv_ref,
):
    rows = pre_ref.shape[0]
    blocks = rows // QB
    half = ROT // 2

    def turn(x, sign, at):
        here = pl.ds(at, x.shape[0])
        return (
            x * keep_ref[here, :]
            + sign * (
                pltpu.roll(x, half, 1) * left_ref[here, :]
                + pltpu.roll(x, PAIR - half, 1) * right_ref[here, :]
            )
        )

    first = lax.broadcasted_iota(jnp.int32, (QB, PAIR), 1) < HD
    top = lax.broadcasted_iota(jnp.int32, (PAIR, QB), 0) < HD
    zero = jnp.zeros((QB, PAIR), FLOAT)
    for i in range(blocks):
        here = pl.ds(i * QB, QB)
        q = turn(pre_ref[here, :PAIR].astype(FLOAT), 1.0, i * QB) * (HD ** -0.5)
        q2_ref[pl.ds(2 * i * QB, QB), :] = jnp.where(first, q, zero).astype(BFLOAT)
        q2_ref[pl.ds((2 * i + 1) * QB, QB), :] = jnp.where(first, zero, q).astype(BFLOAT)
        g = grad_ref[here, :].astype(FLOAT)
        g2_ref[pl.ds(2 * i * QB, QB), :] = jnp.where(first, g, zero).astype(BFLOAT)
        g2_ref[pl.ds((2 * i + 1) * QB, QB), :] = jnp.where(first, zero, g).astype(BFLOAT)
        k = turn(pre_ref[here, PAIR:2 * PAIR].astype(FLOAT), 1.0, i * QB)
        k_ref[here, :] = k.astype(BFLOAT)
        kt_ref[:, here] = k.T.astype(BFLOAT)
        v = pre_ref[here, 2 * PAIR:]
        v_ref[here, :] = v
        vt_ref[:, here] = v.astype(FLOAT).T.astype(BFLOAT)

    for i in range(blocks):
        n = (i + 1) * QB
        here = pl.ds(i * QB, QB)
        q2 = q2_ref[pl.ds(2 * i * QB, 2 * QB), :]
        g2 = g2_ref[pl.ds(2 * i * QB, 2 * QB), :]
        s = lax.dot_general(
            k_ref[:n, :], q2, (((1,), (1,)), ((), ())), preferred_element_type=FLOAT
        )
        start = start_ref[:, here]
        start = jnp.concatenate([start, start], axis=1)
        lane = lax.broadcasted_iota(jnp.int32, (QB, 2 * QB), 1)
        row = lax.broadcasted_iota(jnp.int32, (QB, 2 * QB), 0)
        causal = row <= jnp.where(lane < QB, lane, lane - QB)
        tiles = []
        for j in range(i + 1):
            tile = s[j * QB:(j + 1) * QB]
            allowed = None
            if j == 0 or i * QB >= 1024:
                allowed = row + j * QB >= start
            if j == i:
                allowed = causal if allowed is None else allowed & causal
            tiles.append(tile if allowed is None else jnp.where(allowed, tile, MASKED))
        s = jnp.concatenate(tiles, axis=0) if i else tiles[0]
        e = jnp.exp(s - jnp.max(s, axis=0, keepdims=True))
        p = e * (1.0 / jnp.sum(e, axis=0, keepdims=True))
        dp = lax.dot_general(
            v_ref[:n, :], g2, (((1,), (1,)), ((), ())), preferred_element_type=FLOAT
        )
        delta = jnp.sum(dp * p, axis=0, keepdims=True)
        ds = (p * (dp - delta)).astype(BFLOAT)
        p = p.astype(BFLOAT)
        o = jnp.dot(vt_ref[:, :n], p, preferred_element_type=FLOAT)
        o = jnp.where(top, o[:, :QB], o[:, QB:])
        att_ref[here, :] = o.T.astype(BFLOAT)
        dq = jnp.dot(kt_ref[:, :n], ds, preferred_element_type=FLOAT)
        dq = jnp.where(top, dq[:, :QB], dq[:, QB:]) * (HD ** -0.5)
        dpre_ref[here, :PAIR] = turn(dq.T, -1.0, i * QB).astype(BFLOAT)
        dk = jnp.dot(ds, q2, preferred_element_type=FLOAT)
        dv = jnp.dot(p, g2, preferred_element_type=FLOAT)
        if i:
            before = n - QB
            dk_ref[:before, :] += dk[:before]
            dv_ref[:before, :] += dv[:before]
            dk_ref[here, :] = dk[before:]
            dv_ref[here, :] = dv[before:]
        else:
            dk_ref[here, :] = dk
            dv_ref[here, :] = dv

    for i in range(blocks):
        here = pl.ds(i * QB, QB)
        dpre_ref[here, PAIR:2 * PAIR] = turn(dk_ref[here, :], -1.0, i * QB).astype(BFLOAT)
        dpre_ref[here, 2 * PAIR:] = dv_ref[here, :].astype(BFLOAT)


def attention(qkv_pre, d_attended, keep, left, right, start):
    rows, width = d_attended.shape
    pairs = width // PAIR
    whole = lambda p: (0, 0)
    return pl.pallas_call(
        attention_kernel,
        grid=(pairs,),
        in_specs=[
            pl.BlockSpec((rows, 3 * PAIR), lambda p: (0, p)),
            pl.BlockSpec((rows, PAIR), lambda p: (0, p)),
            pl.BlockSpec((rows, PAIR), whole),
            pl.BlockSpec((rows, PAIR), whole),
            pl.BlockSpec((rows, PAIR), whole),
            pl.BlockSpec((1, rows), whole),
        ],
        out_specs=[
            pl.BlockSpec((rows, PAIR), lambda p: (0, p)),
            pl.BlockSpec((rows, 3 * PAIR), lambda p: (0, p)),
        ],
        out_shape=[
            jax.ShapeDtypeStruct((rows, width), BFLOAT),
            jax.ShapeDtypeStruct((rows, 3 * width), BFLOAT),
        ],
        scratch_shapes=[
            pltpu.VMEM((2 * rows, PAIR), BFLOAT),
            pltpu.VMEM((2 * rows, PAIR), BFLOAT),
            pltpu.VMEM((rows, PAIR), BFLOAT),
            pltpu.VMEM((PAIR, rows), BFLOAT),
            pltpu.VMEM((rows, PAIR), BFLOAT),
            pltpu.VMEM((PAIR, rows), BFLOAT),
            pltpu.VMEM((rows, PAIR), FLOAT),
            pltpu.VMEM((rows, PAIR), FLOAT),
        ],
        compiler_params=pltpu.CompilerParams(vmem_limit_bytes=32 * 1024 * 1024),
        cost_estimate=pl.CostEstimate(
            flops=14 * rows * rows * width // 2 * 4,
            bytes_accessed=rows * width * 16 + rows * PAIR * 12,
            transcendentals=rows * rows * (width // HD) // 2,
        ),
        name="attention",
    )(qkv_pre, d_attended, keep, left, right, start)


def flip_kernel(x_ref, o_ref):
    x = x_ref[...]
    pad = jnp.zeros((o_ref.shape[1] - x.shape[0], x.shape[1]), x.dtype)
    o_ref[...] = jnp.concatenate([x, pad], axis=0).T


def flip(x):
    return pl.pallas_call(
        flip_kernel,
        out_shape=jax.ShapeDtypeStruct((PAIR, PAIR), x.dtype),
        name="flip",
    )(x)[:, :x.shape[0]]


def adamw(weight, moment, second, gradient, step_rate, decay_rate):
    moment = BETA_ONE * moment + (1.0 - BETA_ONE) * gradient
    second = BETA_TWO * second + (1.0 - BETA_TWO) * gradient * gradient
    moment_hat = moment / (1.0 - BETA_ONE**STEP)
    second_hat = second / (1.0 - BETA_TWO**STEP)
    weight = weight - step_rate * (
        moment_hat / (jnp.sqrt(second_hat) + EPS_ADAM) + decay_rate * weight
    )
    return (moment, second, weight)


def mm(a, b):
    return jnp.dot(a, b, preferred_element_type=FLOAT)


def mm_nt(a, b):
    return lax.dot_general(a, b, (((1,), (1,)), ((), ())), preferred_element_type=FLOAT)


def mm_tn(a, b):
    return lax.dot_general(a, b, (((0,), (0,)), ((), ())), preferred_element_type=FLOAT)


def turn_order(index, chips):
    if chips == 8:
        return jnp.where(index < 4, 2 * index, 15 - 2 * index)
    return jnp.where(index < chips // 2, index, 3 * chips // 2 - 1 - index)


class Ring:
    def __init__(self, devices):
        self.n = n = devices // 2
        assert n & (n - 1) == 0
        order = [2 * i if i < 4 else 15 - 2 * i for i in range(n)]
        if n != 8:
            order = [i if i < n // 2 else 3 * n // 2 - 1 - i for i in range(n)]
        me = lax.axis_index("dp")
        self.core = me & 1
        chip = lax.shift_right_logical(me, 1)
        if n == 8:
            z = lax.shift_right_logical(chip, 1)
            self.place = jnp.where(chip & 1 == 0, z, 7 - z)
        else:
            self.place = turn_order(chip, n)
        hop = lambda step: [
            (2 * order[i] + k, 2 * order[(i + step) % n] + k) for i in range(n) for k in range(2)
        ]
        self.up_pairs, self.down_pairs = hop(1), hop(n - 1)
        self.twin_pairs = [(2 * c + k, 2 * c + 1 - k) for c in range(n) for k in range(2)]

    def up(self, x):
        return lax.ppermute(x, "dp", self.up_pairs)

    def down(self, x):
        return lax.ppermute(x, "dp", self.down_pairs)

    def twin(self, x):
        return lax.ppermute(x, "dp", self.twin_pairs)

    def chip_at(self, offset):
        return turn_order((self.place + (offset + self.n)) & (self.n - 1), self.n)

    def reduce_scatter(self, grad):
        n, columns = self.n, grad.shape[1]
        rows = grad.shape[0] // (2 * n)
        cut = rows // 2
        parts = grad.reshape(n, 2, rows, columns)
        theirs = lax.dynamic_index_in_dim(parts, 1 - self.core, 1, keepdims=False)
        came = self.twin(theirs)

        def here(offset):
            chip = self.chip_at(offset)
            own = lax.dynamic_slice(parts, (chip, self.core, 0, 0), (1, 1, rows, columns))
            twin = lax.dynamic_slice(came, (chip, 0, 0), (1, rows, columns))
            return own.reshape(rows, columns).astype(FLOAT) + twin[0].astype(FLOAT)

        far = n // 2
        split = here(far)
        going_up = self.up(split[:cut].astype(BFLOAT)).astype(FLOAT)
        going_down = self.down(split[cut:].astype(BFLOAT)).astype(FLOAT)
        for step in range(far - 1, 0, -1):
            up_sum, down_sum = here(step), here(-step)
            if step == far - 1:
                going_up = jnp.concatenate([up_sum[:cut] + going_up, up_sum[cut:]], axis=0)
                going_down = jnp.concatenate([down_sum[:cut], down_sum[cut:] + going_down], axis=0)
            else:
                going_up, going_down = up_sum + going_up, down_sum + going_down
            going_up = self.up(going_up.astype(BFLOAT)).astype(FLOAT)
            going_down = self.down(going_down.astype(BFLOAT)).astype(FLOAT)
        return here(0) + going_up + going_down

    def all_gather(self, shard):
        n = self.n
        rows, columns = shard.shape
        cut = rows // 2
        full = jnp.zeros((n, 2, rows, columns), shard.dtype)

        def put(full, offset, block, core, row):
            return lax.dynamic_update_slice(
                full, block[None, None], (self.chip_at(offset), core, row, 0)
            )

        def put_both(full, offset, block, row=0):
            full = put(full, offset, block, self.core, row)
            return put(full, offset, self.twin(block), 1 - self.core, row)

        full = put_both(full, 0, shard)
        from_below, from_above = shard, shard
        for step in range(1, n // 2):
            from_below, from_above = self.up(from_below), self.down(from_above)
            full = put_both(full, -step, from_below)
            full = put_both(full, step, from_above)
        full = put_both(full, n // 2, self.up(from_below[:cut]))
        full = put_both(full, n // 2, self.down(from_above[cut:]), cut)
        return full.reshape(2 * n * rows, columns)


def swap(x):
    return lax.ppermute(x, "tensor", [(0, 1), (1, 0)])


def gather_rows(part, ways, axis=0):
    if ways != 2:
        return lax.all_gather(part, "tensor", axis=axis, tiled=True)
    came = swap(part)
    first = lax.axis_index("tensor") == 0
    return jnp.concatenate(
        [jnp.where(first, part, came), jnp.where(first, came, part)], axis=axis
    )


def scatter_rows(pieces, ways):
    if ways == 2:
        return swap(pieces[0].astype(BFLOAT)).astype(FLOAT) + pieces[1]
    return lax.psum_scatter(
        pieces[0].astype(BFLOAT), "tensor", scatter_dimension=0, tiled=True
    ).astype(FLOAT)


def per_device(
    ways, groups,
    tokens, cotangent, lengths,
    qkv_weight, proj_weight, up_weight, down_weight, small_params,
    qkv_first, proj_first, up_first, down_first, small_first,
    qkv_second, proj_second, up_second, down_second, small_second,
):
    ring = Ring(groups)
    tensor_rank = lax.axis_index("tensor")
    in_rows = qkv_weight.shape[0]
    local_width = qkv_weight.shape[2]
    hidden_width = up_weight.shape[1]
    pairs = local_width // PAIR
    own_rows = tokens.shape[0]
    row_count = own_rows * ways
    small_rows = small_params.shape[0]
    qkv_width = 3 * local_width
    att_width = qkv_width + local_width

    def pair_major(t):
        return (
            t.reshape(t.shape[0], 3, pairs, PAIR)
            .transpose(0, 2, 1, 3)
            .reshape(t.shape[0], qkv_width)
        )

    def from_pair_major(t):
        return (
            t.reshape(t.shape[0], pairs, 3, PAIR)
            .transpose(0, 2, 1, 3)
            .reshape(t.shape[0], 3, local_width)
        )

    small_here = gather_rows(small_params, ways, axis=1).T
    small_high = lax.reduce_precision(small_here, 8, 7)
    small_shard = jnp.concatenate(
        [
            small_high.astype(BFLOAT),
            (small_here - small_high).astype(BFLOAT),
            jnp.zeros((in_rows, PAIR - 2 * small_rows), BFLOAT),
        ],
        axis=1,
    )
    att_shard = jnp.concatenate(
        [pair_major(qkv_weight.astype(BFLOAT)), proj_weight.T.astype(BFLOAT), small_shard], axis=1
    )
    mlp_shard = jnp.concatenate(
        [up_weight.astype(BFLOAT), down_weight.T.astype(BFLOAT)], axis=1
    )
    rows_in = gather_rows(tokens, ways)
    later_cotangent, rows_in = lax.optimization_barrier((cotangent, rows_in))
    dy = gather_rows(later_cotangent, ways)
    att_full = ring.all_gather(att_shard)
    mlp_full = lax.all_gather(mlp_shard, "dp", axis=0, tiled=True)
    qkv_full, proj_t = att_full[:, :qkv_width], att_full[:, qkv_width:att_width]
    small = att_full[:, att_width:att_width + 2 * small_rows].astype(FLOAT).T
    small = small[:small_rows] + small[small_rows:]

    bias_qkv = pair_major(
        lax.dynamic_slice_in_dim(small[4:7], tensor_rank * local_width, local_width, 1)[None]
    )[0]
    bias_up = lax.dynamic_slice_in_dim(
        small[8:12].reshape(4 * D), tensor_rank * hidden_width, hidden_width, 0
    )

    inputs = rows_in.astype(FLOAT)
    average = jnp.mean(inputs, axis=-1, keepdims=True)
    centred = inputs - average
    variance = jnp.mean(centred * centred, axis=-1, keepdims=True)
    inv_dev = lax.rsqrt(variance + EPS_NORM)
    xhat = centred * inv_dev
    normed_a = (xhat * small[0] + small[1]).astype(BFLOAT)
    normed_m = (xhat * small[2] + small[3]).astype(BFLOAT)

    start, position = layout(lengths[0], row_count)
    keep, left, right = rotary_tables(position)

    own_at = tensor_rank * own_rows
    cuts = [(own_rows - own_at, own_rows), (own_at, own_rows)] if ways == 2 else [(0, row_count)]
    rows_of = lambda t, cut: lax.dynamic_slice_in_dim(t, cut[0], cut[1], 0)

    qkv_pre = (mm(normed_a, qkv_full) + bias_qkv).astype(BFLOAT)
    d_attended = mm(dy, proj_t).astype(BFLOAT)
    attended, d_qkv = attention(qkv_pre, d_attended, keep, left, right, start[None])
    proj_grad = mm_tn(dy, attended)
    qkv_grad = mm_tn(normed_a, d_qkv)
    qkv_bias_grad = jnp.sum(d_qkv, axis=0, dtype=FLOAT)
    att_grad = jnp.concatenate([qkv_grad.astype(BFLOAT), proj_grad.astype(BFLOAT)], axis=1)
    att_grad, mlp_full = lax.optimization_barrier((att_grad, mlp_full))
    att_own = lax.psum_scatter(att_grad, "dp", scatter_dimension=0, tiled=True).astype(FLOAT)

    up_full, down_t = mlp_full[:, :hidden_width], mlp_full[:, hidden_width:]
    hidden_pre = mm(normed_m, up_full) + bias_up
    cdf = 0.5 * (1.0 + lax.erf(hidden_pre * ROOT_HALF))
    density = jnp.exp(-0.5 * hidden_pre * hidden_pre) * INV_ROOT_TAU
    hidden = (hidden_pre * cdf).astype(BFLOAT)
    d_pre = (mm(dy, down_t) * (cdf + hidden_pre * density)).astype(BFLOAT)
    up_bias_grad = jnp.sum(d_pre, axis=0, dtype=FLOAT)

    summed = scatter_rows(
        [mm_nt(rows_of(attended, c), proj_t) + mm_nt(rows_of(hidden, c), down_t) for c in cuts],
        ways,
    )
    own_inputs = tokens.astype(FLOAT)
    block_out = (own_inputs + summed + small[7] + small[12]).astype(BFLOAT)

    d_a = [mm_nt(rows_of(d_qkv, c), qkv_full) for c in cuts]
    d_m = [mm_nt(rows_of(d_pre, c), up_full) for c in cuts]
    e_own = scatter_rows([a * small[0] + m * small[2] for a, m in zip(d_a, d_m)], ways)
    own_hat = rows_of(xhat, (own_at, own_rows))
    own_inv = rows_of(inv_dev, (own_at, own_rows))
    token_grad = cotangent.astype(FLOAT) + own_inv * (
        e_own
        - jnp.mean(e_own, axis=-1, keepdims=True)
        - own_hat * jnp.mean(e_own * own_hat, axis=-1, keepdims=True)
    )

    out_bias_grad = jnp.sum(cotangent, axis=0, dtype=FLOAT)
    qkv_rows = lax.dynamic_update_slice_in_dim(
        jnp.zeros((3, D), FLOAT),
        from_pair_major(qkv_bias_grad[None])[0],
        tensor_rank * local_width,
        1,
    )
    up_rows = lax.dynamic_update_slice_in_dim(
        jnp.zeros((4 * D,), FLOAT), up_bias_grad, tensor_rank * hidden_width, 0
    )
    with_hat = lambda ds: sum(
        jnp.sum(d * rows_of(xhat, c), axis=0)[None] for d, c in zip(ds, cuts)
    )
    plain = lambda ds: sum(jnp.sum(d, axis=0)[None] for d in ds)
    small_local = jnp.concatenate(
        [
            with_hat(d_a),
            plain(d_a),
            with_hat(d_m),
            plain(d_m),
            qkv_rows,
            out_bias_grad[None],
            up_rows.reshape(4, D),
            out_bias_grad[None],
        ],
        axis=0,
    )
    small_both = small_local + swap(small_local) if ways == 2 else lax.psum(small_local, "tensor")
    small_columns = jnp.pad(small_both.T, ((0, 0), (0, PAIR - small_rows))).astype(BFLOAT)

    down_own = ring.reduce_scatter(mm_tn(dy, hidden).astype(BFLOAT))
    up_own = ring.reduce_scatter(
        jnp.concatenate([mm_tn(normed_m, d_pre).astype(BFLOAT), small_columns], axis=1)
    )
    small_width = small_params.shape[1]
    small_grad = lax.dynamic_slice_in_dim(
        flip(up_own[:, hidden_width:])[:small_rows],
        tensor_rank * small_width,
        small_width,
        1,
    )
    qkv_owned = from_pair_major(att_own[:, :qkv_width])
    proj_owned = att_own[:, qkv_width:].T
    up_owned = up_own[:, :hidden_width]
    down_owned = down_own.T
    qkv_new = adamw(qkv_weight, qkv_first, qkv_second, qkv_owned, D ** (-0.5), DECAY)
    proj_new = adamw(proj_weight, proj_first, proj_second, proj_owned, (D // 64) ** (-0.5), DECAY)
    up_new = adamw(up_weight, up_first, up_second, up_owned, D ** (-0.5), DECAY)
    down_new = adamw(down_weight, down_first, down_second, down_owned, FF ** (-0.5), DECAY)
    small_new = adamw(small_params, small_first, small_second, small_grad, SMALL_RATE, 0.0)
    return (block_out, token_grad) + qkv_new + proj_new + up_new + down_new + small_new


def solution(mesh):
    rows = P(("dp", "tensor"), None)
    weights = (P("dp", None, "tensor"), P("tensor", "dp"), P("dp", "tensor"), P("tensor", "dp"))
    small = P(None, ("dp", "tensor"))
    return jax.shard_map(
        functools.partial(per_device, mesh.shape["tensor"], mesh.shape["dp"]),
        mesh=mesh,
        in_specs=(rows, rows, P("dp", None)) + 3 * (weights + (small,)),
        out_specs=(rows, rows) + tuple(w for w in weights + (small,) for _ in range(3)),
        check_vma=False,
    )
```

```python
import functools
import math

import jax
import jax.numpy as jnp
from jax import lax
from jax.experimental import pallas as pl
from jax.experimental.pallas import tpu as pltpu
from jax.sharding import PartitionSpec as P

D = 1024
HD = 64
FF = 4096
ROT = 16
STEP = 10

EPS_NORM = 1e-05
BETA_ONE = 0.9
BETA_TWO = 0.95
EPS_ADAM = 1e-08
DECAY = 0.01
SMALL_RATE = 0.3
BFLOAT = jnp.bfloat16
FLOAT = jnp.float32
ROOT_HALF = 1.0 / math.sqrt(2.0)
INV_ROOT_TAU = 1.0 / math.sqrt(2.0 * math.pi)
PAIR = 2 * HD
QB = 128
MASKED = -1e30


def layout(lengths_row, row_count):
    starts = jnp.cumsum(lengths_row) - lengths_row
    row_index = jnp.arange(row_count, dtype=jnp.int32)
    own_start = jnp.max(
        jnp.where(row_index[:, None] >= starts[None, :], starts[None, :], 0), axis=1
    )
    return own_start, row_index - own_start


def rotary_tables(position):
    half = ROT // 2
    lane = jnp.arange(PAIR, dtype=jnp.int32) % HD
    frequency = 10000.0 ** (-(2.0 * jnp.arange(half, dtype=FLOAT)) / ROT)
    angles = position.astype(FLOAT)[:, None] * frequency[None, :]
    cos = jnp.tile(jnp.cos(angles), (1, PAIR // half))
    sin = jnp.tile(jnp.sin(angles), (1, PAIR // half))
    keep = jnp.where(lane[None] < ROT, cos, 1.0)
    from_left = jnp.where((lane[None] >= half) & (lane[None] < ROT), sin, 0.0)
    from_right = jnp.where(lane[None] < half, -sin, 0.0)
    return keep, from_left, from_right


def attention_kernel(
    pre_ref, grad_ref, keep_ref, left_ref, right_ref, start_ref,
    att_ref, dpre_ref,
    q2_ref, g2_ref, k_ref, kt_ref, v_ref, vt_ref, dk_ref, dv_ref,
):
    rows = pre_ref.shape[0]
    blocks = rows // QB
    half = ROT // 2

    def turn(x, sign, at):
        here = pl.ds(at, x.shape[0])
        return (
            x * keep_ref[here, :]
            + sign * (
                pltpu.roll(x, half, 1) * left_ref[here, :]
                + pltpu.roll(x, PAIR - half, 1) * right_ref[here, :]
            )
        )

    first = lax.broadcasted_iota(jnp.int32, (QB, PAIR), 1) < HD
    top = lax.broadcasted_iota(jnp.int32, (PAIR, QB), 0) < HD
    zero = jnp.zeros((QB, PAIR), FLOAT)
    for i in range(blocks):
        here = pl.ds(i * QB, QB)
        q = turn(pre_ref[here, :PAIR].astype(FLOAT), 1.0, i * QB) * (HD ** -0.5)
        q2_ref[pl.ds(2 * i * QB, QB), :] = jnp.where(first, q, zero).astype(BFLOAT)
        q2_ref[pl.ds((2 * i + 1) * QB, QB), :] = jnp.where(first, zero, q).astype(BFLOAT)
        g = grad_ref[here, :].astype(FLOAT)
        g2_ref[pl.ds(2 * i * QB, QB), :] = jnp.where(first, g, zero).astype(BFLOAT)
        g2_ref[pl.ds((2 * i + 1) * QB, QB), :] = jnp.where(first, zero, g).astype(BFLOAT)
        k = turn(pre_ref[here, PAIR:2 * PAIR].astype(FLOAT), 1.0, i * QB)
        k_ref[here, :] = k.astype(BFLOAT)
        kt_ref[:, here] = k.T.astype(BFLOAT)
        v = pre_ref[here, 2 * PAIR:]
        v_ref[here, :] = v
        vt_ref[:, here] = v.astype(FLOAT).T.astype(BFLOAT)

    for i in range(blocks):
        n = (i + 1) * QB
        here = pl.ds(i * QB, QB)
        q2 = q2_ref[pl.ds(2 * i * QB, 2 * QB), :]
        g2 = g2_ref[pl.ds(2 * i * QB, 2 * QB), :]
        s = lax.dot_general(
            k_ref[:n, :], q2, (((1,), (1,)), ((), ())), preferred_element_type=FLOAT
        )
        start = start_ref[:, here]
        start = jnp.concatenate([start, start], axis=1)
        lane = lax.broadcasted_iota(jnp.int32, (QB, 2 * QB), 1)
        row = lax.broadcasted_iota(jnp.int32, (QB, 2 * QB), 0)
        causal = row <= jnp.where(lane < QB, lane, lane - QB)
        tiles = []
        for j in range(i + 1):
            tile = s[j * QB:(j + 1) * QB]
            allowed = None
            if j == 0 or i * QB >= 1024:
                allowed = row + j * QB >= start
            if j == i:
                allowed = causal if allowed is None else allowed & causal
            tiles.append(tile if allowed is None else jnp.where(allowed, tile, MASKED))
        s = jnp.concatenate(tiles, axis=0) if i else tiles[0]
        e = jnp.exp(s - jnp.max(s, axis=0, keepdims=True))
        p = e * (1.0 / jnp.sum(e, axis=0, keepdims=True))
        dp = lax.dot_general(
            v_ref[:n, :], g2, (((1,), (1,)), ((), ())), preferred_element_type=FLOAT
        )
        delta = jnp.sum(dp * p, axis=0, keepdims=True)
        ds = (p * (dp - delta)).astype(BFLOAT)
        p = p.astype(BFLOAT)
        o = jnp.dot(vt_ref[:, :n], p, preferred_element_type=FLOAT)
        o = jnp.where(top, o[:, :QB], o[:, QB:])
        att_ref[here, :] = o.T.astype(BFLOAT)
        dq = jnp.dot(kt_ref[:, :n], ds, preferred_element_type=FLOAT)
        dq = jnp.where(top, dq[:, :QB], dq[:, QB:]) * (HD ** -0.5)
        dpre_ref[here, :PAIR] = turn(dq.T, -1.0, i * QB).astype(BFLOAT)
        dk = jnp.dot(ds, q2, preferred_element_type=FLOAT)
        dv = jnp.dot(p, g2, preferred_element_type=FLOAT)
        if i:
            before = n - QB
            dk_ref[:before, :] += dk[:before]
            dv_ref[:before, :] += dv[:before]
            dk_ref[here, :] = dk[before:]
            dv_ref[here, :] = dv[before:]
        else:
            dk_ref[here, :] = dk
            dv_ref[here, :] = dv

    for i in range(blocks):
        here = pl.ds(i * QB, QB)
        dpre_ref[here, PAIR:2 * PAIR] = turn(dk_ref[here, :], -1.0, i * QB).astype(BFLOAT)
        dpre_ref[here, 2 * PAIR:] = dv_ref[here, :].astype(BFLOAT)


def attention(qkv_pre, d_attended, keep, left, right, start):
    rows, width = d_attended.shape
    pairs = width // PAIR
    whole = lambda p: (0, 0)
    return pl.pallas_call(
        attention_kernel,
        grid=(pairs,),
        in_specs=[
            pl.BlockSpec((rows, 3 * PAIR), lambda p: (0, p)),
            pl.BlockSpec((rows, PAIR), lambda p: (0, p)),
            pl.BlockSpec((rows, PAIR), whole),
            pl.BlockSpec((rows, PAIR), whole),
            pl.BlockSpec((rows, PAIR), whole),
            pl.BlockSpec((1, rows), whole),
        ],
        out_specs=[
            pl.BlockSpec((rows, PAIR), lambda p: (0, p)),
            pl.BlockSpec((rows, 3 * PAIR), lambda p: (0, p)),
        ],
        out_shape=[
            jax.ShapeDtypeStruct((rows, width), BFLOAT),
            jax.ShapeDtypeStruct((rows, 3 * width), BFLOAT),
        ],
        scratch_shapes=[
            pltpu.VMEM((2 * rows, PAIR), BFLOAT),
            pltpu.VMEM((2 * rows, PAIR), BFLOAT),
            pltpu.VMEM((rows, PAIR), BFLOAT),
            pltpu.VMEM((PAIR, rows), BFLOAT),
            pltpu.VMEM((rows, PAIR), BFLOAT),
            pltpu.VMEM((PAIR, rows), BFLOAT),
            pltpu.VMEM((rows, PAIR), FLOAT),
            pltpu.VMEM((rows, PAIR), FLOAT),
        ],
        compiler_params=pltpu.CompilerParams(vmem_limit_bytes=32 * 1024 * 1024),
        cost_estimate=pl.CostEstimate(
            flops=14 * rows * rows * width // 2 * 4,
            bytes_accessed=rows * width * 16 + rows * PAIR * 12,
            transcendentals=rows * rows * (width // HD) // 2,
        ),
        name="attention",
    )(qkv_pre, d_attended, keep, left, right, start)


def mlp_kernel(
    x_ref, dy_ref, up_ref, down_ref, bias_ref,
    out_ref, dx_ref, up_grad_ref, down_grad_ref, bias_grad_ref,
    xt_ref, dyt_ref, h_ref, dp_ref,
):
    rows = x_ref.shape[0]
    tile = next(t for t in (384, 128, rows) if rows % t == 0)

    @pl.when(pl.program_id(0) == 0)
    def _():
        for i in range(rows // QB):
            here = pl.ds(i * QB, QB)
            xt_ref[:, here] = x_ref[here, :].astype(FLOAT).T.astype(BFLOAT)
            dyt_ref[:, here] = dy_ref[here, :].astype(FLOAT).T.astype(BFLOAT)
        out_ref[...] = jnp.zeros_like(out_ref)
        dx_ref[...] = jnp.zeros_like(dx_ref)

    up, down, bias = up_ref[...], down_ref[...], bias_ref[...]
    bias_grad = jnp.zeros(bias.shape, FLOAT)
    for i in range(rows // tile):
        here = pl.ds(i * tile, tile)
        pre = mm(x_ref[here, :], up) + bias
        dh = mm(dy_ref[here, :], down)
        cdf = 0.5 * (1.0 + lax.erf(pre * ROOT_HALF))
        density = jnp.exp(-0.5 * pre * pre) * INV_ROOT_TAU
        h = (pre * cdf).astype(BFLOAT)
        dp = (dh * (cdf + pre * density)).astype(BFLOAT)
        h_ref[here, :] = h
        dp_ref[here, :] = dp
        bias_grad += jnp.sum(dp.astype(FLOAT), axis=0, keepdims=True)
        out_ref[here, :] += mm_nt(h, down)
        dx_ref[here, :] += mm_nt(dp, up)
    bias_grad_ref[...] = bias_grad
    up_grad_ref[...] = mm(xt_ref[...], dp_ref[...]).astype(BFLOAT)
    down_grad_ref[...] = mm(dyt_ref[...], h_ref[...]).astype(BFLOAT)


def mlp(normed, dy, up_full, down_t, bias):
    rows, width = normed.shape
    hidden = up_full.shape[1]
    chunk = min(256, hidden)
    whole = lambda c: (0, 0)
    part = lambda c: (0, c)
    return pl.pallas_call(
        mlp_kernel,
        grid=(hidden // chunk,),
        in_specs=[
            pl.BlockSpec((rows, width), whole),
            pl.BlockSpec((rows, width), whole),
            pl.BlockSpec((width, chunk), part),
            pl.BlockSpec((width, chunk), part),
            pl.BlockSpec((1, chunk), part),
        ],
        out_specs=[
            pl.BlockSpec((rows, width), whole),
            pl.BlockSpec((rows, width), whole),
            pl.BlockSpec((width, chunk), part),
            pl.BlockSpec((width, chunk), part),
            pl.BlockSpec((1, chunk), part),
        ],
        out_shape=[
            jax.ShapeDtypeStruct((rows, width), FLOAT),
            jax.ShapeDtypeStruct((rows, width), FLOAT),
            jax.ShapeDtypeStruct((width, hidden), BFLOAT),
            jax.ShapeDtypeStruct((width, hidden), BFLOAT),
            jax.ShapeDtypeStruct((1, hidden), FLOAT),
        ],
        scratch_shapes=[
            pltpu.VMEM((width, rows), BFLOAT),
            pltpu.VMEM((width, rows), BFLOAT),
            pltpu.VMEM((rows, chunk), BFLOAT),
            pltpu.VMEM((rows, chunk), BFLOAT),
        ],
        compiler_params=pltpu.CompilerParams(vmem_limit_bytes=48 * 1024 * 1024),
        cost_estimate=pl.CostEstimate(
            flops=12 * rows * width * hidden,
            bytes_accessed=rows * width * 12 + width * hidden * 8,
            transcendentals=rows * hidden * 2,
        ),
        name="mlp",
    )(normed, dy, up_full, down_t, bias)


def adamw(weight, moment, second, gradient, step_rate, decay_rate):
    moment = BETA_ONE * moment + (1.0 - BETA_ONE) * gradient
    second = BETA_TWO * second + (1.0 - BETA_TWO) * gradient * gradient
    moment_hat = moment / (1.0 - BETA_ONE**STEP)
    second_hat = second / (1.0 - BETA_TWO**STEP)
    weight = weight - step_rate * (
        moment_hat / (jnp.sqrt(second_hat) + EPS_ADAM) + decay_rate * weight
    )
    return (moment, second, weight)


def mm(a, b):
    return jnp.dot(a, b, preferred_element_type=FLOAT)


def mm_nt(a, b):
    return lax.dot_general(a, b, (((1,), (1,)), ((), ())), preferred_element_type=FLOAT)


def mm_tn(a, b):
    return lax.dot_general(a, b, (((0,), (0,)), ((), ())), preferred_element_type=FLOAT)


def turn_order(index, chips):
    if chips == 8:
        return jnp.where(index < 4, 2 * index, 15 - 2 * index)
    return jnp.where(index < chips // 2, index, 3 * chips // 2 - 1 - index)


class Ring:
    def __init__(self, devices):
        self.n = n = devices // 2
        assert n & (n - 1) == 0
        order = [2 * i if i < 4 else 15 - 2 * i for i in range(n)]
        if n != 8:
            order = [i if i < n // 2 else 3 * n // 2 - 1 - i for i in range(n)]
        me = lax.axis_index("dp")
        self.core = me & 1
        chip = lax.shift_right_logical(me, 1)
        if n == 8:
            z = lax.shift_right_logical(chip, 1)
            self.place = jnp.where(chip & 1 == 0, z, 7 - z)
        else:
            self.place = turn_order(chip, n)
        hop = lambda step: [
            (2 * order[i] + k, 2 * order[(i + step) % n] + k) for i in range(n) for k in range(2)
        ]
        self.up_pairs, self.down_pairs = hop(1), hop(n - 1)
        self.groups = [[2 * c + k for c in range(n)] for k in range(2)]
        self.twin_pairs = [(2 * c + k, 2 * c + 1 - k) for c in range(n) for k in range(2)]

    def up(self, x):
        return lax.ppermute(x, "dp", self.up_pairs)

    def down(self, x):
        return lax.ppermute(x, "dp", self.down_pairs)

    def twin(self, x):
        return lax.ppermute(x, "dp", self.twin_pairs)

    def chip_at(self, offset):
        return turn_order((self.place + (offset + self.n)) & (self.n - 1), self.n)

    def reduce_scatter(self, grad, beside):
        n, columns = self.n, grad.shape[1]
        rows = grad.shape[0] // (2 * n)
        cut = rows // 2
        far = n // 2
        parts = grad.reshape(n, 2, rows, columns)
        came_x = {}

        def send(pair, step, move):
            pair = tuple(t.astype(BFLOAT) for t in pair)
            earlier = [came_x[s] for s in came_x if s == step - 1]
            if step in beside:
                pair, going, _ = lax.optimization_barrier((pair, beside[step], earlier))
                came_x[step] = swap(going)
            else:
                pair, _ = lax.optimization_barrier((pair, earlier))
            return tuple(m(t) for m, t in zip(move, pair))

        theirs = lax.dynamic_index_in_dim(parts, 1 - self.core, 1, keepdims=False)
        came = send((theirs,), 0, (self.twin,))[0]

        def here(offset):
            chip = self.chip_at(offset)
            own = lax.dynamic_slice(parts, (chip, self.core, 0, 0), (1, 1, rows, columns))
            twin = lax.dynamic_slice(came, (chip, 0, 0), (1, rows, columns))
            return own.reshape(rows, columns).astype(FLOAT) + twin[0].astype(FLOAT)

        both = (self.up, self.down)
        split = here(far)
        going_up, going_down = send((split[:cut], split[cut:]), 1, both)
        for step in range(2, far + 1):
            up_sum, down_sum = here(far + 1 - step), here(step - far - 1)
            going_up, going_down = going_up.astype(FLOAT), going_down.astype(FLOAT)
            if step == 2:
                going_up = jnp.concatenate([up_sum[:cut] + going_up, up_sum[cut:]], axis=0)
                going_down = jnp.concatenate([down_sum[:cut], down_sum[cut:] + going_down], axis=0)
            else:
                going_up, going_down = up_sum + going_up, down_sum + going_down
            going_up, going_down = send((going_up, going_down), step, both)
        return here(0) + going_up.astype(FLOAT) + going_down.astype(FLOAT), came_x

    def reduce_scatter_once(self, grads):
        n = self.n
        sums = []
        for grad in grads:
            parts = grad.reshape(n, 2, grad.shape[0] // (2 * n), grad.shape[1])
            came = self.twin(lax.dynamic_index_in_dim(parts, 1 - self.core, 1, keepdims=False))
            own = lax.dynamic_index_in_dim(parts, self.core, 1, keepdims=False)
            both = (own.astype(FLOAT) + came.astype(FLOAT)).astype(BFLOAT)
            sums.append(both.reshape(grad.shape[0] // 2, grad.shape[1]))
        return lax.psum_scatter(
            jnp.concatenate(sums, axis=1),
            "dp",
            scatter_dimension=0,
            axis_index_groups=self.groups,
            tiled=True,
        ).astype(FLOAT)

    def all_gather(self, shards, beside):
        n = self.n
        fulls = [jnp.zeros((n, 2) + shard.shape, shard.dtype) for shard in shards]
        came_x = {}

        def put(i, offset, block, row=0):
            chip = self.chip_at(offset)
            for core, part in ((self.core, block), (1 - self.core, self.twin(block))):
                fulls[i] = lax.dynamic_update_slice(
                    fulls[i], part[None, None], (chip, core, row, 0)
                )

        moving = [(shard, shard) for shard in shards]
        for step in range(1, n // 2 + 1):
            earlier = [came_x[s] for s in came_x if s == step - 1]
            if step in beside:
                moving, going, _ = lax.optimization_barrier((moving, beside[step], earlier))
                came_x[step] = swap(going)
            else:
                moving, _ = lax.optimization_barrier((moving, earlier))
            arrived = []
            for below, above in moving:
                cut = below.shape[0] // 2
                if step == n // 2:
                    arrived.append((self.up(below[:cut]), self.down(above[cut:])))
                else:
                    arrived.append((self.up(below), self.down(above)))
            for i, (below, above) in enumerate(moving):
                put(i, 1 - step, below)
                if step > 1:
                    put(i, step - 1, above)
            moving = arrived
        for i, (below, above) in enumerate(moving):
            put(i, n // 2, below)
            put(i, n // 2, above, below.shape[0])
        return [full.reshape(-1, full.shape[-1]) for full in fulls], came_x


def tie(value, *others):
    return lax.optimization_barrier((value,) + others)[0]


def swap(x):
    return lax.ppermute(x, "tensor", [(0, 1), (1, 0)])


def gather_rows(part, ways, came=None, axis=0):
    if ways != 2:
        return lax.all_gather(part, "tensor", axis=axis, tiled=True)
    came = swap(part) if came is None else came
    first = lax.axis_index("tensor") == 0
    return jnp.concatenate(
        [jnp.where(first, part, came), jnp.where(first, came, part)], axis=axis
    )


def per_device(
    ways, groups,
    tokens, cotangent, lengths,
    qkv_weight, proj_weight, up_weight, down_weight, small_params,
    qkv_first, proj_first, up_first, down_first, small_first,
    qkv_second, proj_second, up_second, down_second, small_second,
):
    ring = Ring(groups)
    tensor_rank = lax.axis_index("tensor")
    in_rows = qkv_weight.shape[0]
    local_width = qkv_weight.shape[2]
    hidden_width = up_weight.shape[1]
    pairs = local_width // PAIR
    own_rows = tokens.shape[0]
    row_count = own_rows * ways
    small_rows = small_params.shape[0]
    qkv_width = 3 * local_width
    att_width = qkv_width + local_width

    def pair_major(t):
        return (
            t.reshape(t.shape[0], 3, pairs, PAIR)
            .transpose(0, 2, 1, 3)
            .reshape(t.shape[0], qkv_width)
        )

    def from_pair_major(t):
        return (
            t.reshape(t.shape[0], pairs, 3, PAIR)
            .transpose(0, 2, 1, 3)
            .reshape(t.shape[0], 3, local_width)
        )

    small_here = gather_rows(small_params, ways, axis=1).T
    small_high = lax.reduce_precision(small_here, 8, 7)
    small_shard = jnp.concatenate(
        [
            small_high.astype(BFLOAT),
            (small_here - small_high).astype(BFLOAT),
            jnp.zeros((in_rows, PAIR - 2 * small_rows), BFLOAT),
        ],
        axis=1,
    )
    up_shard = up_weight.astype(BFLOAT)
    down_shard = jnp.concatenate([down_weight.T.astype(BFLOAT), small_shard], axis=1)
    att_shard = jnp.concatenate(
        [pair_major(qkv_weight.astype(BFLOAT)), proj_weight.T.astype(BFLOAT)], axis=1
    )
    beside, came = {}, [None, None]
    if ways == 2:
        cut = own_rows // 2
        halves = [tokens[:cut], tokens[cut:], cotangent[:cut], cotangent[cut:]]
        beside = {step + 1: half for step, half in enumerate(halves)}
    (up_full, down_full), came_x = ring.all_gather([up_shard, down_shard], beside)
    if ways == 2:
        came = [jnp.concatenate([came_x[i], came_x[i + 1]], axis=0) for i in (1, 3)]
    rows_in = gather_rows(tokens, ways, came[0])
    dy = gather_rows(cotangent, ways, came[1])
    down_t = down_full[:, :hidden_width]
    small = down_full[:, hidden_width:hidden_width + 2 * small_rows].astype(FLOAT).T
    small = small[:small_rows] + small[small_rows:]
    att_shard, up_full, down_full = lax.optimization_barrier((att_shard, up_full, down_full))
    att_full = lax.all_gather(att_shard, "dp", axis=0, tiled=True)

    bias_qkv = pair_major(
        lax.dynamic_slice_in_dim(small[4:7], tensor_rank * local_width, local_width, 1)[None]
    )[0]
    bias_up = lax.dynamic_slice_in_dim(
        small[8:12].reshape(4 * D), tensor_rank * hidden_width, hidden_width, 0
    )

    inputs = rows_in.astype(FLOAT)
    average = jnp.mean(inputs, axis=-1, keepdims=True)
    centred = inputs - average
    variance = jnp.mean(centred * centred, axis=-1, keepdims=True)
    inv_dev = lax.rsqrt(variance + EPS_NORM)
    xhat = centred * inv_dev
    normed_a = (xhat * small[0] + small[1]).astype(BFLOAT)
    normed_m = (xhat * small[2] + small[3]).astype(BFLOAT)

    start, position = layout(lengths[0], row_count)
    keep, left, right = rotary_tables(position)

    own_at = tensor_rank * own_rows
    cuts = [(own_rows - own_at, own_rows), (own_at, own_rows)] if ways == 2 else [(0, row_count)]
    rows_of = lambda t, cut: lax.dynamic_slice_in_dim(t, cut[0], cut[1], 0)

    out_m, d_m, up_grad, down_grad, up_bias_grad = mlp(
        normed_m, dy, up_full, down_t, bias_up[None]
    )
    mlp_own = ring.reduce_scatter_once([up_grad, down_grad])

    normed_a, out_m = lax.optimization_barrier((normed_a, out_m))
    qkv_full, proj_t = att_full[:, :qkv_width], att_full[:, qkv_width:]
    qkv_pre = (mm(normed_a, qkv_full) + bias_qkv).astype(BFLOAT)
    d_attended = mm(dy, proj_t).astype(BFLOAT)
    attended, d_qkv = attention(qkv_pre, d_attended, keep, left, right, start[None])
    proj_grad = mm_tn(dy, attended).astype(BFLOAT)
    qkv_grad = mm_tn(normed_a, d_qkv).astype(BFLOAT)
    qkv_grad, proj_grad, mlp_own = lax.optimization_barrier((qkv_grad, proj_grad, mlp_own))
    qkv_bias_grad = jnp.sum(d_qkv, axis=0, dtype=FLOAT)

    out_part = [mm_nt(rows_of(attended, c), proj_t) + rows_of(out_m, c) for c in cuts]
    beside = {}
    if ways == 2:
        out_first, beside[0] = jnp.split(out_part[0].astype(BFLOAT), 2)
        out_came = swap(out_first)
        beside[0] = tie(beside[0], out_came)

    d_a = [mm_nt(rows_of(d_qkv, c), qkv_full) for c in cuts]
    d_m = [rows_of(d_m, c) for c in cuts]
    e_part = [a * small[0] + m * small[2] for a, m in zip(d_a, d_m)]
    if ways == 2:
        beside[1], beside[2] = jnp.split(e_part[0].astype(BFLOAT), 2)
    att_own, came_x = ring.reduce_scatter(jnp.concatenate([qkv_grad, proj_grad], axis=1), beside)
    if ways == 2:
        out_came = jnp.concatenate([out_came, came_x[0]], axis=0)
        e_came = jnp.concatenate([came_x[1], came_x[2]], axis=0)
        summed = out_came.astype(FLOAT) + out_part[1]
        e_own = e_came.astype(FLOAT) + e_part[1]
    else:
        summed, e_own = (
            lax.psum_scatter(
                part[0].astype(BFLOAT), "tensor", scatter_dimension=0, tiled=True
            ).astype(FLOAT)
            for part in (out_part, e_part)
        )
    own_inputs = tokens.astype(FLOAT)
    block_out = (own_inputs + summed + small[7] + small[12]).astype(BFLOAT)
    own_hat = rows_of(xhat, (own_at, own_rows))
    own_inv = rows_of(inv_dev, (own_at, own_rows))
    token_grad = cotangent.astype(FLOAT) + own_inv * (
        e_own
        - jnp.mean(e_own, axis=-1, keepdims=True)
        - own_hat * jnp.mean(e_own * own_hat, axis=-1, keepdims=True)
    )

    out_bias_grad = jnp.sum(cotangent, axis=0, dtype=FLOAT)
    qkv_rows = lax.dynamic_update_slice_in_dim(
        jnp.zeros((3, D), FLOAT),
        from_pair_major(qkv_bias_grad[None])[0],
        tensor_rank * local_width,
        1,
    )
    up_rows = lax.dynamic_update_slice_in_dim(
        jnp.zeros((4 * D,), FLOAT), up_bias_grad[0], tensor_rank * hidden_width, 0
    )
    with_hat = lambda ds: sum(
        jnp.sum(d * rows_of(xhat, c), axis=0)[None] for d, c in zip(ds, cuts)
    )
    plain = lambda ds: sum(jnp.sum(d, axis=0)[None] for d in ds)
    small_local = jnp.concatenate(
        [
            with_hat(d_a),
            plain(d_a),
            with_hat(d_m),
            plain(d_m),
            qkv_rows,
            out_bias_grad[None],
            up_rows.reshape(4, D),
            out_bias_grad[None],
        ],
        axis=0,
    )
    small_both = small_local + swap(small_local) if ways == 2 else lax.psum(small_local, "tensor")
    reach = 1
    while reach < groups:
        small_both += lax.ppermute(small_both, "dp", [(i, i ^ reach) for i in range(groups)])
        reach *= 2
    small_width = small_params.shape[1]
    small_grad = lax.dynamic_slice_in_dim(
        small_both,
        (lax.axis_index("dp") * ways + tensor_rank) * small_width,
        small_width,
        1,
    )
    qkv_owned = from_pair_major(att_own[:, :qkv_width])
    proj_owned = att_own[:, qkv_width:att_width].T
    up_owned = mlp_own[:, :hidden_width]
    down_owned = mlp_own[:, hidden_width:].T
    qkv_new = adamw(qkv_weight, qkv_first, qkv_second, qkv_owned, D ** (-0.5), DECAY)
    proj_new = adamw(proj_weight, proj_first, proj_second, proj_owned, (D // 64) ** (-0.5), DECAY)
    up_new = adamw(up_weight, up_first, up_second, up_owned, D ** (-0.5), DECAY)
    down_new = adamw(down_weight, down_first, down_second, down_owned, FF ** (-0.5), DECAY)
    small_new = adamw(small_params, small_first, small_second, small_grad, SMALL_RATE, 0.0)
    return (block_out, token_grad) + qkv_new + proj_new + up_new + down_new + small_new


def solution(mesh):
    rows = P(("dp", "tensor"), None)
    weights = (P("dp", None, "tensor"), P("tensor", "dp"), P("dp", "tensor"), P("tensor", "dp"))
    small = P(None, ("dp", "tensor"))
    return jax.shard_map(
        functools.partial(per_device, mesh.shape["tensor"], mesh.shape["dp"]),
        mesh=mesh,
        in_specs=(rows, rows, P("dp", None)) + 3 * (weights + (small,)),
        out_specs=(rows, rows) + tuple(w for w in weights + (small,) for _ in range(3)),
        check_vma=False,
    )
```

```python
import functools
import math

import jax
import jax.numpy as jnp
from jax import lax
from jax.experimental import pallas as pl
from jax.experimental.pallas import tpu as pltpu
from jax.sharding import PartitionSpec as P

D = 1024
HD = 64
FF = 4096
ROT = 16
STEP = 10

EPS_NORM = 1e-05
BETA_ONE = 0.9
BETA_TWO = 0.95
EPS_ADAM = 1e-08
DECAY = 0.01
SMALL_RATE = 0.3
BFLOAT = jnp.bfloat16
FLOAT = jnp.float32
ROOT_HALF = 1.0 / math.sqrt(2.0)
INV_ROOT_TAU = 1.0 / math.sqrt(2.0 * math.pi)
PAIR = 2 * HD
QB = 128
MASKED = -1e30


def layout(lengths_row, row_count):
    starts = jnp.cumsum(lengths_row) - lengths_row
    row_index = jnp.arange(row_count, dtype=jnp.int32)
    own_start = jnp.max(
        jnp.where(row_index[:, None] >= starts[None, :], starts[None, :], 0), axis=1
    )
    return own_start, row_index - own_start


def rotary_tables(position):
    half = ROT // 2
    lane = jnp.arange(PAIR, dtype=jnp.int32) % HD
    frequency = 10000.0 ** (-(2.0 * jnp.arange(half, dtype=FLOAT)) / ROT)
    angles = position.astype(FLOAT)[:, None] * frequency[None, :]
    cos = jnp.tile(jnp.cos(angles), (1, PAIR // half))
    sin = jnp.tile(jnp.sin(angles), (1, PAIR // half))
    keep = jnp.where(lane[None] < ROT, cos, 1.0)
    from_left = jnp.where((lane[None] >= half) & (lane[None] < ROT), sin, 0.0)
    from_right = jnp.where(lane[None] < half, -sin, 0.0)
    return keep, from_left, from_right


def attention_kernel(
    pre_ref, grad_ref, keep_ref, left_ref, right_ref, start_ref,
    att_ref, dpre_ref,
    q2_ref, g2_ref, k_ref, kt_ref, v_ref, vt_ref, dk_ref, dv_ref,
):
    rows = pre_ref.shape[0]
    blocks = rows // QB
    half = ROT // 2

    def turn(x, sign, at):
        here = pl.ds(at, x.shape[0])
        return (
            x * keep_ref[here, :]
            + sign * (
                pltpu.roll(x, half, 1) * left_ref[here, :]
                + pltpu.roll(x, PAIR - half, 1) * right_ref[here, :]
            )
        )

    first = lax.broadcasted_iota(jnp.int32, (QB, PAIR), 1) < HD
    top = lax.broadcasted_iota(jnp.int32, (PAIR, QB), 0) < HD
    zero = jnp.zeros((QB, PAIR), FLOAT)
    for i in range(blocks):
        here = pl.ds(i * QB, QB)
        q = turn(pre_ref[here, :PAIR].astype(FLOAT), 1.0, i * QB) * (HD ** -0.5)
        q2_ref[pl.ds(2 * i * QB, QB), :] = jnp.where(first, q, zero).astype(BFLOAT)
        q2_ref[pl.ds((2 * i + 1) * QB, QB), :] = jnp.where(first, zero, q).astype(BFLOAT)
        g = grad_ref[here, :].astype(FLOAT)
        g2_ref[pl.ds(2 * i * QB, QB), :] = jnp.where(first, g, zero).astype(BFLOAT)
        g2_ref[pl.ds((2 * i + 1) * QB, QB), :] = jnp.where(first, zero, g).astype(BFLOAT)
        k = turn(pre_ref[here, PAIR:2 * PAIR].astype(FLOAT), 1.0, i * QB)
        k_ref[here, :] = k.astype(BFLOAT)
        kt_ref[:, here] = k.T.astype(BFLOAT)
        v = pre_ref[here, 2 * PAIR:]
        v_ref[here, :] = v
        vt_ref[:, here] = v.astype(FLOAT).T.astype(BFLOAT)

    for i in range(blocks):
        n = (i + 1) * QB
        here = pl.ds(i * QB, QB)
        q2 = q2_ref[pl.ds(2 * i * QB, 2 * QB), :]
        g2 = g2_ref[pl.ds(2 * i * QB, 2 * QB), :]
        s = lax.dot_general(
            k_ref[:n, :], q2, (((1,), (1,)), ((), ())), preferred_element_type=FLOAT
        )
        start = start_ref[:, here]
        start = jnp.concatenate([start, start], axis=1)
        lane = lax.broadcasted_iota(jnp.int32, (QB, 2 * QB), 1)
        row = lax.broadcasted_iota(jnp.int32, (QB, 2 * QB), 0)
        causal = row <= jnp.where(lane < QB, lane, lane - QB)
        tiles = []
        for j in range(i + 1):
            tile = s[j * QB:(j + 1) * QB]
            allowed = None
            if j == 0 or i * QB >= 1024:
                allowed = row + j * QB >= start
            if j == i:
                allowed = causal if allowed is None else allowed & causal
            tiles.append(tile if allowed is None else jnp.where(allowed, tile, MASKED))
        s = jnp.concatenate(tiles, axis=0) if i else tiles[0]
        e = jnp.exp(s - jnp.max(s, axis=0, keepdims=True))
        p = e * (1.0 / jnp.sum(e, axis=0, keepdims=True))
        dp = lax.dot_general(
            v_ref[:n, :], g2, (((1,), (1,)), ((), ())), preferred_element_type=FLOAT
        )
        delta = jnp.sum(dp * p, axis=0, keepdims=True)
        ds = (p * (dp - delta)).astype(BFLOAT)
        p = p.astype(BFLOAT)
        o = jnp.dot(vt_ref[:, :n], p, preferred_element_type=FLOAT)
        o = jnp.where(top, o[:, :QB], o[:, QB:])
        att_ref[here, :] = o.T.astype(BFLOAT)
        dq = jnp.dot(kt_ref[:, :n], ds, preferred_element_type=FLOAT)
        dq = jnp.where(top, dq[:, :QB], dq[:, QB:]) * (HD ** -0.5)
        dpre_ref[here, :PAIR] = turn(dq.T, -1.0, i * QB).astype(BFLOAT)
        dk = jnp.dot(ds, q2, preferred_element_type=FLOAT)
        dv = jnp.dot(p, g2, preferred_element_type=FLOAT)
        if i:
            before = n - QB
            dk_ref[:before, :] += dk[:before]
            dv_ref[:before, :] += dv[:before]
            dk_ref[here, :] = dk[before:]
            dv_ref[here, :] = dv[before:]
        else:
            dk_ref[here, :] = dk
            dv_ref[here, :] = dv

    for i in range(blocks):
        here = pl.ds(i * QB, QB)
        dpre_ref[here, PAIR:2 * PAIR] = turn(dk_ref[here, :], -1.0, i * QB).astype(BFLOAT)
        dpre_ref[here, 2 * PAIR:] = dv_ref[here, :].astype(BFLOAT)


def attention(qkv_pre, d_attended, keep, left, right, start):
    rows, width = d_attended.shape
    pairs = width // PAIR
    whole = lambda p: (0, 0)
    return pl.pallas_call(
        attention_kernel,
        grid=(pairs,),
        in_specs=[
            pl.BlockSpec((rows, 3 * PAIR), lambda p: (0, p)),
            pl.BlockSpec((rows, PAIR), lambda p: (0, p)),
            pl.BlockSpec((rows, PAIR), whole),
            pl.BlockSpec((rows, PAIR), whole),
            pl.BlockSpec((rows, PAIR), whole),
            pl.BlockSpec((1, rows), whole),
        ],
        out_specs=[
            pl.BlockSpec((rows, PAIR), lambda p: (0, p)),
            pl.BlockSpec((rows, 3 * PAIR), lambda p: (0, p)),
        ],
        out_shape=[
            jax.ShapeDtypeStruct((rows, width), BFLOAT),
            jax.ShapeDtypeStruct((rows, 3 * width), BFLOAT),
        ],
        scratch_shapes=[
            pltpu.VMEM((2 * rows, PAIR), BFLOAT),
            pltpu.VMEM((2 * rows, PAIR), BFLOAT),
            pltpu.VMEM((rows, PAIR), BFLOAT),
            pltpu.VMEM((PAIR, rows), BFLOAT),
            pltpu.VMEM((rows, PAIR), BFLOAT),
            pltpu.VMEM((PAIR, rows), BFLOAT),
            pltpu.VMEM((rows, PAIR), FLOAT),
            pltpu.VMEM((rows, PAIR), FLOAT),
        ],
        compiler_params=pltpu.CompilerParams(vmem_limit_bytes=32 * 1024 * 1024),
        cost_estimate=pl.CostEstimate(
            flops=14 * rows * rows * width // 2 * 4,
            bytes_accessed=rows * width * 16 + rows * PAIR * 12,
            transcendentals=rows * rows * (width // HD) // 2,
        ),
        name="attention",
    )(qkv_pre, d_attended, keep, left, right, start)


def mlp_kernel(
    chips,
    core_ref, x_ref, dy_ref, up_ref, down_ref, bias_ref,
    out_ref, dx_ref, mine_ref, theirs_ref, bias_grad_ref,
    xt_ref, dyt_ref, h_ref, dp_ref,
):
    rows = x_ref.shape[0]
    tile = next(t for t in (384, 128, rows) if rows % t == 0)

    @pl.when(pl.program_id(0) == 0)
    def _():
        for i in range(rows // QB):
            here = pl.ds(i * QB, QB)
            xt_ref[:, here] = x_ref[here, :].astype(FLOAT).T.astype(BFLOAT)
            dyt_ref[:, here] = dy_ref[here, :].astype(FLOAT).T.astype(BFLOAT)
        out_ref[...] = jnp.zeros_like(out_ref)
        dx_ref[...] = jnp.zeros_like(dx_ref)

    up, down, bias = up_ref[...], down_ref[...], bias_ref[...]
    bias_grad = jnp.zeros(bias.shape, FLOAT)
    for i in range(rows // tile):
        here = pl.ds(i * tile, tile)
        pre = mm(x_ref[here, :], up) + bias
        dh = mm(dy_ref[here, :], down)
        cdf = 0.5 * (1.0 + lax.erf(pre * ROOT_HALF))
        density = jnp.exp(-0.5 * pre * pre) * INV_ROOT_TAU
        h = (pre * cdf).astype(BFLOAT)
        dp = (dh * (cdf + pre * density)).astype(BFLOAT)
        h_ref[here, :] = h
        dp_ref[here, :] = dp
        bias_grad += jnp.sum(dp.astype(FLOAT), axis=0, keepdims=True)
        out_ref[here, :] += mm_nt(h, down)
        dx_ref[here, :] += mm_nt(dp, up)
    bias_grad_ref[...] = bias_grad
    first = core_ref[0] == 0
    chunk = up.shape[1]
    for at, grad in (
        (0, mm(xt_ref[...], dp_ref[...])),
        (chunk, mm(dyt_ref[...], h_ref[...])),
    ):
        parts = grad.reshape(chips, 2, -1, chunk)
        even, odd = (parts[:, core].reshape(-1, chunk) for core in range(2))
        mine_ref[:, at:at + chunk] = jnp.where(first, even, odd).astype(BFLOAT)
        theirs_ref[:, at:at + chunk] = jnp.where(first, odd, even).astype(BFLOAT)


def mlp_chunk(hidden):
    return min(256, hidden)


def mlp(normed, dy, up_full, down_t, bias, core, chips):
    rows, width = normed.shape
    hidden = up_full.shape[1]
    chunk = mlp_chunk(hidden)
    whole = lambda c: (0, 0)
    part = lambda c: (0, c)
    return pl.pallas_call(
        functools.partial(mlp_kernel, chips),
        grid=(hidden // chunk,),
        in_specs=[
            pl.BlockSpec(memory_space=pltpu.SMEM),
            pl.BlockSpec((rows, width), whole),
            pl.BlockSpec((rows, width), whole),
            pl.BlockSpec((width, chunk), part),
            pl.BlockSpec((width, chunk), part),
            pl.BlockSpec((1, chunk), part),
        ],
        out_specs=[
            pl.BlockSpec((rows, width), whole),
            pl.BlockSpec((rows, width), whole),
            pl.BlockSpec((width // 2, 2 * chunk), part),
            pl.BlockSpec((width // 2, 2 * chunk), part),
            pl.BlockSpec((1, chunk), part),
        ],
        out_shape=[
            jax.ShapeDtypeStruct((rows, width), FLOAT),
            jax.ShapeDtypeStruct((rows, width), FLOAT),
            jax.ShapeDtypeStruct((width // 2, 2 * hidden), BFLOAT),
            jax.ShapeDtypeStruct((width // 2, 2 * hidden), BFLOAT),
            jax.ShapeDtypeStruct((1, hidden), FLOAT),
        ],
        scratch_shapes=[
            pltpu.VMEM((width, rows), BFLOAT),
            pltpu.VMEM((width, rows), BFLOAT),
            pltpu.VMEM((rows, chunk), BFLOAT),
            pltpu.VMEM((rows, chunk), BFLOAT),
        ],
        compiler_params=pltpu.CompilerParams(vmem_limit_bytes=48 * 1024 * 1024),
        cost_estimate=pl.CostEstimate(
            flops=12 * rows * width * hidden,
            bytes_accessed=rows * width * 12 + width * hidden * 8,
            transcendentals=rows * hidden * 2,
        ),
        name="mlp",
    )(core, normed, dy, up_full, down_t, bias)


def adamw(weight, moment, second, gradient, step_rate, decay_rate):
    moment = BETA_ONE * moment + (1.0 - BETA_ONE) * gradient
    second = BETA_TWO * second + (1.0 - BETA_TWO) * gradient * gradient
    moment_hat = moment / (1.0 - BETA_ONE**STEP)
    second_hat = second / (1.0 - BETA_TWO**STEP)
    weight = weight - step_rate * (
        moment_hat / (jnp.sqrt(second_hat) + EPS_ADAM) + decay_rate * weight
    )
    return (moment, second, weight)


def mm(a, b):
    return jnp.dot(a, b, preferred_element_type=FLOAT)


def mm_nt(a, b):
    return lax.dot_general(a, b, (((1,), (1,)), ((), ())), preferred_element_type=FLOAT)


def mm_tn(a, b):
    return lax.dot_general(a, b, (((0,), (0,)), ((), ())), preferred_element_type=FLOAT)


def turn_order(index, chips):
    if chips == 8:
        return jnp.where(index < 4, 2 * index, 15 - 2 * index)
    return jnp.where(index < chips // 2, index, 3 * chips // 2 - 1 - index)


class Ring:
    def __init__(self, devices):
        self.n = n = devices // 2
        assert n & (n - 1) == 0
        order = [2 * i if i < 4 else 15 - 2 * i for i in range(n)]
        if n != 8:
            order = [i if i < n // 2 else 3 * n // 2 - 1 - i for i in range(n)]
        me = lax.axis_index("dp")
        self.core = me & 1
        chip = lax.shift_right_logical(me, 1)
        if n == 8:
            z = lax.shift_right_logical(chip, 1)
            self.place = jnp.where(chip & 1 == 0, z, 7 - z)
        else:
            self.place = turn_order(chip, n)
        hop = lambda step: [
            (2 * order[i] + k, 2 * order[(i + step) % n] + k) for i in range(n) for k in range(2)
        ]
        self.up_pairs, self.down_pairs = hop(1), hop(n - 1)
        self.groups = [[2 * c + k for c in range(n)] for k in range(2)]
        self.twin_pairs = [(2 * c + k, 2 * c + 1 - k) for c in range(n) for k in range(2)]

    def up(self, x):
        return lax.ppermute(x, "dp", self.up_pairs)

    def down(self, x):
        return lax.ppermute(x, "dp", self.down_pairs)

    def twin(self, x):
        return lax.ppermute(x, "dp", self.twin_pairs)

    def chip_at(self, offset):
        return turn_order((self.place + (offset + self.n)) & (self.n - 1), self.n)

    def split(self, grad):
        parts = grad.reshape(self.n, 2, grad.shape[0] // (2 * self.n), grad.shape[1])
        return tuple(
            lax.dynamic_index_in_dim(parts, core, 1, keepdims=False).reshape(-1, grad.shape[1])
            for core in (self.core, 1 - self.core)
        )

    def pair_sum(self, mine, theirs):
        return (mine.astype(FLOAT) + self.twin(theirs).astype(FLOAT)).astype(BFLOAT)

    def scatter(self, total):
        return lax.psum_scatter(
            total, "dp", scatter_dimension=0, axis_index_groups=self.groups, tiled=True
        ).astype(FLOAT)

    def all_gather(self, shards, before):
        n = self.n
        fulls = [jnp.zeros((n, 2) + shard.shape, shard.dtype) for shard in shards]

        def put(i, offset, block, row=0):
            chip = self.chip_at(offset)
            for core, part in ((self.core, block), (1 - self.core, self.twin(block))):
                fulls[i] = lax.dynamic_update_slice(
                    fulls[i], part[None, None], (chip, core, row, 0)
                )

        moving = [(shard, shard) for shard in shards]
        for step in range(1, n // 2 + 1):
            if step in before:
                moving = before[step](moving)
            last = step == n // 2
            arrived = []
            for below, above in moving:
                cut = below.shape[0] // 2
                if last:
                    below, above = below[:cut], above[cut:]
                arrived.append((self.up(below), self.down(above)))
            for i, (below, above) in enumerate(moving):
                if step == 1:
                    put(i, 0, shards[i])
                elif step <= n // 2:
                    put(i, 1 - step, below)
                    put(i, step - 1, above)
            moving = arrived
        for i, (below, above) in enumerate(moving):
            put(i, n // 2, below)
            put(i, n // 2, above, below.shape[0])
        return [full.reshape(-1, full.shape[-1]) for full in fulls]


def tie(value, *others):
    return lax.optimization_barrier((value,) + others)[0]


def swap(x):
    return lax.ppermute(x, "tensor", [(0, 1), (1, 0)])


def gather_rows(part, ways, axis=0):
    if ways != 2:
        return lax.all_gather(part, "tensor", axis=axis, tiled=True)
    came = swap(part)
    first = lax.axis_index("tensor") == 0
    return jnp.concatenate(
        [jnp.where(first, part, came), jnp.where(first, came, part)], axis=axis
    )


def scatter_rows(pieces, ways):
    if ways == 2:
        return swap(pieces[0].astype(BFLOAT)).astype(FLOAT) + pieces[1]
    return lax.psum_scatter(
        pieces[0].astype(BFLOAT), "tensor", scatter_dimension=0, tiled=True
    ).astype(FLOAT)


def per_device(
    ways, groups,
    tokens, cotangent, lengths,
    qkv_weight, proj_weight, up_weight, down_weight, small_params,
    qkv_first, proj_first, up_first, down_first, small_first,
    qkv_second, proj_second, up_second, down_second, small_second,
):
    ring = Ring(groups)
    tensor_rank = lax.axis_index("tensor")
    in_rows = qkv_weight.shape[0]
    local_width = qkv_weight.shape[2]
    hidden_width = up_weight.shape[1]
    pairs = local_width // PAIR
    own_rows = tokens.shape[0]
    row_count = own_rows * ways
    small_rows = small_params.shape[0]
    qkv_width = 3 * local_width
    att_width = qkv_width + local_width

    def pair_major(t):
        return (
            t.reshape(t.shape[0], 3, pairs, PAIR)
            .transpose(0, 2, 1, 3)
            .reshape(t.shape[0], qkv_width)
        )

    def from_pair_major(t):
        return (
            t.reshape(t.shape[0], pairs, 3, PAIR)
            .transpose(0, 2, 1, 3)
            .reshape(t.shape[0], 3, local_width)
        )

    small_here = gather_rows(small_params, ways, axis=1).T
    small_high = lax.reduce_precision(small_here, 8, 7)
    small_shard = jnp.concatenate(
        [
            small_high.astype(BFLOAT),
            (small_here - small_high).astype(BFLOAT),
            jnp.zeros((in_rows, PAIR - 2 * small_rows), BFLOAT),
        ],
        axis=1,
    )
    up_shard = up_weight.astype(BFLOAT)
    down_shard = jnp.concatenate([down_weight.T.astype(BFLOAT), small_shard], axis=1)
    att_shard = jnp.concatenate(
        [pair_major(qkv_weight.astype(BFLOAT)), proj_weight.T.astype(BFLOAT)], axis=1
    )
    rows_in = gather_rows(tokens, ways)
    dy = lax.all_gather(cotangent, "tensor", axis=0, tiled=True)
    up_full, down_full = ring.all_gather(
        [up_shard, down_shard],
        {3: lambda moving: tie(moving, rows_in), ring.n // 2: lambda moving: tie(moving, dy)},
    )
    small = down_full[:, hidden_width:hidden_width + 2 * small_rows].astype(FLOAT).T
    small = small[:small_rows] + small[small_rows:]
    att_shard, up_full, down_full = lax.optimization_barrier((att_shard, up_full, down_full))
    att_full = lax.all_gather(att_shard, "dp", axis=0, tiled=True)

    bias_qkv = pair_major(
        lax.dynamic_slice_in_dim(small[4:7], tensor_rank * local_width, local_width, 1)[None]
    )[0]
    bias_up = lax.dynamic_slice_in_dim(
        small[8:12].reshape(4 * D), tensor_rank * hidden_width, hidden_width, 0
    )

    inputs = rows_in.astype(FLOAT)
    average = jnp.mean(inputs, axis=-1, keepdims=True)
    centred = inputs - average
    variance = jnp.mean(centred * centred, axis=-1, keepdims=True)
    inv_dev = lax.rsqrt(variance + EPS_NORM)
    xhat = centred * inv_dev
    normed_a = (xhat * small[0] + small[1]).astype(BFLOAT)
    normed_m = (xhat * small[2] + small[3]).astype(BFLOAT)

    own_at = tensor_rank * own_rows
    cuts = [(own_rows - own_at, own_rows), (own_at, own_rows)] if ways == 2 else [(0, row_count)]
    rows_of = lambda t, cut: lax.dynamic_slice_in_dim(t, cut[0], cut[1], 0)

    start, position = layout(lengths[0], row_count)
    keep, left, right = rotary_tables(position)
    normed_m, keep, left, right = lax.optimization_barrier((normed_m, keep, left, right))

    out_m, d_m, mlp_mine, mlp_theirs, up_bias_grad = mlp(
        normed_m, dy, up_full, down_full, bias_up[None], ring.core[None], ring.n
    )
    mlp_total = ring.pair_sum(mlp_mine, mlp_theirs)
    mlp_own = ring.scatter(mlp_total)

    normed_a, out_m, mlp_total = lax.optimization_barrier((normed_a, out_m, mlp_total))
    qkv_full, proj_t = att_full[:, :qkv_width], att_full[:, qkv_width:]
    qkv_pre = (mm(normed_a, qkv_full) + bias_qkv).astype(BFLOAT)
    d_attended = mm(dy, proj_t).astype(BFLOAT)
    attended, d_qkv = attention(qkv_pre, d_attended, keep, left, right, start[None])
    proj_grad = mm_tn(dy, attended).astype(BFLOAT)
    qkv_grad = mm_tn(normed_a, d_qkv).astype(BFLOAT)
    qkv_grad, proj_grad, mlp_own = lax.optimization_barrier((qkv_grad, proj_grad, mlp_own))
    att_mine, att_theirs = ring.split(jnp.concatenate([qkv_grad, proj_grad], axis=1))
    att_total = ring.pair_sum(att_mine, att_theirs)
    att_own = ring.scatter(att_total)
    qkv_bias_grad = jnp.sum(d_qkv, axis=0, dtype=FLOAT)

    summed = scatter_rows(
        [mm_nt(rows_of(attended, c), proj_t) + rows_of(out_m, c) for c in cuts],
        ways,
    )
    own_inputs = tokens.astype(FLOAT)
    block_out = (own_inputs + summed + small[7] + small[12]).astype(BFLOAT)

    d_a = [mm_nt(rows_of(d_qkv, c), qkv_full) for c in cuts]
    d_m = [rows_of(d_m, c) for c in cuts]
    e_own = scatter_rows([a * small[0] + m * small[2] for a, m in zip(d_a, d_m)], ways)
    own_hat = rows_of(xhat, (own_at, own_rows))
    own_inv = rows_of(inv_dev, (own_at, own_rows))
    token_grad = cotangent.astype(FLOAT) + own_inv * (
        e_own
        - jnp.mean(e_own, axis=-1, keepdims=True)
        - own_hat * jnp.mean(e_own * own_hat, axis=-1, keepdims=True)
    )

    out_bias_grad = jnp.sum(cotangent, axis=0, dtype=FLOAT)
    qkv_rows = lax.dynamic_update_slice_in_dim(
        jnp.zeros((3, D), FLOAT),
        from_pair_major(qkv_bias_grad[None])[0],
        tensor_rank * local_width,
        1,
    )
    up_rows = lax.dynamic_update_slice_in_dim(
        jnp.zeros((4 * D,), FLOAT), up_bias_grad[0], tensor_rank * hidden_width, 0
    )
    with_hat = lambda ds: sum(
        jnp.sum(d * rows_of(xhat, c), axis=0)[None] for d, c in zip(ds, cuts)
    )
    plain = lambda ds: sum(jnp.sum(d, axis=0)[None] for d in ds)
    small_local = jnp.concatenate(
        [
            with_hat(d_a),
            plain(d_a),
            with_hat(d_m),
            plain(d_m),
            qkv_rows,
            out_bias_grad[None],
            up_rows.reshape(4, D),
            out_bias_grad[None],
        ],
        axis=0,
    )
    small_both = small_local + swap(small_local) if ways == 2 else lax.psum(small_local, "tensor")
    reach = 1
    while reach < groups:
        small_both += lax.ppermute(small_both, "dp", [(i, i ^ reach) for i in range(groups)])
        reach *= 2
    small_width = small_params.shape[1]
    small_grad = lax.dynamic_slice_in_dim(
        small_both,
        (lax.axis_index("dp") * ways + tensor_rank) * small_width,
        small_width,
        1,
    )
    mlp_parts = mlp_own.reshape(in_rows, -1, 2, mlp_chunk(hidden_width))
    qkv_owned = from_pair_major(att_own[:, :qkv_width])
    proj_owned = att_own[:, qkv_width:att_width].T
    up_owned = mlp_parts[:, :, 0].reshape(in_rows, hidden_width)
    down_owned = mlp_parts[:, :, 1].reshape(in_rows, hidden_width).T
    qkv_new = adamw(qkv_weight, qkv_first, qkv_second, qkv_owned, D ** (-0.5), DECAY)
    proj_new = adamw(proj_weight, proj_first, proj_second, proj_owned, (D // 64) ** (-0.5), DECAY)
    up_new = adamw(up_weight, up_first, up_second, up_owned, D ** (-0.5), DECAY)
    down_new = adamw(down_weight, down_first, down_second, down_owned, FF ** (-0.5), DECAY)
    small_new = adamw(small_params, small_first, small_second, small_grad, SMALL_RATE, 0.0)
    return (block_out, token_grad) + qkv_new + proj_new + up_new + down_new + small_new


def solution(mesh):
    rows = P(("dp", "tensor"), None)
    weights = (P("dp", None, "tensor"), P("tensor", "dp"), P("dp", "tensor"), P("tensor", "dp"))
    small = P(None, ("dp", "tensor"))
    return jax.shard_map(
        functools.partial(per_device, mesh.shape["tensor"], mesh.shape["dp"]),
        mesh=mesh,
        in_specs=(rows, rows, P("dp", None)) + 3 * (weights + (small,)),
        out_specs=(rows, rows) + tuple(w for w in weights + (small,) for _ in range(3)),
        check_vma=False,
    )
```

```python
import functools
import math

import jax
import jax.numpy as jnp
from jax import lax
from jax.experimental import pallas as pl
from jax.experimental.pallas import tpu as pltpu
from jax.sharding import PartitionSpec as P

D = 1024
HD = 64
FF = 4096
ROT = 16
STEP = 10

EPS_NORM = 1e-05
BETA_ONE = 0.9
BETA_TWO = 0.95
EPS_ADAM = 1e-08
DECAY = 0.01
SMALL_RATE = 0.3
BFLOAT = jnp.bfloat16
FLOAT = jnp.float32
ROOT_HALF = 1.0 / math.sqrt(2.0)
INV_ROOT_TAU = 1.0 / math.sqrt(2.0 * math.pi)
PAIR = 2 * HD
QB = 128
MASKED = -1e30


def layout(lengths_row, row_count):
    starts = jnp.cumsum(lengths_row) - lengths_row
    row_index = jnp.arange(row_count, dtype=jnp.int32)
    own_start = jnp.max(
        jnp.where(row_index[:, None] >= starts[None, :], starts[None, :], 0), axis=1
    )
    return own_start, row_index - own_start


def rotary_tables(position):
    half = ROT // 2
    lane = jnp.arange(PAIR, dtype=jnp.int32) % HD
    frequency = 10000.0 ** (-(2.0 * jnp.arange(half, dtype=FLOAT)) / ROT)
    angles = position.astype(FLOAT)[:, None] * frequency[None, :]
    cos = jnp.tile(jnp.cos(angles), (1, PAIR // half))
    sin = jnp.tile(jnp.sin(angles), (1, PAIR // half))
    keep = jnp.where(lane[None] < ROT, cos, 1.0)
    from_left = jnp.where((lane[None] >= half) & (lane[None] < ROT), sin, 0.0)
    from_right = jnp.where(lane[None] < half, -sin, 0.0)
    return keep, from_left, from_right


def attention_kernel(
    pre_ref, grad_ref, keep_ref, left_ref, right_ref, start_ref,
    att_ref, dpre_ref,
    q2_ref, g2_ref, k_ref, kt_ref, v_ref, vt_ref, dk_ref, dv_ref,
):
    rows = pre_ref.shape[0]
    blocks = rows // QB
    half = ROT // 2

    def turn(x, sign, at):
        here = pl.ds(at, x.shape[0])
        return (
            x * keep_ref[here, :]
            + sign * (
                pltpu.roll(x, half, 1) * left_ref[here, :]
                + pltpu.roll(x, PAIR - half, 1) * right_ref[here, :]
            )
        )

    first = lax.broadcasted_iota(jnp.int32, (QB, PAIR), 1) < HD
    top = lax.broadcasted_iota(jnp.int32, (PAIR, QB), 0) < HD
    zero = jnp.zeros((QB, PAIR), FLOAT)
    for i in range(blocks):
        here = pl.ds(i * QB, QB)
        q = turn(pre_ref[here, :PAIR].astype(FLOAT), 1.0, i * QB) * (HD ** -0.5)
        q2_ref[pl.ds(2 * i * QB, QB), :] = jnp.where(first, q, zero).astype(BFLOAT)
        q2_ref[pl.ds((2 * i + 1) * QB, QB), :] = jnp.where(first, zero, q).astype(BFLOAT)
        g = grad_ref[here, :].astype(FLOAT)
        g2_ref[pl.ds(2 * i * QB, QB), :] = jnp.where(first, g, zero).astype(BFLOAT)
        g2_ref[pl.ds((2 * i + 1) * QB, QB), :] = jnp.where(first, zero, g).astype(BFLOAT)
        k = turn(pre_ref[here, PAIR:2 * PAIR].astype(FLOAT), 1.0, i * QB)
        k_ref[here, :] = k.astype(BFLOAT)
        kt_ref[:, here] = k.T.astype(BFLOAT)
        v = pre_ref[here, 2 * PAIR:]
        v_ref[here, :] = v
        vt_ref[:, here] = v.astype(FLOAT).T.astype(BFLOAT)

    for i in range(blocks):
        n = (i + 1) * QB
        here = pl.ds(i * QB, QB)
        q2 = q2_ref[pl.ds(2 * i * QB, 2 * QB), :]
        g2 = g2_ref[pl.ds(2 * i * QB, 2 * QB), :]
        s = lax.dot_general(
            k_ref[:n, :], q2, (((1,), (1,)), ((), ())), preferred_element_type=FLOAT
        )
        start = start_ref[:, here]
        start = jnp.concatenate([start, start], axis=1)
        lane = lax.broadcasted_iota(jnp.int32, (QB, 2 * QB), 1)
        row = lax.broadcasted_iota(jnp.int32, (QB, 2 * QB), 0)
        causal = row <= jnp.where(lane < QB, lane, lane - QB)
        tiles = []
        for j in range(i + 1):
            tile = s[j * QB:(j + 1) * QB]
            allowed = None
            if j == 0 or i * QB >= 1024:
                allowed = row + j * QB >= start
            if j == i:
                allowed = causal if allowed is None else allowed & causal
            tiles.append(tile if allowed is None else jnp.where(allowed, tile, MASKED))
        s = jnp.concatenate(tiles, axis=0) if i else tiles[0]
        e = jnp.exp(s - jnp.max(s, axis=0, keepdims=True))
        p = e * (1.0 / jnp.sum(e, axis=0, keepdims=True))
        dp = lax.dot_general(
            v_ref[:n, :], g2, (((1,), (1,)), ((), ())), preferred_element_type=FLOAT
        )
        delta = jnp.sum(dp * p, axis=0, keepdims=True)
        ds = (p * (dp - delta)).astype(BFLOAT)
        p = p.astype(BFLOAT)
        o = jnp.dot(vt_ref[:, :n], p, preferred_element_type=FLOAT)
        o = jnp.where(top, o[:, :QB], o[:, QB:])
        att_ref[here, :] = o.T.astype(BFLOAT)
        dq = jnp.dot(kt_ref[:, :n], ds, preferred_element_type=FLOAT)
        dq = jnp.where(top, dq[:, :QB], dq[:, QB:]) * (HD ** -0.5)
        dpre_ref[here, :PAIR] = turn(dq.T, -1.0, i * QB).astype(BFLOAT)
        dk = jnp.dot(ds, q2, preferred_element_type=FLOAT)
        dv = jnp.dot(p, g2, preferred_element_type=FLOAT)
        if i:
            before = n - QB
            dk_ref[:before, :] += dk[:before]
            dv_ref[:before, :] += dv[:before]
            dk_ref[here, :] = dk[before:]
            dv_ref[here, :] = dv[before:]
        else:
            dk_ref[here, :] = dk
            dv_ref[here, :] = dv

    for i in range(blocks):
        here = pl.ds(i * QB, QB)
        dpre_ref[here, PAIR:2 * PAIR] = turn(dk_ref[here, :], -1.0, i * QB).astype(BFLOAT)
        dpre_ref[here, 2 * PAIR:] = dv_ref[here, :].astype(BFLOAT)


def attention(pair, qkv_pre, d_attended, keep, left, right, start, so_far):
    rows, width = d_attended.shape
    whole = lambda _: (0, 0)
    mine = lambda _: (0, pair)
    kernel = attention_kernel
    if so_far:
        kernel = lambda *refs: attention_kernel(*refs[:6], *refs[8:])
    return pl.pallas_call(
        kernel,
        grid=(1,),
        in_specs=[
            pl.BlockSpec((rows, 3 * PAIR), mine),
            pl.BlockSpec((rows, PAIR), mine),
            pl.BlockSpec((rows, PAIR), whole),
            pl.BlockSpec((rows, PAIR), whole),
            pl.BlockSpec((rows, PAIR), whole),
            pl.BlockSpec((1, rows), whole),
        ] + [pl.BlockSpec(memory_space=pl.ANY)] * len(so_far),
        out_specs=[
            pl.BlockSpec((rows, PAIR), mine),
            pl.BlockSpec((rows, 3 * PAIR), mine),
        ],
        out_shape=[
            jax.ShapeDtypeStruct((rows, width), BFLOAT),
            jax.ShapeDtypeStruct((rows, 3 * width), BFLOAT),
        ],
        input_output_aliases={6: 0, 7: 1} if so_far else {},
        scratch_shapes=[
            pltpu.VMEM((2 * rows, PAIR), BFLOAT),
            pltpu.VMEM((2 * rows, PAIR), BFLOAT),
            pltpu.VMEM((rows, PAIR), BFLOAT),
            pltpu.VMEM((PAIR, rows), BFLOAT),
            pltpu.VMEM((rows, PAIR), BFLOAT),
            pltpu.VMEM((PAIR, rows), BFLOAT),
            pltpu.VMEM((rows, PAIR), FLOAT),
            pltpu.VMEM((rows, PAIR), FLOAT),
        ],
        compiler_params=pltpu.CompilerParams(vmem_limit_bytes=32 * 1024 * 1024),
        cost_estimate=pl.CostEstimate(
            flops=56 * rows * rows * PAIR,
            bytes_accessed=rows * PAIR * 28,
            transcendentals=rows * rows,
        ),
        name="attention",
    )(qkv_pre, d_attended, keep, left, right, start, *so_far)


def mlp_kernel(
    chips,
    core_ref, x_ref, dy_ref, up_ref, down_ref, bias_ref,
    out_ref, dx_ref, mine_ref, theirs_ref, bias_grad_ref,
    xt_ref, dyt_ref, h_ref, dp_ref,
):
    rows = x_ref.shape[0]
    tile = next(t for t in (384, 128, rows) if rows % t == 0)

    @pl.when(pl.program_id(0) == 0)
    def _():
        for i in range(rows // QB):
            here = pl.ds(i * QB, QB)
            xt_ref[:, here] = x_ref[here, :].astype(FLOAT).T.astype(BFLOAT)
            dyt_ref[:, here] = dy_ref[here, :].astype(FLOAT).T.astype(BFLOAT)
        out_ref[...] = jnp.zeros_like(out_ref)
        dx_ref[...] = jnp.zeros_like(dx_ref)

    up, down, bias = up_ref[...], down_ref[...], bias_ref[...]
    bias_grad = jnp.zeros(bias.shape, FLOAT)
    for i in range(rows // tile):
        here = pl.ds(i * tile, tile)
        pre = mm(x_ref[here, :], up) + bias
        dh = mm(dy_ref[here, :], down)
        cdf = 0.5 * (1.0 + lax.erf(pre * ROOT_HALF))
        density = jnp.exp(-0.5 * pre * pre) * INV_ROOT_TAU
        h = (pre * cdf).astype(BFLOAT)
        dp = (dh * (cdf + pre * density)).astype(BFLOAT)
        h_ref[here, :] = h
        dp_ref[here, :] = dp
        bias_grad += jnp.sum(dp.astype(FLOAT), axis=0, keepdims=True)
        out_ref[here, :] += mm_nt(h, down)
        dx_ref[here, :] += mm_nt(dp, up)
    bias_grad_ref[...] = bias_grad
    first = core_ref[0] == 0
    chunk = up.shape[1]
    for at, grad in (
        (0, mm(xt_ref[...], dp_ref[...])),
        (chunk, mm(dyt_ref[...], h_ref[...])),
    ):
        parts = grad.reshape(chips, 2, -1, chunk)
        even, odd = (parts[:, core].reshape(-1, chunk) for core in range(2))
        mine_ref[:, at:at + chunk] = jnp.where(first, even, odd).astype(BFLOAT)
        theirs_ref[:, at:at + chunk] = jnp.where(first, odd, even).astype(BFLOAT)


def mlp_chunk(hidden):
    return min(256, hidden)


def mlp(normed, dy, up_full, down_t, bias, core, chips):
    rows, width = normed.shape
    hidden = up_full.shape[1]
    chunk = mlp_chunk(hidden)
    whole = lambda c: (0, 0)
    part = lambda c: (0, c)
    return pl.pallas_call(
        functools.partial(mlp_kernel, chips),
        grid=(hidden // chunk,),
        in_specs=[
            pl.BlockSpec(memory_space=pltpu.SMEM),
            pl.BlockSpec((rows, width), whole),
            pl.BlockSpec((rows, width), whole),
            pl.BlockSpec((width, chunk), part),
            pl.BlockSpec((width, chunk), part),
            pl.BlockSpec((1, chunk), part),
        ],
        out_specs=[
            pl.BlockSpec((rows, width), whole),
            pl.BlockSpec((rows, width), whole),
            pl.BlockSpec((width // 2, 2 * chunk), part),
            pl.BlockSpec((width // 2, 2 * chunk), part),
            pl.BlockSpec((1, chunk), part),
        ],
        out_shape=[
            jax.ShapeDtypeStruct((rows, width), FLOAT),
            jax.ShapeDtypeStruct((rows, width), FLOAT),
            jax.ShapeDtypeStruct((width // 2, 2 * hidden), BFLOAT),
            jax.ShapeDtypeStruct((width // 2, 2 * hidden), BFLOAT),
            jax.ShapeDtypeStruct((1, hidden), FLOAT),
        ],
        scratch_shapes=[
            pltpu.VMEM((width, rows), BFLOAT),
            pltpu.VMEM((width, rows), BFLOAT),
            pltpu.VMEM((rows, chunk), BFLOAT),
            pltpu.VMEM((rows, chunk), BFLOAT),
        ],
        compiler_params=pltpu.CompilerParams(vmem_limit_bytes=48 * 1024 * 1024),
        cost_estimate=pl.CostEstimate(
            flops=20 * rows * width * hidden,
            bytes_accessed=rows * width * 12 + width * hidden * 8,
            transcendentals=rows * hidden * 2,
        ),
        name="mlp",
    )(core, normed, dy, up_full, down_t, bias)


def adamw(weight, moment, second, gradient, step_rate, decay_rate):
    moment = BETA_ONE * moment + (1.0 - BETA_ONE) * gradient
    second = BETA_TWO * second + (1.0 - BETA_TWO) * gradient * gradient
    moment_hat = moment / (1.0 - BETA_ONE**STEP)
    second_hat = second / (1.0 - BETA_TWO**STEP)
    weight = weight - step_rate * (
        moment_hat / (jnp.sqrt(second_hat) + EPS_ADAM) + decay_rate * weight
    )
    return (moment, second, weight)


def mm(a, b):
    return jnp.dot(a, b, preferred_element_type=FLOAT)


def mm_nt(a, b):
    return lax.dot_general(a, b, (((1,), (1,)), ((), ())), preferred_element_type=FLOAT)


def mm_tn(a, b):
    return lax.dot_general(a, b, (((0,), (0,)), ((), ())), preferred_element_type=FLOAT)


def turn_order(index, chips):
    if chips == 8:
        return jnp.where(index < 4, 2 * index, 15 - 2 * index)
    return jnp.where(index < chips // 2, index, 3 * chips // 2 - 1 - index)


class Ring:
    def __init__(self, devices):
        self.n = n = devices // 2
        assert n & (n - 1) == 0
        order = [2 * i if i < 4 else 15 - 2 * i for i in range(n)]
        if n != 8:
            order = [i if i < n // 2 else 3 * n // 2 - 1 - i for i in range(n)]
        me = lax.axis_index("dp")
        self.core = me & 1
        chip = lax.shift_right_logical(me, 1)
        if n == 8:
            z = lax.shift_right_logical(chip, 1)
            self.place = jnp.where(chip & 1 == 0, z, 7 - z)
        else:
            self.place = turn_order(chip, n)
        hop = lambda step: [
            (2 * order[i] + k, 2 * order[(i + step) % n] + k) for i in range(n) for k in range(2)
        ]
        self.up_pairs, self.down_pairs = hop(1), hop(n - 1)
        self.twin_pairs = [(2 * c + k, 2 * c + 1 - k) for c in range(n) for k in range(2)]

    def up(self, x):
        return lax.ppermute(x, "dp", self.up_pairs)

    def down(self, x):
        return lax.ppermute(x, "dp", self.down_pairs)

    def twin(self, x):
        return lax.ppermute(x, "dp", self.twin_pairs)

    def chip_at(self, offset):
        return turn_order((self.place + (offset + self.n)) & (self.n - 1), self.n)

    def split(self, grad):
        parts = grad.reshape(self.n, 2, grad.shape[0] // (2 * self.n), grad.shape[1])
        return tuple(
            lax.dynamic_index_in_dim(parts, core, 1, keepdims=False).reshape(-1, grad.shape[1])
            for core in (self.core, 1 - self.core)
        )

    def reduce_scatter(self, mine, theirs, after):
        n, columns = self.n, mine.shape[1]
        rows = mine.shape[0] // n
        cut = rows // 2
        far = n // 2

        def send(step, move, *pair):
            pair = lax.optimization_barrier(tuple(t.astype(BFLOAT) for t in pair))
            arrived = tuple(m(t) for m, t in zip(move, pair))
            return after[step](arrived) if step in after else arrived

        mine = mine.reshape(n, rows, columns)
        came = send(0, (self.twin,), theirs)[0].reshape(n, rows, columns)

        def here(offset):
            at = (self.chip_at(offset), 0, 0)
            own, twin = (lax.dynamic_slice(t, at, (1, rows, columns))[0] for t in (mine, came))
            return own.astype(FLOAT) + twin.astype(FLOAT)

        both = (self.up, self.down)
        split = here(far)
        going_up, going_down = send(1, both, split[:cut], split[cut:])
        for step in range(2, far + 1):
            up_sum, down_sum = here(far + 1 - step), here(step - far - 1)
            going_up, going_down = going_up.astype(FLOAT), going_down.astype(FLOAT)
            if step == 2:
                going_up = jnp.concatenate([up_sum[:cut] + going_up, up_sum[cut:]], axis=0)
                going_down = jnp.concatenate([down_sum[:cut], down_sum[cut:] + going_down], axis=0)
            else:
                going_up, going_down = up_sum + going_up, down_sum + going_down
            going_up, going_down = send(step, both, going_up, going_down)
        return here(0) + going_up.astype(FLOAT) + going_down.astype(FLOAT)

    def all_gather(self, shards, before):
        n = self.n
        fulls = [jnp.zeros((n, 2) + shard.shape, shard.dtype) for shard in shards]

        def put(i, offset, block, row=0):
            chip = self.chip_at(offset)
            for core, part in ((self.core, block), (1 - self.core, self.twin(block))):
                fulls[i] = lax.dynamic_update_slice(
                    fulls[i], part[None, None], (chip, core, row, 0)
                )

        moving = [(shard, shard) for shard in shards]
        for step in range(1, n // 2 + 1):
            if step in before:
                moving = before[step](moving)
            last = step == n // 2
            arrived = []
            for below, above in moving:
                cut = below.shape[0] // 2
                if last:
                    below, above = below[:cut], above[cut:]
                arrived.append((self.up(below), self.down(above)))
            for i, (below, above) in enumerate(moving):
                if step == 1:
                    put(i, 0, shards[i])
                elif step <= n // 2:
                    put(i, 1 - step, below)
                    put(i, step - 1, above)
            moving = arrived
        for i, (below, above) in enumerate(moving):
            put(i, n // 2, below)
            put(i, n // 2, above, below.shape[0])
        return [full.reshape(-1, full.shape[-1]) for full in fulls]


def tie(value, *others):
    return lax.optimization_barrier((value,) + others)[0]


def swap(x):
    return lax.ppermute(x, "tensor", [(0, 1), (1, 0)])


def gather_rows(part, ways, axis=0):
    if ways != 2:
        return lax.all_gather(part, "tensor", axis=axis, tiled=True)
    came = swap(part)
    first = lax.axis_index("tensor") == 0
    return jnp.concatenate(
        [jnp.where(first, part, came), jnp.where(first, came, part)], axis=axis
    )


def scatter_rows(pieces, ways):
    if ways == 2:
        return swap(pieces[0].astype(BFLOAT)).astype(FLOAT) + pieces[1]
    return lax.psum_scatter(
        pieces[0].astype(BFLOAT), "tensor", scatter_dimension=0, tiled=True
    ).astype(FLOAT)


def per_device(
    ways, groups,
    tokens, cotangent, lengths,
    qkv_weight, proj_weight, up_weight, down_weight, small_params,
    qkv_first, proj_first, up_first, down_first, small_first,
    qkv_second, proj_second, up_second, down_second, small_second,
):
    ring = Ring(groups)
    tensor_rank = lax.axis_index("tensor")
    in_rows = qkv_weight.shape[0]
    local_width = qkv_weight.shape[2]
    hidden_width = up_weight.shape[1]
    pairs = local_width // PAIR
    own_rows = tokens.shape[0]
    row_count = own_rows * ways
    small_rows = small_params.shape[0]
    qkv_width = 3 * local_width
    att_width = qkv_width + local_width

    def pair_major(t):
        return (
            t.reshape(t.shape[0], 3, pairs, PAIR)
            .transpose(0, 2, 1, 3)
            .reshape(t.shape[0], qkv_width)
        )

    def from_pair_major(t):
        return (
            t.reshape(t.shape[0], pairs, 3, PAIR)
            .transpose(0, 2, 1, 3)
            .reshape(t.shape[0], 3, local_width)
        )

    small_here = gather_rows(small_params, ways, axis=1).T
    small_high = lax.reduce_precision(small_here, 8, 7)
    small_shard = jnp.concatenate(
        [
            small_high.astype(BFLOAT),
            (small_here - small_high).astype(BFLOAT),
            jnp.zeros((in_rows, PAIR - 2 * small_rows), BFLOAT),
        ],
        axis=1,
    )
    up_shard = up_weight.astype(BFLOAT)
    down_shard = jnp.concatenate([down_weight.T.astype(BFLOAT), small_shard], axis=1)
    att_shard = jnp.concatenate(
        [pair_major(qkv_weight.astype(BFLOAT)), proj_weight.T.astype(BFLOAT)], axis=1
    )
    both_in = lax.all_gather(jnp.stack([tokens, cotangent]), "tensor", axis=1, tiled=True)
    rows_in, dy = both_in[0], both_in[1]
    up_full, down_full = ring.all_gather([up_shard, down_shard], {})
    small = down_full[:, hidden_width:hidden_width + 2 * small_rows].astype(FLOAT).T
    small = small[:small_rows] + small[small_rows:]
    att_shard, up_full, down_full = lax.optimization_barrier((att_shard, up_full, down_full))
    att_full = lax.all_gather(att_shard, "dp", axis=0, tiled=True)

    bias_qkv = pair_major(
        lax.dynamic_slice_in_dim(small[4:7], tensor_rank * local_width, local_width, 1)[None]
    )[0]
    bias_up = lax.dynamic_slice_in_dim(
        small[8:12].reshape(4 * D), tensor_rank * hidden_width, hidden_width, 0
    )

    inputs = rows_in.astype(FLOAT)
    average = jnp.mean(inputs, axis=-1, keepdims=True)
    centred = inputs - average
    variance = jnp.mean(centred * centred, axis=-1, keepdims=True)
    inv_dev = lax.rsqrt(variance + EPS_NORM)
    xhat = centred * inv_dev
    normed_a = (xhat * small[0] + small[1]).astype(BFLOAT)
    normed_m = (xhat * small[2] + small[3]).astype(BFLOAT)

    own_at = tensor_rank * own_rows
    cuts = [(own_rows - own_at, own_rows), (own_at, own_rows)] if ways == 2 else [(0, row_count)]
    rows_of = lambda t, cut: lax.dynamic_slice_in_dim(t, cut[0], cut[1], 0)

    start, position = layout(lengths[0], row_count)
    keep, left, right = rotary_tables(position)
    normed_m, keep, left, right = lax.optimization_barrier((normed_m, keep, left, right))

    out_m, d_m, mlp_mine, mlp_theirs, up_bias_grad = mlp(
        normed_m, dy, up_full, down_full, bias_up[None], ring.core[None], ring.n
    )
    normed_a, out_m = lax.optimization_barrier((normed_a, out_m))
    qkv_full, proj_t = att_full[:, :qkv_width], att_full[:, qkv_width:]
    work = [
        (mm(normed_a, qkv_full) + bias_qkv).astype(BFLOAT),
        mm(dy, proj_t).astype(BFLOAT),
        (),
    ]

    def attend_after(pair, arrived):
        if pair < pairs:
            work[0], arrived = lax.optimization_barrier((work[0], arrived))
            work[2] = attention(
                pair, work[0], work[1], keep, left, right, start[None], tuple(work[2])
            )
        return arrived

    steps = {i: functools.partial(attend_after, i) for i in range(ring.n // 2)}
    mlp_own = ring.reduce_scatter(mlp_mine, mlp_theirs, steps)
    attended, d_qkv = work[2]
    proj_grad = mm_tn(dy, attended).astype(BFLOAT)
    qkv_grad = mm_tn(normed_a, d_qkv).astype(BFLOAT)
    att_mine, att_theirs = ring.split(jnp.concatenate([qkv_grad, proj_grad], axis=1))
    attended, d_qkv, att_theirs = lax.optimization_barrier((attended, d_qkv, att_theirs))
    att_theirs, mlp_own = lax.optimization_barrier((att_theirs, mlp_own))
    att_own = ring.reduce_scatter(att_mine, att_theirs, {})
    qkv_bias_grad = jnp.sum(d_qkv, axis=0, dtype=FLOAT)

    summed = scatter_rows(
        [mm_nt(rows_of(attended, c), proj_t) + rows_of(out_m, c) for c in cuts],
        ways,
    )
    own_inputs = tokens.astype(FLOAT)
    block_out = (own_inputs + summed + small[7] + small[12]).astype(BFLOAT)

    d_a = [mm_nt(rows_of(d_qkv, c), qkv_full) for c in cuts]
    d_m = [rows_of(d_m, c) for c in cuts]
    e_own = scatter_rows([a * small[0] + m * small[2] for a, m in zip(d_a, d_m)], ways)
    own_hat = rows_of(xhat, (own_at, own_rows))
    own_inv = rows_of(inv_dev, (own_at, own_rows))
    token_grad = cotangent.astype(FLOAT) + own_inv * (
        e_own
        - jnp.mean(e_own, axis=-1, keepdims=True)
        - own_hat * jnp.mean(e_own * own_hat, axis=-1, keepdims=True)
    )

    out_bias_grad = jnp.sum(cotangent, axis=0, dtype=FLOAT)
    qkv_rows = lax.dynamic_update_slice_in_dim(
        jnp.zeros((3, D), FLOAT),
        from_pair_major(qkv_bias_grad[None])[0],
        tensor_rank * local_width,
        1,
    )
    up_rows = lax.dynamic_update_slice_in_dim(
        jnp.zeros((4 * D,), FLOAT), up_bias_grad[0], tensor_rank * hidden_width, 0
    )
    with_hat = lambda ds: sum(
        jnp.sum(d * rows_of(xhat, c), axis=0)[None] for d, c in zip(ds, cuts)
    )
    plain = lambda ds: sum(jnp.sum(d, axis=0)[None] for d in ds)
    small_local = jnp.concatenate(
        [
            with_hat(d_a),
            plain(d_a),
            with_hat(d_m),
            plain(d_m),
            qkv_rows,
            out_bias_grad[None],
            up_rows.reshape(4, D),
            out_bias_grad[None],
        ],
        axis=0,
    )
    small_both = small_local + swap(small_local) if ways == 2 else lax.psum(small_local, "tensor")
    reach = 1
    while reach < groups:
        small_both += lax.ppermute(small_both, "dp", [(i, i ^ reach) for i in range(groups)])
        reach *= 2
    small_width = small_params.shape[1]
    small_grad = lax.dynamic_slice_in_dim(
        small_both,
        (lax.axis_index("dp") * ways + tensor_rank) * small_width,
        small_width,
        1,
    )
    mlp_parts = mlp_own.reshape(in_rows, -1, 2, mlp_chunk(hidden_width))
    qkv_owned = from_pair_major(att_own[:, :qkv_width])
    proj_owned = att_own[:, qkv_width:att_width].T
    up_owned = mlp_parts[:, :, 0].reshape(in_rows, hidden_width)
    down_owned = mlp_parts[:, :, 1].reshape(in_rows, hidden_width).T
    qkv_new = adamw(qkv_weight, qkv_first, qkv_second, qkv_owned, D ** (-0.5), DECAY)
    proj_new = adamw(proj_weight, proj_first, proj_second, proj_owned, (D // 64) ** (-0.5), DECAY)
    up_new = adamw(up_weight, up_first, up_second, up_owned, D ** (-0.5), DECAY)
    down_new = adamw(down_weight, down_first, down_second, down_owned, FF ** (-0.5), DECAY)
    small_new = adamw(small_params, small_first, small_second, small_grad, SMALL_RATE, 0.0)
    return (block_out, token_grad) + qkv_new + proj_new + up_new + down_new + small_new


def solution(mesh):
    rows = P(("dp", "tensor"), None)
    weights = (P("dp", None, "tensor"), P("tensor", "dp"), P("dp", "tensor"), P("tensor", "dp"))
    small = P(None, ("dp", "tensor"))
    return jax.shard_map(
        functools.partial(per_device, mesh.shape["tensor"], mesh.shape["dp"]),
        mesh=mesh,
        in_specs=(rows, rows, P("dp", None)) + 3 * (weights + (small,)),
        out_specs=(rows, rows) + tuple(w for w in weights + (small,) for _ in range(3)),
        check_vma=False,
    )
```

```python
import functools
import math

import jax
import jax.numpy as jnp
from jax import lax
from jax.experimental import pallas as pl
from jax.experimental.pallas import tpu as pltpu
from jax.sharding import PartitionSpec as P

D = 1024
HD = 64
FF = 4096
ROT = 16
STEP = 10

EPS_NORM = 1e-05
BETA_ONE = 0.9
BETA_TWO = 0.95
EPS_ADAM = 1e-08
DECAY = 0.01
SMALL_RATE = 0.3
BFLOAT = jnp.bfloat16
FLOAT = jnp.float32
ROOT_HALF = 1.0 / math.sqrt(2.0)
INV_ROOT_TAU = 1.0 / math.sqrt(2.0 * math.pi)
PAIR = 2 * HD
QB = 128
MASKED = -1e30


def layout(lengths_row, row_count):
    starts = jnp.cumsum(lengths_row) - lengths_row
    row_index = jnp.arange(row_count, dtype=jnp.int32)
    own_start = jnp.max(
        jnp.where(row_index[:, None] >= starts[None, :], starts[None, :], 0), axis=1
    )
    return own_start, row_index - own_start


def rotary_tables(position):
    half = ROT // 2
    lane = jnp.arange(PAIR, dtype=jnp.int32) % HD
    frequency = 10000.0 ** (-(2.0 * jnp.arange(half, dtype=FLOAT)) / ROT)
    angles = position.astype(FLOAT)[:, None] * frequency[None, :]
    cos = jnp.tile(jnp.cos(angles), (1, PAIR // half))
    sin = jnp.tile(jnp.sin(angles), (1, PAIR // half))
    keep = jnp.where(lane[None] < ROT, cos, 1.0)
    from_left = jnp.where((lane[None] >= half) & (lane[None] < ROT), sin, 0.0)
    from_right = jnp.where(lane[None] < half, -sin, 0.0)
    return keep, from_left, from_right


def attention_kernel(
    pre_ref, grad_ref, keep_ref, left_ref, right_ref, start_ref,
    att_ref, dpre_ref,
    q2_ref, g2_ref, k_ref, kt_ref, v_ref, vt_ref, dk_ref, dv_ref,
):
    rows = pre_ref.shape[0]
    blocks = rows // QB
    half = ROT // 2

    def turn(x, sign, at):
        here = pl.ds(at, x.shape[0])
        return (
            x * keep_ref[here, :]
            + sign * (
                pltpu.roll(x, half, 1) * left_ref[here, :]
                + pltpu.roll(x, PAIR - half, 1) * right_ref[here, :]
            )
        )

    first = lax.broadcasted_iota(jnp.int32, (QB, PAIR), 1) < HD
    top = lax.broadcasted_iota(jnp.int32, (PAIR, QB), 0) < HD
    zero = jnp.zeros((QB, PAIR), FLOAT)
    for i in range(blocks):
        here = pl.ds(i * QB, QB)
        q = turn(pre_ref[here, :PAIR].astype(FLOAT), 1.0, i * QB) * (HD ** -0.5)
        q2_ref[pl.ds(2 * i * QB, QB), :] = jnp.where(first, q, zero).astype(BFLOAT)
        q2_ref[pl.ds((2 * i + 1) * QB, QB), :] = jnp.where(first, zero, q).astype(BFLOAT)
        g = grad_ref[here, :].astype(FLOAT)
        g2_ref[pl.ds(2 * i * QB, QB), :] = jnp.where(first, g, zero).astype(BFLOAT)
        g2_ref[pl.ds((2 * i + 1) * QB, QB), :] = jnp.where(first, zero, g).astype(BFLOAT)
        k = turn(pre_ref[here, PAIR:2 * PAIR].astype(FLOAT), 1.0, i * QB)
        k_ref[here, :] = k.astype(BFLOAT)
        kt_ref[:, here] = k.T.astype(BFLOAT)
        v = pre_ref[here, 2 * PAIR:]
        v_ref[here, :] = v
        vt_ref[:, here] = v.astype(FLOAT).T.astype(BFLOAT)

    for i in range(blocks):
        n = (i + 1) * QB
        here = pl.ds(i * QB, QB)
        q2 = q2_ref[pl.ds(2 * i * QB, 2 * QB), :]
        g2 = g2_ref[pl.ds(2 * i * QB, 2 * QB), :]
        s = lax.dot_general(
            k_ref[:n, :], q2, (((1,), (1,)), ((), ())), preferred_element_type=FLOAT
        )
        start = start_ref[:, here]
        start = jnp.concatenate([start, start], axis=1)
        lane = lax.broadcasted_iota(jnp.int32, (QB, 2 * QB), 1)
        row = lax.broadcasted_iota(jnp.int32, (QB, 2 * QB), 0)
        causal = row <= jnp.where(lane < QB, lane, lane - QB)
        tiles = []
        for j in range(i + 1):
            tile = s[j * QB:(j + 1) * QB]
            allowed = None
            if j == 0 or i * QB >= 1024:
                allowed = row + j * QB >= start
            if j == i:
                allowed = causal if allowed is None else allowed & causal
            tiles.append(tile if allowed is None else jnp.where(allowed, tile, MASKED))
        s = jnp.concatenate(tiles, axis=0) if i else tiles[0]
        e = jnp.exp(s - jnp.max(s, axis=0, keepdims=True))
        p = e * (1.0 / jnp.sum(e, axis=0, keepdims=True))
        dp = lax.dot_general(
            v_ref[:n, :], g2, (((1,), (1,)), ((), ())), preferred_element_type=FLOAT
        )
        delta = jnp.sum(dp * p, axis=0, keepdims=True)
        ds = (p * (dp - delta)).astype(BFLOAT)
        p = p.astype(BFLOAT)
        o = jnp.dot(vt_ref[:, :n], p, preferred_element_type=FLOAT)
        o = jnp.where(top, o[:, :QB], o[:, QB:])
        att_ref[here, :] = o.T.astype(BFLOAT)
        dq = jnp.dot(kt_ref[:, :n], ds, preferred_element_type=FLOAT)
        dq = jnp.where(top, dq[:, :QB], dq[:, QB:]) * (HD ** -0.5)
        dpre_ref[here, :PAIR] = turn(dq.T, -1.0, i * QB).astype(BFLOAT)
        dk = jnp.dot(ds, q2, preferred_element_type=FLOAT)
        dv = jnp.dot(p, g2, preferred_element_type=FLOAT)
        if i:
            before = n - QB
            dk_ref[:before, :] += dk[:before]
            dv_ref[:before, :] += dv[:before]
            dk_ref[here, :] = dk[before:]
            dv_ref[here, :] = dv[before:]
        else:
            dk_ref[here, :] = dk
            dv_ref[here, :] = dv

    for i in range(blocks):
        here = pl.ds(i * QB, QB)
        dpre_ref[here, PAIR:2 * PAIR] = turn(dk_ref[here, :], -1.0, i * QB).astype(BFLOAT)
        dpre_ref[here, 2 * PAIR:] = dv_ref[here, :].astype(BFLOAT)


def attention(pair, qkv_pre, d_attended, keep, left, right, start, so_far):
    rows, width = d_attended.shape
    whole = lambda _: (0, 0)
    mine = lambda _: (0, pair)
    kernel = attention_kernel
    if so_far:
        kernel = lambda *refs: attention_kernel(*refs[:6], *refs[8:])
    return pl.pallas_call(
        kernel,
        grid=(1,),
        in_specs=[
            pl.BlockSpec((rows, 3 * PAIR), mine),
            pl.BlockSpec((rows, PAIR), mine),
            pl.BlockSpec((rows, PAIR), whole),
            pl.BlockSpec((rows, PAIR), whole),
            pl.BlockSpec((rows, PAIR), whole),
            pl.BlockSpec((1, rows), whole),
        ] + [pl.BlockSpec(memory_space=pl.ANY)] * len(so_far),
        out_specs=[
            pl.BlockSpec((rows, PAIR), mine),
            pl.BlockSpec((rows, 3 * PAIR), mine),
        ],
        out_shape=[
            jax.ShapeDtypeStruct((rows, width), BFLOAT),
            jax.ShapeDtypeStruct((rows, 3 * width), BFLOAT),
        ],
        input_output_aliases={6: 0, 7: 1} if so_far else {},
        scratch_shapes=[
            pltpu.VMEM((2 * rows, PAIR), BFLOAT),
            pltpu.VMEM((2 * rows, PAIR), BFLOAT),
            pltpu.VMEM((rows, PAIR), BFLOAT),
            pltpu.VMEM((PAIR, rows), BFLOAT),
            pltpu.VMEM((rows, PAIR), BFLOAT),
            pltpu.VMEM((PAIR, rows), BFLOAT),
            pltpu.VMEM((rows, PAIR), FLOAT),
            pltpu.VMEM((rows, PAIR), FLOAT),
        ],
        compiler_params=pltpu.CompilerParams(vmem_limit_bytes=32 * 1024 * 1024),
        cost_estimate=pl.CostEstimate(
            flops=56 * rows * rows * PAIR,
            bytes_accessed=rows * PAIR * 28,
            transcendentals=rows * rows,
        ),
        name="attention",
    )(qkv_pre, d_attended, keep, left, right, start, *so_far)


def mlp_kernel(
    chips,
    core_ref, x_ref, dy_ref, up_ref, down_ref, bias_ref,
    out_ref, dx_ref, mine_ref, theirs_ref, bias_grad_ref,
    xt_ref, dyt_ref, h_ref, dp_ref,
):
    rows = x_ref.shape[0]
    tile = next(t for t in (384, 128, rows) if rows % t == 0)

    @pl.when(pl.program_id(0) == 0)
    def _():
        for i in range(rows // QB):
            here = pl.ds(i * QB, QB)
            xt_ref[:, here] = x_ref[here, :].astype(FLOAT).T.astype(BFLOAT)
            dyt_ref[:, here] = dy_ref[here, :].astype(FLOAT).T.astype(BFLOAT)
        out_ref[...] = jnp.zeros_like(out_ref)
        dx_ref[...] = jnp.zeros_like(dx_ref)

    up, down, bias = up_ref[...], down_ref[...], bias_ref[...]
    bias_grad = jnp.zeros(bias.shape, FLOAT)
    for i in range(rows // tile):
        here = pl.ds(i * tile, tile)
        pre = mm(x_ref[here, :], up) + bias
        dh = mm(dy_ref[here, :], down)
        cdf = 0.5 * (1.0 + lax.erf(pre * ROOT_HALF))
        density = jnp.exp(-0.5 * pre * pre) * INV_ROOT_TAU
        h = (pre * cdf).astype(BFLOAT)
        dp = (dh * (cdf + pre * density)).astype(BFLOAT)
        h_ref[here, :] = h
        dp_ref[here, :] = dp
        bias_grad += jnp.sum(dp.astype(FLOAT), axis=0, keepdims=True)
        out_ref[here, :] += mm_nt(h, down)
        dx_ref[here, :] += mm_nt(dp, up)
    bias_grad_ref[...] = bias_grad
    first = core_ref[0] == 0
    chunk = up.shape[1]
    for at, grad in (
        (0, mm(xt_ref[...], dp_ref[...])),
        (chunk, mm(dyt_ref[...], h_ref[...])),
    ):
        parts = grad.reshape(chips, 2, -1, chunk)
        even, odd = (parts[:, core].reshape(-1, chunk) for core in range(2))
        mine_ref[:, at:at + chunk] = jnp.where(first, even, odd).astype(BFLOAT)
        theirs_ref[:, at:at + chunk] = jnp.where(first, odd, even).astype(BFLOAT)


def mlp_chunk(hidden):
    return min(256, hidden)


def mlp(normed, dy, up_full, down_t, bias, core, chips):
    rows, width = normed.shape
    hidden = up_full.shape[1]
    chunk = mlp_chunk(hidden)
    whole = lambda c: (0, 0)
    part = lambda c: (0, c)
    return pl.pallas_call(
        functools.partial(mlp_kernel, chips),
        grid=(hidden // chunk,),
        in_specs=[
            pl.BlockSpec(memory_space=pltpu.SMEM),
            pl.BlockSpec((rows, width), whole),
            pl.BlockSpec((rows, width), whole),
            pl.BlockSpec((width, chunk), part),
            pl.BlockSpec((width, chunk), part),
            pl.BlockSpec((1, chunk), part),
        ],
        out_specs=[
            pl.BlockSpec((rows, width), whole),
            pl.BlockSpec((rows, width), whole),
            pl.BlockSpec((width // 2, 2 * chunk), part),
            pl.BlockSpec((width // 2, 2 * chunk), part),
            pl.BlockSpec((1, chunk), part),
        ],
        out_shape=[
            jax.ShapeDtypeStruct((rows, width), FLOAT),
            jax.ShapeDtypeStruct((rows, width), FLOAT),
            jax.ShapeDtypeStruct((width // 2, 2 * hidden), BFLOAT),
            jax.ShapeDtypeStruct((width // 2, 2 * hidden), BFLOAT),
            jax.ShapeDtypeStruct((1, hidden), FLOAT),
        ],
        scratch_shapes=[
            pltpu.VMEM((width, rows), BFLOAT),
            pltpu.VMEM((width, rows), BFLOAT),
            pltpu.VMEM((rows, chunk), BFLOAT),
            pltpu.VMEM((rows, chunk), BFLOAT),
        ],
        compiler_params=pltpu.CompilerParams(vmem_limit_bytes=48 * 1024 * 1024),
        cost_estimate=pl.CostEstimate(
            flops=20 * rows * width * hidden,
            bytes_accessed=rows * width * 12 + width * hidden * 8,
            transcendentals=rows * hidden * 2,
        ),
        name="mlp",
    )(core, normed, dy, up_full, down_t, bias)


def adamw(weight, moment, second, gradient, step_rate, decay_rate):
    moment = BETA_ONE * moment + (1.0 - BETA_ONE) * gradient
    second = BETA_TWO * second + (1.0 - BETA_TWO) * gradient * gradient
    moment_hat = moment / (1.0 - BETA_ONE**STEP)
    second_hat = second / (1.0 - BETA_TWO**STEP)
    weight = weight - step_rate * (
        moment_hat / (jnp.sqrt(second_hat) + EPS_ADAM) + decay_rate * weight
    )
    return (moment, second, weight)


def mm(a, b):
    return jnp.dot(a, b, preferred_element_type=FLOAT)


def mm_nt(a, b):
    return lax.dot_general(a, b, (((1,), (1,)), ((), ())), preferred_element_type=FLOAT)


def mm_tn(a, b):
    return lax.dot_general(a, b, (((0,), (0,)), ((), ())), preferred_element_type=FLOAT)


def turn_order(index, chips):
    if chips == 8:
        return jnp.where(index < 4, 2 * index, 15 - 2 * index)
    return jnp.where(index < chips // 2, index, 3 * chips // 2 - 1 - index)


class Ring:
    def __init__(self, devices):
        self.n = n = devices // 2
        assert n & (n - 1) == 0
        order = [2 * i if i < 4 else 15 - 2 * i for i in range(n)]
        if n != 8:
            order = [i if i < n // 2 else 3 * n // 2 - 1 - i for i in range(n)]
        me = lax.axis_index("dp")
        self.core = me & 1
        chip = lax.shift_right_logical(me, 1)
        if n == 8:
            z = lax.shift_right_logical(chip, 1)
            self.place = jnp.where(chip & 1 == 0, z, 7 - z)
        else:
            self.place = turn_order(chip, n)
        hop = lambda step: [
            (2 * order[i] + k, 2 * order[(i + step) % n] + k) for i in range(n) for k in range(2)
        ]
        self.up_pairs, self.down_pairs = hop(1), hop(n - 1)
        self.twin_pairs = [(2 * c + k, 2 * c + 1 - k) for c in range(n) for k in range(2)]

    def up(self, x):
        return lax.ppermute(x, "dp", self.up_pairs)

    def down(self, x):
        return lax.ppermute(x, "dp", self.down_pairs)

    def twin(self, x):
        return lax.ppermute(x, "dp", self.twin_pairs)

    def chip_at(self, offset):
        return turn_order((self.place + (offset + self.n)) & (self.n - 1), self.n)

    def split(self, grad):
        parts = grad.reshape(self.n, 2, grad.shape[0] // (2 * self.n), grad.shape[1])
        return tuple(
            lax.dynamic_index_in_dim(parts, core, 1, keepdims=False).reshape(-1, grad.shape[1])
            for core in (self.core, 1 - self.core)
        )

    def reduce_scatter(self, mine, theirs, after, before={}):
        n, columns = self.n, mine.shape[1]
        rows = mine.shape[0] // n
        cut = rows // 2
        far = n // 2

        def send(step, move, *pair):
            pair = lax.optimization_barrier(tuple(t.astype(BFLOAT) for t in pair))
            pair = before[step](pair) if step in before else pair
            arrived = tuple(m(t) for m, t in zip(move, pair))
            return after[step](arrived) if step in after else arrived

        mine = mine.reshape(n, rows, columns)
        came = send(0, (self.twin,), theirs)[0].reshape(n, rows, columns)

        def here(offset):
            at = (self.chip_at(offset), 0, 0)
            own, twin = (lax.dynamic_slice(t, at, (1, rows, columns))[0] for t in (mine, came))
            return own.astype(FLOAT) + twin.astype(FLOAT)

        both = (self.up, self.down)
        split = here(far)
        going_up, going_down = send(1, both, split[:cut], split[cut:])
        for step in range(2, far + 1):
            up_sum, down_sum = here(far + 1 - step), here(step - far - 1)
            going_up, going_down = going_up.astype(FLOAT), going_down.astype(FLOAT)
            if step == 2:
                going_up = jnp.concatenate([up_sum[:cut] + going_up, up_sum[cut:]], axis=0)
                going_down = jnp.concatenate([down_sum[:cut], down_sum[cut:] + going_down], axis=0)
            else:
                going_up, going_down = up_sum + going_up, down_sum + going_down
            going_up, going_down = send(step, both, going_up, going_down)
        return here(0) + going_up.astype(FLOAT) + going_down.astype(FLOAT)

    def all_gather(self, shards, before):
        n = self.n
        fulls = [unwritten((n, 2) + shard.shape, shard.dtype) for shard in shards]

        def put(i, offset, block, row=0):
            chip = self.chip_at(offset)
            for core, part in ((self.core, block), (1 - self.core, self.twin(block))):
                fulls[i] = lax.dynamic_update_slice(
                    fulls[i], part[None, None], (chip, core, row, 0)
                )

        moving = [(shard, shard) for shard in shards]
        for step in range(1, n // 2 + 1):
            if step in before:
                moving = before[step](moving)
            last = step == n // 2
            arrived = []
            for below, above in moving:
                cut = below.shape[0] // 2
                if last:
                    below, above = below[:cut], above[cut:]
                arrived.append((self.up(below), self.down(above)))
            for i, (below, above) in enumerate(moving):
                if step == 1:
                    put(i, 0, shards[i])
                elif step <= n // 2:
                    put(i, 1 - step, below)
                    put(i, step - 1, above)
            moving = arrived
        for i, (below, above) in enumerate(moving):
            put(i, n // 2, below)
            put(i, n // 2, above, below.shape[0])
        return [full.reshape(-1, full.shape[-1]) for full in fulls]


def unwritten(shape, dtype):
    return pl.pallas_call(
        lambda out_ref: None,
        out_specs=pl.BlockSpec(memory_space=pl.ANY),
        out_shape=jax.ShapeDtypeStruct(shape, dtype),
        name="unwritten",
    )()


def tie(value, *others):
    return lax.optimization_barrier((value,) + others)[0]


def swap(x):
    return lax.ppermute(x, "tensor", [(0, 1), (1, 0)])


def gather_rows(part, ways, axis=0):
    if ways != 2:
        return lax.all_gather(part, "tensor", axis=axis, tiled=True)
    came = swap(part)
    first = lax.axis_index("tensor") == 0
    return jnp.concatenate(
        [jnp.where(first, part, came), jnp.where(first, came, part)], axis=axis
    )


def per_device(
    ways, groups,
    tokens, cotangent, lengths,
    qkv_weight, proj_weight, up_weight, down_weight, small_params,
    qkv_first, proj_first, up_first, down_first, small_first,
    qkv_second, proj_second, up_second, down_second, small_second,
):
    ring = Ring(groups)
    tensor_rank = lax.axis_index("tensor")
    in_rows = qkv_weight.shape[0]
    local_width = qkv_weight.shape[2]
    hidden_width = up_weight.shape[1]
    pairs = local_width // PAIR
    own_rows = tokens.shape[0]
    row_count = own_rows * ways
    small_rows = small_params.shape[0]
    qkv_width = 3 * local_width
    att_width = qkv_width + local_width

    def pair_major(t):
        return (
            t.reshape(t.shape[0], 3, pairs, PAIR)
            .transpose(0, 2, 1, 3)
            .reshape(t.shape[0], qkv_width)
        )

    def from_pair_major(t):
        return (
            t.reshape(t.shape[0], pairs, 3, PAIR)
            .transpose(0, 2, 1, 3)
            .reshape(t.shape[0], 3, local_width)
        )

    small_here = gather_rows(small_params, ways, axis=1).T
    small_high = lax.reduce_precision(small_here, 8, 7)
    small_shard = jnp.concatenate(
        [
            small_high.astype(BFLOAT),
            (small_here - small_high).astype(BFLOAT),
            jnp.zeros((in_rows, PAIR - 2 * small_rows), BFLOAT),
        ],
        axis=1,
    )
    up_shard = up_weight.astype(BFLOAT)
    down_shard = jnp.concatenate([down_weight.T.astype(BFLOAT), small_shard], axis=1)
    att_shard = jnp.concatenate(
        [pair_major(qkv_weight.astype(BFLOAT)), proj_weight.T.astype(BFLOAT)], axis=1
    )
    both_in = jnp.stack([tokens, cotangent])
    up_shard, both_in = lax.optimization_barrier((up_shard, both_in))
    both_in = lax.all_gather(both_in, "tensor", axis=1, tiled=True)
    rows_in, dy = both_in[0], both_in[1]
    up_full, down_full = ring.all_gather([up_shard, down_shard], {})
    small = down_full[:, hidden_width:hidden_width + 2 * small_rows].astype(FLOAT).T
    small = small[:small_rows] + small[small_rows:]
    att_shard, up_full, down_full = lax.optimization_barrier((att_shard, up_full, down_full))
    att_full = lax.all_gather(att_shard, "dp", axis=0, tiled=True)

    bias_qkv = pair_major(
        lax.dynamic_slice_in_dim(small[4:7], tensor_rank * local_width, local_width, 1)[None]
    )[0]
    bias_up = lax.dynamic_slice_in_dim(
        small[8:12].reshape(4 * D), tensor_rank * hidden_width, hidden_width, 0
    )

    inputs = rows_in.astype(FLOAT)
    average = jnp.mean(inputs, axis=-1, keepdims=True)
    centred = inputs - average
    variance = jnp.mean(centred * centred, axis=-1, keepdims=True)
    inv_dev = lax.rsqrt(variance + EPS_NORM)
    xhat = centred * inv_dev
    normed_a = (xhat * small[0] + small[1]).astype(BFLOAT)
    normed_m = (xhat * small[2] + small[3]).astype(BFLOAT)

    own_at = tensor_rank * own_rows
    cuts = [(own_rows - own_at, own_rows), (own_at, own_rows)] if ways == 2 else [(0, row_count)]
    rows_of = lambda t, cut: lax.dynamic_slice_in_dim(t, cut[0], cut[1], 0)

    start, position = layout(lengths[0], row_count)
    keep, left, right = rotary_tables(position)
    normed_m, keep, left, right = lax.optimization_barrier((normed_m, keep, left, right))

    out_m, d_m, mlp_mine, mlp_theirs, up_bias_grad = mlp(
        normed_m, dy, up_full, down_full, bias_up[None], ring.core[None], ring.n
    )
    normed_a, out_m = lax.optimization_barrier((normed_a, out_m))
    qkv_full, proj_t = att_full[:, :qkv_width], att_full[:, qkv_width:]
    work = [
        (mm(normed_a, qkv_full) + bias_qkv).astype(BFLOAT),
        mm(dy, proj_t).astype(BFLOAT),
        (),
    ]

    def attend_after(pair, arrived):
        if pair < pairs:
            work[0], arrived = lax.optimization_barrier((work[0], arrived))
            work[2] = attention(
                pair, work[0], work[1], keep, left, right, start[None], tuple(work[2])
            )
        return arrived

    steps = {i: functools.partial(attend_after, i) for i in range(ring.n // 2)}
    mlp_own = ring.reduce_scatter(mlp_mine, mlp_theirs, steps)
    attended, d_qkv = work[2]
    proj_grad = mm_tn(dy, attended).astype(BFLOAT)
    qkv_grad = mm_tn(normed_a, d_qkv).astype(BFLOAT)
    att_mine, att_theirs = ring.split(jnp.concatenate([qkv_grad, proj_grad], axis=1))
    attended, att_theirs = lax.optimization_barrier((attended, att_theirs))
    att_theirs, mlp_own = lax.optimization_barrier((att_theirs, mlp_own))
    qkv_bias_grad = jnp.sum(d_qkv, axis=0, dtype=FLOAT)

    out_part = [mm_nt(rows_of(attended, c), proj_t) + rows_of(out_m, c) for c in cuts]
    d_m = [rows_of(d_m, c) for c in cuts]
    held = {}
    if ways == 2:
        held["out"] = lax.all_gather(out_part[0].astype(BFLOAT), "tensor")

    def norm_work(arrived):
        arrived, grad = lax.optimization_barrier((arrived, d_qkv))
        held["d_a"] = [mm_nt(rows_of(grad, c), qkv_full) for c in cuts]
        held["e"] = [a * small[0] + m * small[2] for a, m in zip(held["d_a"], d_m)]
        return arrived

    def small_sums(d_a):
        out_bias_grad = jnp.sum(cotangent, axis=0, dtype=FLOAT)
        qkv_rows = lax.dynamic_update_slice_in_dim(
            jnp.zeros((3, D), FLOAT),
            from_pair_major(qkv_bias_grad[None])[0],
            tensor_rank * local_width,
            1,
        )
        up_rows = lax.dynamic_update_slice_in_dim(
            jnp.zeros((4 * D,), FLOAT), up_bias_grad[0], tensor_rank * hidden_width, 0
        )
        with_hat = lambda ds: sum(
            jnp.sum(d * rows_of(xhat, c), axis=0)[None] for d, c in zip(ds, cuts)
        )
        plain = lambda ds: sum(jnp.sum(d, axis=0)[None] for d in ds)
        return jnp.concatenate(
            [
                with_hat(d_a),
                plain(d_a),
                with_hat(d_m),
                plain(d_m),
                qkv_rows,
                out_bias_grad[None],
                up_rows.reshape(4, D),
                out_bias_grad[None],
            ],
            axis=0,
        )

    def small_work(pair):
        held["small"] = small_sums(held["d_a"])
        pair, held["small"] = lax.optimization_barrier((pair, held["small"]))
        return pair

    def out_work(arrived):
        if ways == 2:
            arrived, held["out"] = lax.optimization_barrier((arrived, held["out"]))
        return arrived

    def e_exchange(pair):
        if ways == 2:
            pair, e_other = lax.optimization_barrier((pair, held["e"][0].astype(BFLOAT)))
            held["e_came"] = swap(e_other)
        return pair

    last = ring.n // 2
    att_own = ring.reduce_scatter(
        att_mine, att_theirs, {0: norm_work, last: out_work}, {last - 1: small_work, last: e_exchange}
    )
    if ways == 2:
        out_came = lax.dynamic_index_in_dim(held["out"], 1 - tensor_rank, 0, keepdims=False)
        summed = out_came.astype(FLOAT) + out_part[1]
        e_own = held["e_came"].astype(FLOAT) + held["e"][1]
    else:
        summed, e_own = (
            lax.psum_scatter(
                part[0].astype(BFLOAT), "tensor", scatter_dimension=0, tiled=True
            ).astype(FLOAT)
            for part in (out_part, held["e"])
        )
    own_inputs = tokens.astype(FLOAT)
    block_out = (own_inputs + summed + small[7] + small[12]).astype(BFLOAT)
    own_hat = rows_of(xhat, (own_at, own_rows))
    own_inv = rows_of(inv_dev, (own_at, own_rows))
    token_grad = cotangent.astype(FLOAT) + own_inv * (
        e_own
        - jnp.mean(e_own, axis=-1, keepdims=True)
        - own_hat * jnp.mean(e_own * own_hat, axis=-1, keepdims=True)
    )

    small_both = held["small"] + swap(held["small"]) if ways == 2 else lax.psum(held["small"], "tensor")
    reach = 1
    while reach < groups:
        small_both += lax.ppermute(small_both, "dp", [(i, i ^ reach) for i in range(groups)])
        reach *= 2
    small_width = small_params.shape[1]
    small_grad = lax.dynamic_slice_in_dim(
        small_both,
        (lax.axis_index("dp") * ways + tensor_rank) * small_width,
        small_width,
        1,
    )
    mlp_parts = mlp_own.reshape(in_rows, -1, 2, mlp_chunk(hidden_width))
    qkv_owned = from_pair_major(att_own[:, :qkv_width])
    proj_owned = att_own[:, qkv_width:att_width].T
    up_owned = mlp_parts[:, :, 0].reshape(in_rows, hidden_width)
    down_owned = mlp_parts[:, :, 1].reshape(in_rows, hidden_width).T
    qkv_new = adamw(qkv_weight, qkv_first, qkv_second, qkv_owned, D ** (-0.5), DECAY)
    proj_new = adamw(proj_weight, proj_first, proj_second, proj_owned, (D // 64) ** (-0.5), DECAY)
    up_new = adamw(up_weight, up_first, up_second, up_owned, D ** (-0.5), DECAY)
    down_new = adamw(down_weight, down_first, down_second, down_owned, FF ** (-0.5), DECAY)
    small_new = adamw(small_params, small_first, small_second, small_grad, SMALL_RATE, 0.0)
    return (block_out, token_grad) + qkv_new + proj_new + up_new + down_new + small_new


def solution(mesh):
    rows = P(("dp", "tensor"), None)
    weights = (P("dp", None, "tensor"), P("tensor", "dp"), P("dp", "tensor"), P("tensor", "dp"))
    small = P(None, ("dp", "tensor"))
    return jax.shard_map(
        functools.partial(per_device, mesh.shape["tensor"], mesh.shape["dp"]),
        mesh=mesh,
        in_specs=(rows, rows, P("dp", None)) + 3 * (weights + (small,)),
        out_specs=(rows, rows) + tuple(w for w in weights + (small,) for _ in range(3)),
        check_vma=False,
    )
```

```python
import functools
import math

import jax
import jax.numpy as jnp
from jax import lax
from jax.experimental import pallas as pl
from jax.experimental.pallas import tpu as pltpu
from jax.sharding import PartitionSpec as P

D = 1024
HD = 64
FF = 4096
ROT = 16
STEP = 10

EPS_NORM = 1e-05
BETA_ONE = 0.9
BETA_TWO = 0.95
EPS_ADAM = 1e-08
DECAY = 0.01
SMALL_RATE = 0.3
BFLOAT = jnp.bfloat16
FLOAT = jnp.float32
ROOT_HALF = 1.0 / math.sqrt(2.0)
INV_ROOT_TAU = 1.0 / math.sqrt(2.0 * math.pi)
PAIR = 2 * HD
QB = 128
MASKED = -1e30


def layout(lengths_row, row_count):
    starts = jnp.cumsum(lengths_row) - lengths_row
    row_index = jnp.arange(row_count, dtype=jnp.int32)
    own_start = jnp.max(
        jnp.where(row_index[:, None] >= starts[None, :], starts[None, :], 0), axis=1
    )
    return own_start, row_index - own_start


def rotary_tables(position):
    half = ROT // 2
    lane = jnp.arange(PAIR, dtype=jnp.int32) % HD
    frequency = 10000.0 ** (-(2.0 * jnp.arange(half, dtype=FLOAT)) / ROT)
    angles = position.astype(FLOAT)[:, None] * frequency[None, :]
    cos = jnp.tile(jnp.cos(angles), (1, PAIR // half))
    sin = jnp.tile(jnp.sin(angles), (1, PAIR // half))
    keep = jnp.where(lane[None] < ROT, cos, 1.0)
    from_left = jnp.where((lane[None] >= half) & (lane[None] < ROT), sin, 0.0)
    from_right = jnp.where(lane[None] < half, -sin, 0.0)
    return keep, from_left, from_right


def attention_kernel(
    pre_ref, grad_ref, keep_ref, left_ref, right_ref, start_ref,
    att_ref, dpre_ref,
    q2_ref, g2_ref, k_ref, kt_ref, v_ref, vt_ref, dk_ref, dv_ref,
):
    rows = pre_ref.shape[0]
    blocks = rows // QB
    half = ROT // 2

    def turn(x, sign, at):
        here = pl.ds(at, x.shape[0])
        return (
            x * keep_ref[here, :]
            + sign * (
                pltpu.roll(x, half, 1) * left_ref[here, :]
                + pltpu.roll(x, PAIR - half, 1) * right_ref[here, :]
            )
        )

    first = lax.broadcasted_iota(jnp.int32, (QB, PAIR), 1) < HD
    top = lax.broadcasted_iota(jnp.int32, (PAIR, QB), 0) < HD
    zero = jnp.zeros((QB, PAIR), FLOAT)
    for i in range(blocks):
        here = pl.ds(i * QB, QB)
        q = turn(pre_ref[here, :PAIR].astype(FLOAT), 1.0, i * QB) * (HD ** -0.5)
        q2_ref[pl.ds(2 * i * QB, QB), :] = jnp.where(first, q, zero).astype(BFLOAT)
        q2_ref[pl.ds((2 * i + 1) * QB, QB), :] = jnp.where(first, zero, q).astype(BFLOAT)
        g = grad_ref[here, :].astype(FLOAT)
        g2_ref[pl.ds(2 * i * QB, QB), :] = jnp.where(first, g, zero).astype(BFLOAT)
        g2_ref[pl.ds((2 * i + 1) * QB, QB), :] = jnp.where(first, zero, g).astype(BFLOAT)
        k = turn(pre_ref[here, PAIR:2 * PAIR].astype(FLOAT), 1.0, i * QB)
        k_ref[here, :] = k.astype(BFLOAT)
        kt_ref[:, here] = k.T.astype(BFLOAT)
        v = pre_ref[here, 2 * PAIR:]
        v_ref[here, :] = v
        vt_ref[:, here] = v.astype(FLOAT).T.astype(BFLOAT)

    for i in range(blocks):
        n = (i + 1) * QB
        here = pl.ds(i * QB, QB)
        q2 = q2_ref[pl.ds(2 * i * QB, 2 * QB), :]
        g2 = g2_ref[pl.ds(2 * i * QB, 2 * QB), :]
        s = lax.dot_general(
            k_ref[:n, :], q2, (((1,), (1,)), ((), ())), preferred_element_type=FLOAT
        )
        start = start_ref[:, here]
        start = jnp.concatenate([start, start], axis=1)
        lane = lax.broadcasted_iota(jnp.int32, (QB, 2 * QB), 1)
        row = lax.broadcasted_iota(jnp.int32, (QB, 2 * QB), 0)
        causal = row <= jnp.where(lane < QB, lane, lane - QB)
        tiles = []
        for j in range(i + 1):
            tile = s[j * QB:(j + 1) * QB]
            allowed = None
            if j == 0 or i * QB >= 1024:
                allowed = row + j * QB >= start
            if j == i:
                allowed = causal if allowed is None else allowed & causal
            tiles.append(tile if allowed is None else jnp.where(allowed, tile, MASKED))
        s = jnp.concatenate(tiles, axis=0) if i else tiles[0]
        e = jnp.exp(s - jnp.max(s, axis=0, keepdims=True))
        p = e * (1.0 / jnp.sum(e, axis=0, keepdims=True))
        dp = lax.dot_general(
            v_ref[:n, :], g2, (((1,), (1,)), ((), ())), preferred_element_type=FLOAT
        )
        delta = jnp.sum(dp * p, axis=0, keepdims=True)
        ds = (p * (dp - delta)).astype(BFLOAT)
        p = p.astype(BFLOAT)
        o = jnp.dot(vt_ref[:, :n], p, preferred_element_type=FLOAT)
        o = jnp.where(top, o[:, :QB], o[:, QB:])
        att_ref[here, :] = o.T.astype(BFLOAT)
        dq = jnp.dot(kt_ref[:, :n], ds, preferred_element_type=FLOAT)
        dq = jnp.where(top, dq[:, :QB], dq[:, QB:]) * (HD ** -0.5)
        dpre_ref[here, :PAIR] = turn(dq.T, -1.0, i * QB).astype(BFLOAT)
        dk = jnp.dot(ds, q2, preferred_element_type=FLOAT)
        dv = jnp.dot(p, g2, preferred_element_type=FLOAT)
        if i:
            before = n - QB
            dk_ref[:before, :] += dk[:before]
            dv_ref[:before, :] += dv[:before]
            dk_ref[here, :] = dk[before:]
            dv_ref[here, :] = dv[before:]
        else:
            dk_ref[here, :] = dk
            dv_ref[here, :] = dv

    for i in range(blocks):
        here = pl.ds(i * QB, QB)
        dpre_ref[here, PAIR:2 * PAIR] = turn(dk_ref[here, :], -1.0, i * QB).astype(BFLOAT)
        dpre_ref[here, 2 * PAIR:] = dv_ref[here, :].astype(BFLOAT)


def attention(pair, qkv_pre, d_attended, keep, left, right, start, so_far):
    rows, width = d_attended.shape
    whole = lambda _: (0, 0)
    mine = lambda _: (0, pair)
    kernel = attention_kernel
    if so_far:
        kernel = lambda *refs: attention_kernel(*refs[:6], *refs[8:])
    return pl.pallas_call(
        kernel,
        grid=(1,),
        in_specs=[
            pl.BlockSpec((rows, 3 * PAIR), mine),
            pl.BlockSpec((rows, PAIR), mine),
            pl.BlockSpec((rows, PAIR), whole),
            pl.BlockSpec((rows, PAIR), whole),
            pl.BlockSpec((rows, PAIR), whole),
            pl.BlockSpec((1, rows), whole),
        ] + [pl.BlockSpec(memory_space=pl.ANY)] * len(so_far),
        out_specs=[
            pl.BlockSpec((rows, PAIR), mine),
            pl.BlockSpec((rows, 3 * PAIR), mine),
        ],
        out_shape=[
            jax.ShapeDtypeStruct((rows, width), BFLOAT),
            jax.ShapeDtypeStruct((rows, 3 * width), BFLOAT),
        ],
        input_output_aliases={6: 0, 7: 1} if so_far else {},
        scratch_shapes=[
            pltpu.VMEM((2 * rows, PAIR), BFLOAT),
            pltpu.VMEM((2 * rows, PAIR), BFLOAT),
            pltpu.VMEM((rows, PAIR), BFLOAT),
            pltpu.VMEM((PAIR, rows), BFLOAT),
            pltpu.VMEM((rows, PAIR), BFLOAT),
            pltpu.VMEM((PAIR, rows), BFLOAT),
            pltpu.VMEM((rows, PAIR), FLOAT),
            pltpu.VMEM((rows, PAIR), FLOAT),
        ],
        compiler_params=pltpu.CompilerParams(vmem_limit_bytes=32 * 1024 * 1024),
        cost_estimate=pl.CostEstimate(
            flops=56 * rows * rows * PAIR,
            bytes_accessed=rows * PAIR * 28,
            transcendentals=rows * rows,
        ),
        name="attention",
    )(qkv_pre, d_attended, keep, left, right, start, *so_far)


def mlp_kernel(
    chips,
    core_ref, x_ref, dy_ref, up_ref, down_ref, bias_ref,
    out_ref, dx_ref, mine_ref, theirs_ref, bias_grad_ref,
    xt_ref, dyt_ref, h_ref, dp_ref,
):
    rows = x_ref.shape[0]
    tile = next(t for t in (384, 128, rows) if rows % t == 0)

    @pl.when(pl.program_id(0) == 0)
    def _():
        for i in range(rows // QB):
            here = pl.ds(i * QB, QB)
            xt_ref[:, here] = x_ref[here, :].astype(FLOAT).T.astype(BFLOAT)
            dyt_ref[:, here] = dy_ref[here, :].astype(FLOAT).T.astype(BFLOAT)
        out_ref[...] = jnp.zeros_like(out_ref)
        dx_ref[...] = jnp.zeros_like(dx_ref)

    up, down, bias = up_ref[...], down_ref[...], bias_ref[...]
    bias_grad = jnp.zeros(bias.shape, FLOAT)
    for i in range(rows // tile):
        here = pl.ds(i * tile, tile)
        pre = mm(x_ref[here, :], up) + bias
        dh = mm(dy_ref[here, :], down)
        cdf = 0.5 * (1.0 + lax.erf(pre * ROOT_HALF))
        density = jnp.exp(-0.5 * pre * pre) * INV_ROOT_TAU
        h = (pre * cdf).astype(BFLOAT)
        dp = (dh * (cdf + pre * density)).astype(BFLOAT)
        h_ref[here, :] = h
        dp_ref[here, :] = dp
        bias_grad += jnp.sum(dp.astype(FLOAT), axis=0, keepdims=True)
        out_ref[here, :] += mm_nt(h, down)
        dx_ref[here, :] += mm_nt(dp, up)
    bias_grad_ref[...] = bias_grad
    first = core_ref[0] == 0
    chunk = up.shape[1]
    for at, grad in (
        (0, mm(xt_ref[...], dp_ref[...])),
        (chunk, mm(dyt_ref[...], h_ref[...])),
    ):
        parts = grad.reshape(chips, 2, -1, chunk)
        even, odd = (parts[:, core].reshape(-1, chunk) for core in range(2))
        mine_ref[:, at:at + chunk] = jnp.where(first, even, odd).astype(BFLOAT)
        theirs_ref[:, at:at + chunk] = jnp.where(first, odd, even).astype(BFLOAT)


def mlp_chunk(hidden):
    return min(512, hidden)


def mlp(normed, dy, up_full, down_t, bias, core, chips):
    rows, width = normed.shape
    hidden = up_full.shape[1]
    chunk = mlp_chunk(hidden)
    whole = lambda c: (0, 0)
    part = lambda c: (0, c)
    once = pl.BlockSpec((rows, width), whole, pipeline_mode=pl.Buffered(1))
    return pl.pallas_call(
        functools.partial(mlp_kernel, chips),
        grid=(hidden // chunk,),
        in_specs=[
            pl.BlockSpec(memory_space=pltpu.SMEM),
            once,
            once,
            pl.BlockSpec((width, chunk), part),
            pl.BlockSpec((width, chunk), part),
            pl.BlockSpec((1, chunk), part),
        ],
        out_specs=[
            once,
            once,
            pl.BlockSpec((width // 2, 2 * chunk), part),
            pl.BlockSpec((width // 2, 2 * chunk), part),
            pl.BlockSpec((1, chunk), part),
        ],
        out_shape=[
            jax.ShapeDtypeStruct((rows, width), FLOAT),
            jax.ShapeDtypeStruct((rows, width), FLOAT),
            jax.ShapeDtypeStruct((width // 2, 2 * hidden), BFLOAT),
            jax.ShapeDtypeStruct((width // 2, 2 * hidden), BFLOAT),
            jax.ShapeDtypeStruct((1, hidden), FLOAT),
        ],
        scratch_shapes=[
            pltpu.VMEM((width, rows), BFLOAT),
            pltpu.VMEM((width, rows), BFLOAT),
            pltpu.VMEM((rows, chunk), BFLOAT),
            pltpu.VMEM((rows, chunk), BFLOAT),
        ],
        compiler_params=pltpu.CompilerParams(vmem_limit_bytes=48 * 1024 * 1024),
        cost_estimate=pl.CostEstimate(
            flops=20 * rows * width * hidden,
            bytes_accessed=rows * width * 12 + width * hidden * 8,
            transcendentals=rows * hidden * 2,
        ),
        name="mlp",
    )(core, normed, dy, up_full, down_t, bias)


def adamw(weight, moment, second, gradient, step_rate, decay_rate):
    moment = BETA_ONE * moment + (1.0 - BETA_ONE) * gradient
    second = BETA_TWO * second + (1.0 - BETA_TWO) * gradient * gradient
    moment_hat = moment / (1.0 - BETA_ONE**STEP)
    second_hat = second / (1.0 - BETA_TWO**STEP)
    weight = weight - step_rate * (
        moment_hat / (jnp.sqrt(second_hat) + EPS_ADAM) + decay_rate * weight
    )
    return (moment, second, weight)


def mm(a, b):
    return jnp.dot(a, b, preferred_element_type=FLOAT)


def mm_nt(a, b):
    return lax.dot_general(a, b, (((1,), (1,)), ((), ())), preferred_element_type=FLOAT)


def mm_tn(a, b):
    return lax.dot_general(a, b, (((0,), (0,)), ((), ())), preferred_element_type=FLOAT)


def turn_order(index, chips):
    if chips == 8:
        return jnp.where(index < 4, 2 * index, 15 - 2 * index)
    return jnp.where(index < chips // 2, index, 3 * chips // 2 - 1 - index)


class Ring:
    def __init__(self, devices):
        self.n = n = devices // 2
        assert n & (n - 1) == 0
        order = [2 * i if i < 4 else 15 - 2 * i for i in range(n)]
        if n != 8:
            order = [i if i < n // 2 else 3 * n // 2 - 1 - i for i in range(n)]
        me = lax.axis_index("dp")
        self.core = me & 1
        chip = lax.shift_right_logical(me, 1)
        if n == 8:
            z = lax.shift_right_logical(chip, 1)
            self.place = jnp.where(chip & 1 == 0, z, 7 - z)
        else:
            self.place = turn_order(chip, n)
        hop = lambda step: [
            (2 * order[i] + k, 2 * order[(i + step) % n] + k) for i in range(n) for k in range(2)
        ]
        self.up_pairs, self.down_pairs = hop(1), hop(n - 1)
        self.twin_pairs = [(2 * c + k, 2 * c + 1 - k) for c in range(n) for k in range(2)]

    def up(self, x):
        return lax.ppermute(x, "dp", self.up_pairs)

    def down(self, x):
        return lax.ppermute(x, "dp", self.down_pairs)

    def twin(self, x):
        return lax.ppermute(x, "dp", self.twin_pairs)

    def chip_at(self, offset):
        return turn_order((self.place + (offset + self.n)) & (self.n - 1), self.n)

    def split(self, grad):
        parts = grad.reshape(self.n, 2, grad.shape[0] // (2 * self.n), grad.shape[1])
        return tuple(
            lax.dynamic_index_in_dim(parts, core, 1, keepdims=False).reshape(-1, grad.shape[1])
            for core in (self.core, 1 - self.core)
        )

    def reduce_scatter(self, mine, theirs, after, before={}):
        n, columns = self.n, mine.shape[1]
        rows = mine.shape[0] // n
        cut = rows // 2
        far = n // 2

        def send(step, move, *pair):
            pair = lax.optimization_barrier(tuple(t.astype(BFLOAT) for t in pair))
            pair = before[step](pair) if step in before else pair
            arrived = tuple(m(t) for m, t in zip(move, pair))
            return after[step](arrived) if step in after else arrived

        mine = mine.reshape(n, rows, columns)
        came = send(0, (self.twin,), theirs)[0].reshape(n, rows, columns)

        def here(offset):
            at = (self.chip_at(offset), 0, 0)
            own, twin = (lax.dynamic_slice(t, at, (1, rows, columns))[0] for t in (mine, came))
            return own.astype(FLOAT) + twin.astype(FLOAT)

        both = (self.up, self.down)
        split = here(far)
        going_up, going_down = send(1, both, split[:cut], split[cut:])
        for step in range(2, far + 1):
            up_sum, down_sum = here(far + 1 - step), here(step - far - 1)
            going_up, going_down = going_up.astype(FLOAT), going_down.astype(FLOAT)
            if step == 2:
                going_up = jnp.concatenate([up_sum[:cut] + going_up, up_sum[cut:]], axis=0)
                going_down = jnp.concatenate([down_sum[:cut], down_sum[cut:] + going_down], axis=0)
            else:
                going_up, going_down = up_sum + going_up, down_sum + going_down
            going_up, going_down = send(step, both, going_up, going_down)
        return here(0) + going_up.astype(FLOAT) + going_down.astype(FLOAT)

    def all_gather(self, shards, before):
        n = self.n
        fulls = [unwritten((n, 2) + shard.shape, shard.dtype) for shard in shards]

        def put(i, offset, block, row=0):
            chip = self.chip_at(offset)
            for core, part in ((self.core, block), (1 - self.core, self.twin(block))):
                fulls[i] = lax.dynamic_update_slice(
                    fulls[i], part[None, None], (chip, core, row, 0)
                )

        moving = [(shard, shard) for shard in shards]
        for step in range(1, n // 2 + 1):
            if step in before:
                moving = before[step](moving)
            last = step == n // 2
            arrived = []
            for below, above in moving:
                cut = below.shape[0] // 2
                if last:
                    below, above = below[:cut], above[cut:]
                arrived.append((self.up(below), self.down(above)))
            for i, (below, above) in enumerate(moving):
                if step == 1:
                    put(i, 0, shards[i])
                elif step <= n // 2:
                    put(i, 1 - step, below)
                    put(i, step - 1, above)
            moving = arrived
        for i, (below, above) in enumerate(moving):
            put(i, n // 2, below)
            put(i, n // 2, above, below.shape[0])
        return [full.reshape(-1, full.shape[-1]) for full in fulls]


def unwritten(shape, dtype):
    return pl.pallas_call(
        lambda out_ref: None,
        out_specs=pl.BlockSpec(memory_space=pl.ANY),
        out_shape=jax.ShapeDtypeStruct(shape, dtype),
        name="unwritten",
    )()


def tie(value, *others):
    return lax.optimization_barrier((value,) + others)[0]


def swap(x):
    return lax.ppermute(x, "tensor", [(0, 1), (1, 0)])


def gather_rows(part, ways, axis=0):
    if ways != 2:
        return lax.all_gather(part, "tensor", axis=axis, tiled=True)
    came = swap(part)
    first = lax.axis_index("tensor") == 0
    return jnp.concatenate(
        [jnp.where(first, part, came), jnp.where(first, came, part)], axis=axis
    )


def per_device(
    ways, groups,
    tokens, cotangent, lengths,
    qkv_weight, proj_weight, up_weight, down_weight, small_params,
    qkv_first, proj_first, up_first, down_first, small_first,
    qkv_second, proj_second, up_second, down_second, small_second,
):
    ring = Ring(groups)
    tensor_rank = lax.axis_index("tensor")
    in_rows = qkv_weight.shape[0]
    local_width = qkv_weight.shape[2]
    hidden_width = up_weight.shape[1]
    pairs = local_width // PAIR
    own_rows = tokens.shape[0]
    row_count = own_rows * ways
    small_rows = small_params.shape[0]
    qkv_width = 3 * local_width
    att_width = qkv_width + local_width

    def pair_major(t):
        return (
            t.reshape(t.shape[0], 3, pairs, PAIR)
            .transpose(0, 2, 1, 3)
            .reshape(t.shape[0], qkv_width)
        )

    def from_pair_major(t):
        return (
            t.reshape(t.shape[0], pairs, 3, PAIR)
            .transpose(0, 2, 1, 3)
            .reshape(t.shape[0], 3, local_width)
        )

    small_here = gather_rows(small_params, ways, axis=1).T
    small_high = lax.reduce_precision(small_here, 8, 7)
    small_shard = jnp.concatenate(
        [
            small_high.astype(BFLOAT),
            (small_here - small_high).astype(BFLOAT),
            jnp.zeros((in_rows, PAIR - 2 * small_rows), BFLOAT),
        ],
        axis=1,
    )
    up_shard = up_weight.astype(BFLOAT)
    down_shard = jnp.concatenate([down_weight.T.astype(BFLOAT), small_shard], axis=1)
    att_shard = jnp.concatenate(
        [pair_major(qkv_weight.astype(BFLOAT)), proj_weight.T.astype(BFLOAT)], axis=1
    )
    both_in = jnp.stack([tokens, cotangent])
    up_shard, both_in = lax.optimization_barrier((up_shard, both_in))
    both_in = lax.all_gather(both_in, "tensor", axis=1, tiled=True)
    rows_in, dy = both_in[0], both_in[1]
    up_full, down_full = ring.all_gather([up_shard, down_shard], {})
    small = down_full[:, hidden_width:hidden_width + 2 * small_rows].astype(FLOAT).T
    small = small[:small_rows] + small[small_rows:]
    att_shard, up_full, down_full = lax.optimization_barrier((att_shard, up_full, down_full))
    att_full = lax.all_gather(att_shard, "dp", axis=0, tiled=True)

    bias_qkv = pair_major(
        lax.dynamic_slice_in_dim(small[4:7], tensor_rank * local_width, local_width, 1)[None]
    )[0]
    bias_up = lax.dynamic_slice_in_dim(
        small[8:12].reshape(4 * D), tensor_rank * hidden_width, hidden_width, 0
    )

    inputs = rows_in.astype(FLOAT)
    average = jnp.mean(inputs, axis=-1, keepdims=True)
    centred = inputs - average
    variance = jnp.mean(centred * centred, axis=-1, keepdims=True)
    inv_dev = lax.rsqrt(variance + EPS_NORM)
    xhat = centred * inv_dev
    normed_a = (xhat * small[0] + small[1]).astype(BFLOAT)
    normed_m = (xhat * small[2] + small[3]).astype(BFLOAT)

    own_at = tensor_rank * own_rows
    cuts = [(own_rows - own_at, own_rows), (own_at, own_rows)] if ways == 2 else [(0, row_count)]
    rows_of = lambda t, cut: lax.dynamic_slice_in_dim(t, cut[0], cut[1], 0)

    start, position = layout(lengths[0], row_count)
    keep, left, right = rotary_tables(position)
    out_bias_grad = jnp.sum(cotangent, axis=0, dtype=FLOAT)[None]
    normed_m, keep, left, right, out_bias_grad = lax.optimization_barrier(
        (normed_m, keep, left, right, out_bias_grad)
    )

    out_m, d_m, mlp_mine, mlp_theirs, up_bias_grad = mlp(
        normed_m, dy, up_full, down_full, bias_up[None], ring.core[None], ring.n
    )
    up_rows = lax.dynamic_update_slice_in_dim(
        jnp.zeros((4 * D,), FLOAT), up_bias_grad[0], tensor_rank * hidden_width, 0
    ).reshape(4, D)
    normed_a, out_m, up_rows = lax.optimization_barrier((normed_a, out_m, up_rows))
    qkv_full, proj_t = att_full[:, :qkv_width], att_full[:, qkv_width:]
    work = [
        (mm(normed_a, qkv_full) + bias_qkv).astype(BFLOAT),
        mm(dy, proj_t).astype(BFLOAT),
        (),
    ]

    def attend_after(pair, arrived):
        if pair < pairs:
            work[0], arrived = lax.optimization_barrier((work[0], arrived))
            work[2] = attention(
                pair, work[0], work[1], keep, left, right, start[None], tuple(work[2])
            )
        return arrived

    steps = {i: functools.partial(attend_after, i) for i in range(ring.n // 2)}
    mlp_own = ring.reduce_scatter(mlp_mine, mlp_theirs, steps)
    attended, d_qkv = work[2]
    proj_grad = mm_tn(dy, attended).astype(BFLOAT)
    qkv_grad = mm_tn(normed_a, d_qkv).astype(BFLOAT)
    att_mine, att_theirs = ring.split(jnp.concatenate([qkv_grad, proj_grad], axis=1))
    attended, att_theirs = lax.optimization_barrier((attended, att_theirs))
    att_theirs, mlp_own = lax.optimization_barrier((att_theirs, mlp_own))

    out_part = [mm_nt(rows_of(attended, c), proj_t) + rows_of(out_m, c) for c in cuts]
    d_m = [rows_of(d_m, c) for c in cuts]
    held = {}
    if ways == 2:
        held["out"] = lax.all_gather(out_part[0].astype(BFLOAT), "tensor")

    def norm_work(arrived):
        arrived, grad = lax.optimization_barrier((arrived, d_qkv))
        held["d_a"] = [mm_nt(rows_of(grad, c), qkv_full) for c in cuts]
        held["sums"] = [
            sums(ds) for ds in (held["d_a"], d_m) for sums in (with_hat, plain)
        ]
        held["e"] = [a * small[0] + m * small[2] for a, m in zip(held["d_a"], d_m)]
        return arrived

    with_hat = lambda ds: sum(
        jnp.sum(d * rows_of(xhat, c), axis=0)[None] for d, c in zip(ds, cuts)
    )
    plain = lambda ds: sum(jnp.sum(d, axis=0)[None] for d in ds)

    def small_sums(grad, norm_sums):
        qkv_rows = lax.dynamic_update_slice_in_dim(
            jnp.zeros((3, D), FLOAT),
            from_pair_major(jnp.sum(grad, axis=0, dtype=FLOAT)[None])[0],
            tensor_rank * local_width,
            1,
        )
        return jnp.concatenate(
            norm_sums + [qkv_rows, out_bias_grad, up_rows, out_bias_grad],
            axis=0,
        )

    def out_work(arrived):
        if ways == 2:
            arrived, held["out"] = lax.optimization_barrier((arrived, held["out"]))
        arrived, held["late"] = lax.optimization_barrier((arrived, (d_qkv, held["sums"])))
        return arrived

    def last_send(pair):
        if ways == 2:
            pair, e_other = lax.optimization_barrier((pair, held["e"][0].astype(BFLOAT)))
            held["e_came"] = swap(e_other)
        return pair

    last = ring.n // 2
    att_own = ring.reduce_scatter(
        att_mine, att_theirs, {0: norm_work, last: out_work}, {last: last_send}
    )
    if ways == 2:
        out_came = lax.dynamic_index_in_dim(held["out"], 1 - tensor_rank, 0, keepdims=False)
        summed = out_came.astype(FLOAT) + out_part[1]
        e_own = tie(held["e_came"], held["late"]).astype(FLOAT) + held["e"][1]
    else:
        summed, e_own = (
            lax.psum_scatter(
                part[0].astype(BFLOAT), "tensor", scatter_dimension=0, tiled=True
            ).astype(FLOAT)
            for part in (out_part, held["e"])
        )
    own_inputs = tokens.astype(FLOAT)
    block_out = (own_inputs + summed + small[7] + small[12]).astype(BFLOAT)
    own_hat = rows_of(xhat, (own_at, own_rows))
    own_inv = rows_of(inv_dev, (own_at, own_rows))
    token_grad = cotangent.astype(FLOAT) + own_inv * (
        e_own
        - jnp.mean(e_own, axis=-1, keepdims=True)
        - own_hat * jnp.mean(e_own * own_hat, axis=-1, keepdims=True)
    )

    held["small"] = small_sums(*held["late"])
    small_both = held["small"] + swap(held["small"]) if ways == 2 else lax.psum(held["small"], "tensor")
    reach = 1
    while reach < groups:
        small_both += lax.ppermute(small_both, "dp", [(i, i ^ reach) for i in range(groups)])
        reach *= 2
    small_width = small_params.shape[1]
    small_grad = lax.dynamic_slice_in_dim(
        small_both,
        (lax.axis_index("dp") * ways + tensor_rank) * small_width,
        small_width,
        1,
    )
    mlp_parts = mlp_own.reshape(in_rows, -1, 2, mlp_chunk(hidden_width))
    qkv_owned = from_pair_major(att_own[:, :qkv_width])
    proj_owned = att_own[:, qkv_width:att_width].T
    up_owned = mlp_parts[:, :, 0].reshape(in_rows, hidden_width)
    down_owned = mlp_parts[:, :, 1].reshape(in_rows, hidden_width).T
    qkv_new = adamw(qkv_weight, qkv_first, qkv_second, qkv_owned, D ** (-0.5), DECAY)
    proj_new = adamw(proj_weight, proj_first, proj_second, proj_owned, (D // 64) ** (-0.5), DECAY)
    up_new = adamw(up_weight, up_first, up_second, up_owned, D ** (-0.5), DECAY)
    down_new = adamw(down_weight, down_first, down_second, down_owned, FF ** (-0.5), DECAY)
    small_new = adamw(small_params, small_first, small_second, small_grad, SMALL_RATE, 0.0)
    return (block_out, token_grad) + qkv_new + proj_new + up_new + down_new + small_new


def solution(mesh):
    rows = P(("dp", "tensor"), None)
    weights = (P("dp", None, "tensor"), P("tensor", "dp"), P("dp", "tensor"), P("tensor", "dp"))
    small = P(None, ("dp", "tensor"))
    return jax.shard_map(
        functools.partial(per_device, mesh.shape["tensor"], mesh.shape["dp"]),
        mesh=mesh,
        in_specs=(rows, rows, P("dp", None)) + 3 * (weights + (small,)),
        out_specs=(rows, rows) + tuple(w for w in weights + (small,) for _ in range(3)),
        check_vma=False,
    )
```

```python
import functools
import math

import jax
import jax.numpy as jnp
from jax import lax
from jax.experimental import pallas as pl
from jax.experimental.pallas import tpu as pltpu
from jax.sharding import PartitionSpec as P

D = 1024
HD = 64
FF = 4096
ROT = 16
STEP = 10

EPS_NORM = 1e-05
BETA_ONE = 0.9
BETA_TWO = 0.95
EPS_ADAM = 1e-08
DECAY = 0.01
SMALL_RATE = 0.3
BFLOAT = jnp.bfloat16
FLOAT = jnp.float32
ROOT_HALF = 1.0 / math.sqrt(2.0)
INV_ROOT_TAU = 1.0 / math.sqrt(2.0 * math.pi)
PAIR = 2 * HD
QB = 128
MASKED = -1e30


def layout(lengths_row, row_count):
    starts = jnp.cumsum(lengths_row) - lengths_row
    row_index = jnp.arange(row_count, dtype=jnp.int32)
    own_start = jnp.max(
        jnp.where(row_index[:, None] >= starts[None, :], starts[None, :], 0), axis=1
    )
    return own_start, row_index - own_start


def rotary_tables(position):
    half = ROT // 2
    lane = jnp.arange(PAIR, dtype=jnp.int32) % HD
    frequency = 10000.0 ** (-(2.0 * jnp.arange(half, dtype=FLOAT)) / ROT)
    angles = position.astype(FLOAT)[:, None] * frequency[None, :]
    cos = jnp.tile(jnp.cos(angles), (1, PAIR // half))
    sin = jnp.tile(jnp.sin(angles), (1, PAIR // half))
    keep = jnp.where(lane[None] < ROT, cos, 1.0)
    from_left = jnp.where((lane[None] >= half) & (lane[None] < ROT), sin, 0.0)
    from_right = jnp.where(lane[None] < half, -sin, 0.0)
    return keep, from_left, from_right


def attention_kernel(
    pre_ref, grad_ref, keep_ref, left_ref, right_ref, start_ref,
    att_ref, dpre_ref,
    q2_ref, g2_ref, k_ref, kt_ref, v_ref, vt_ref, dk_ref, dv_ref,
):
    rows = pre_ref.shape[0]
    blocks = rows // QB
    half = ROT // 2

    def turn(x, sign, at):
        here = pl.ds(at, x.shape[0])
        return (
            x * keep_ref[here, :]
            + sign * (
                pltpu.roll(x, half, 1) * left_ref[here, :]
                + pltpu.roll(x, PAIR - half, 1) * right_ref[here, :]
            )
        )

    first = lax.broadcasted_iota(jnp.int32, (QB, PAIR), 1) < HD
    top = lax.broadcasted_iota(jnp.int32, (PAIR, QB), 0) < HD
    zero = jnp.zeros((QB, PAIR), FLOAT)
    for i in range(blocks):
        here = pl.ds(i * QB, QB)
        q = turn(pre_ref[here, :PAIR].astype(FLOAT), 1.0, i * QB) * (HD ** -0.5)
        q2_ref[pl.ds(2 * i * QB, QB), :] = jnp.where(first, q, zero).astype(BFLOAT)
        q2_ref[pl.ds((2 * i + 1) * QB, QB), :] = jnp.where(first, zero, q).astype(BFLOAT)
        g = grad_ref[here, :].astype(FLOAT)
        g2_ref[pl.ds(2 * i * QB, QB), :] = jnp.where(first, g, zero).astype(BFLOAT)
        g2_ref[pl.ds((2 * i + 1) * QB, QB), :] = jnp.where(first, zero, g).astype(BFLOAT)
        k = turn(pre_ref[here, PAIR:2 * PAIR].astype(FLOAT), 1.0, i * QB)
        k_ref[here, :] = k.astype(BFLOAT)
        kt_ref[:, here] = k.T.astype(BFLOAT)
        v = pre_ref[here, 2 * PAIR:]
        v_ref[here, :] = v
        vt_ref[:, here] = v.astype(FLOAT).T.astype(BFLOAT)

    for i in range(blocks):
        n = (i + 1) * QB
        here = pl.ds(i * QB, QB)
        q2 = q2_ref[pl.ds(2 * i * QB, 2 * QB), :]
        g2 = g2_ref[pl.ds(2 * i * QB, 2 * QB), :]
        s = lax.dot_general(
            k_ref[:n, :], q2, (((1,), (1,)), ((), ())), preferred_element_type=FLOAT
        )
        start = start_ref[:, here]
        start = jnp.concatenate([start, start], axis=1)
        lane = lax.broadcasted_iota(jnp.int32, (QB, 2 * QB), 1)
        row = lax.broadcasted_iota(jnp.int32, (QB, 2 * QB), 0)
        causal = row <= jnp.where(lane < QB, lane, lane - QB)
        tiles = []
        for j in range(i + 1):
            tile = s[j * QB:(j + 1) * QB]
            allowed = None
            if j == 0 or i * QB >= 1024:
                allowed = row + j * QB >= start
            if j == i:
                allowed = causal if allowed is None else allowed & causal
            tiles.append(tile if allowed is None else jnp.where(allowed, tile, MASKED))
        s = jnp.concatenate(tiles, axis=0) if i else tiles[0]
        e = jnp.exp(s - jnp.max(s, axis=0, keepdims=True))
        p = e * (1.0 / jnp.sum(e, axis=0, keepdims=True))
        dp = lax.dot_general(
            v_ref[:n, :], g2, (((1,), (1,)), ((), ())), preferred_element_type=FLOAT
        )
        delta = jnp.sum(dp * p, axis=0, keepdims=True)
        ds = (p * (dp - delta)).astype(BFLOAT)
        p = p.astype(BFLOAT)
        o = jnp.dot(vt_ref[:, :n], p, preferred_element_type=FLOAT)
        o = jnp.where(top, o[:, :QB], o[:, QB:])
        att_ref[here, :] = o.T.astype(BFLOAT)
        dq = jnp.dot(kt_ref[:, :n], ds, preferred_element_type=FLOAT)
        dq = jnp.where(top, dq[:, :QB], dq[:, QB:]) * (HD ** -0.5)
        dpre_ref[here, :PAIR] = turn(dq.T, -1.0, i * QB).astype(BFLOAT)
        dk = jnp.dot(ds, q2, preferred_element_type=FLOAT)
        dv = jnp.dot(p, g2, preferred_element_type=FLOAT)
        if i:
            before = n - QB
            dk_ref[:before, :] += dk[:before]
            dv_ref[:before, :] += dv[:before]
            dk_ref[here, :] = dk[before:]
            dv_ref[here, :] = dv[before:]
        else:
            dk_ref[here, :] = dk
            dv_ref[here, :] = dv

    for i in range(blocks):
        here = pl.ds(i * QB, QB)
        dpre_ref[here, PAIR:2 * PAIR] = turn(dk_ref[here, :], -1.0, i * QB).astype(BFLOAT)
        dpre_ref[here, 2 * PAIR:] = dv_ref[here, :].astype(BFLOAT)


def attention(pair, qkv_pre, d_attended, keep, left, right, start, so_far):
    rows, width = d_attended.shape
    whole = lambda _: (0, 0)
    mine = lambda _: (0, pair)
    kernel = attention_kernel
    if so_far:
        kernel = lambda *refs: attention_kernel(*refs[:6], *refs[8:])
    return pl.pallas_call(
        kernel,
        grid=(1,),
        in_specs=[
            pl.BlockSpec((rows, 3 * PAIR), mine),
            pl.BlockSpec((rows, PAIR), mine),
            pl.BlockSpec((rows, PAIR), whole),
            pl.BlockSpec((rows, PAIR), whole),
            pl.BlockSpec((rows, PAIR), whole),
            pl.BlockSpec((1, rows), whole),
        ] + [pl.BlockSpec(memory_space=pl.ANY)] * len(so_far),
        out_specs=[
            pl.BlockSpec((rows, PAIR), mine),
            pl.BlockSpec((rows, 3 * PAIR), mine),
        ],
        out_shape=[
            jax.ShapeDtypeStruct((rows, width), BFLOAT),
            jax.ShapeDtypeStruct((rows, 3 * width), BFLOAT),
        ],
        input_output_aliases={6: 0, 7: 1} if so_far else {},
        scratch_shapes=[
            pltpu.VMEM((2 * rows, PAIR), BFLOAT),
            pltpu.VMEM((2 * rows, PAIR), BFLOAT),
            pltpu.VMEM((rows, PAIR), BFLOAT),
            pltpu.VMEM((PAIR, rows), BFLOAT),
            pltpu.VMEM((rows, PAIR), BFLOAT),
            pltpu.VMEM((PAIR, rows), BFLOAT),
            pltpu.VMEM((rows, PAIR), FLOAT),
            pltpu.VMEM((rows, PAIR), FLOAT),
        ],
        compiler_params=pltpu.CompilerParams(vmem_limit_bytes=32 * 1024 * 1024),
        cost_estimate=pl.CostEstimate(
            flops=56 * rows * rows * PAIR,
            bytes_accessed=rows * PAIR * 28,
            transcendentals=rows * rows,
        ),
        name="attention",
    )(qkv_pre, d_attended, keep, left, right, start, *so_far)


def mlp_kernel(
    chips,
    core_ref, x_ref, dy_ref, up_ref, down_ref, bias_ref,
    out_ref, dx_ref, mine_ref, theirs_ref, bias_grad_ref,
    xt_ref, dyt_ref, h_ref, dp_ref,
):
    rows = x_ref.shape[0]
    tile = next(t for t in (384, 128, rows) if rows % t == 0)

    @pl.when(pl.program_id(0) == 0)
    def _():
        for i in range(rows // QB):
            here = pl.ds(i * QB, QB)
            xt_ref[:, here] = x_ref[here, :].astype(FLOAT).T.astype(BFLOAT)
            dyt_ref[:, here] = dy_ref[here, :].astype(FLOAT).T.astype(BFLOAT)
        out_ref[...] = jnp.zeros_like(out_ref)
        dx_ref[...] = jnp.zeros_like(dx_ref)

    up, down, bias = up_ref[...], down_ref[...], bias_ref[...]
    bias_grad = jnp.zeros(bias.shape, FLOAT)
    for i in range(rows // tile):
        here = pl.ds(i * tile, tile)
        pre = mm(x_ref[here, :], up) + bias
        dh = mm(dy_ref[here, :], down)
        cdf = 0.5 * (1.0 + lax.erf(pre * ROOT_HALF))
        density = jnp.exp(-0.5 * pre * pre) * INV_ROOT_TAU
        h = (pre * cdf).astype(BFLOAT)
        dp = (dh * (cdf + pre * density)).astype(BFLOAT)
        h_ref[here, :] = h
        dp_ref[here, :] = dp
        bias_grad += jnp.sum(dp.astype(FLOAT), axis=0, keepdims=True)
        out_ref[here, :] += mm_nt(h, down)
        dx_ref[here, :] += mm_nt(dp, up)
    bias_grad_ref[...] = bias_grad
    first = core_ref[0] == 0
    chunk = up.shape[1]
    for at, grad in (
        (0, mm(xt_ref[...], dp_ref[...])),
        (chunk, mm(dyt_ref[...], h_ref[...])),
    ):
        parts = grad.reshape(chips, 2, -1, chunk)
        even, odd = (parts[:, core].reshape(-1, chunk) for core in range(2))
        mine_ref[:, at:at + chunk] = jnp.where(first, even, odd).astype(BFLOAT)
        theirs_ref[:, at:at + chunk] = jnp.where(first, odd, even).astype(BFLOAT)


def mlp_chunk(hidden):
    return min(512, hidden)


def mlp(normed, dy, up_full, down_t, bias, core, chips):
    rows, width = normed.shape
    hidden = up_full.shape[1]
    chunk = mlp_chunk(hidden)
    whole = lambda c: (0, 0)
    part = lambda c: (0, c)
    once = pl.BlockSpec((rows, width), whole, pipeline_mode=pl.Buffered(1))
    return pl.pallas_call(
        functools.partial(mlp_kernel, chips),
        grid=(hidden // chunk,),
        in_specs=[
            pl.BlockSpec(memory_space=pltpu.SMEM),
            once,
            once,
            pl.BlockSpec((width, chunk), part),
            pl.BlockSpec((width, chunk), part),
            pl.BlockSpec((1, chunk), part),
        ],
        out_specs=[
            once,
            once,
            pl.BlockSpec((width // 2, 2 * chunk), part),
            pl.BlockSpec((width // 2, 2 * chunk), part),
            pl.BlockSpec((1, chunk), part),
        ],
        out_shape=[
            jax.ShapeDtypeStruct((rows, width), FLOAT),
            jax.ShapeDtypeStruct((rows, width), FLOAT),
            jax.ShapeDtypeStruct((width // 2, 2 * hidden), BFLOAT),
            jax.ShapeDtypeStruct((width // 2, 2 * hidden), BFLOAT),
            jax.ShapeDtypeStruct((1, hidden), FLOAT),
        ],
        scratch_shapes=[
            pltpu.VMEM((width, rows), BFLOAT),
            pltpu.VMEM((width, rows), BFLOAT),
            pltpu.VMEM((rows, chunk), BFLOAT),
            pltpu.VMEM((rows, chunk), BFLOAT),
        ],
        compiler_params=pltpu.CompilerParams(vmem_limit_bytes=48 * 1024 * 1024),
        cost_estimate=pl.CostEstimate(
            flops=20 * rows * width * hidden,
            bytes_accessed=rows * width * 12 + width * hidden * 8,
            transcendentals=rows * hidden * 2,
        ),
        name="mlp",
    )(core, normed, dy, up_full, down_t, bias)


def adamw(weight, moment, second, gradient, step_rate, decay_rate):
    moment = BETA_ONE * moment + (1.0 - BETA_ONE) * gradient
    second = BETA_TWO * second + (1.0 - BETA_TWO) * gradient * gradient
    moment_hat = moment / (1.0 - BETA_ONE**STEP)
    second_hat = second / (1.0 - BETA_TWO**STEP)
    weight = weight - step_rate * (
        moment_hat / (jnp.sqrt(second_hat) + EPS_ADAM) + decay_rate * weight
    )
    return (moment, second, weight)


def mm(a, b):
    return jnp.dot(a, b, preferred_element_type=FLOAT)


def mm_nt(a, b):
    return lax.dot_general(a, b, (((1,), (1,)), ((), ())), preferred_element_type=FLOAT)


def mm_tn(a, b):
    return lax.dot_general(a, b, (((0,), (0,)), ((), ())), preferred_element_type=FLOAT)


def turn_order(index, chips):
    if chips == 8:
        return jnp.where(index < 4, 2 * index, 15 - 2 * index)
    return jnp.where(index < chips // 2, index, 3 * chips // 2 - 1 - index)


class Ring:
    def __init__(self, devices):
        self.n = n = devices // 2
        assert n & (n - 1) == 0
        order = [2 * i if i < 4 else 15 - 2 * i for i in range(n)]
        if n != 8:
            order = [i if i < n // 2 else 3 * n // 2 - 1 - i for i in range(n)]
        me = lax.axis_index("dp")
        self.core = me & 1
        chip = lax.shift_right_logical(me, 1)
        if n == 8:
            z = lax.shift_right_logical(chip, 1)
            self.place = jnp.where(chip & 1 == 0, z, 7 - z)
        else:
            self.place = turn_order(chip, n)
        hop = lambda step: [
            (2 * order[i] + k, 2 * order[(i + step) % n] + k) for i in range(n) for k in range(2)
        ]
        self.up_pairs, self.down_pairs = hop(1), hop(n - 1)
        self.twin_pairs = [(2 * c + k, 2 * c + 1 - k) for c in range(n) for k in range(2)]

    def up(self, x):
        return lax.ppermute(x, "dp", self.up_pairs)

    def down(self, x):
        return lax.ppermute(x, "dp", self.down_pairs)

    def twin(self, x):
        return lax.ppermute(x, "dp", self.twin_pairs)

    def chip_at(self, offset):
        return turn_order((self.place + (offset + self.n)) & (self.n - 1), self.n)

    def split(self, grad):
        parts = grad.reshape(self.n, 2, grad.shape[0] // (2 * self.n), grad.shape[1])
        return tuple(
            lax.dynamic_index_in_dim(parts, core, 1, keepdims=False).reshape(-1, grad.shape[1])
            for core in (self.core, 1 - self.core)
        )

    def reduce_scatter(self, mine, theirs, after, before={}):
        n, columns = self.n, mine.shape[1]
        rows = mine.shape[0] // n
        cut = rows // 2
        far = n // 2

        def send(step, move, *pair):
            pair = lax.optimization_barrier(tuple(t.astype(BFLOAT) for t in pair))
            pair = before[step](pair) if step in before else pair
            arrived = tuple(m(t) for m, t in zip(move, pair))
            return after[step](arrived) if step in after else arrived

        mine = mine.reshape(n, rows, columns)
        came = send(0, (self.twin,), theirs)[0].reshape(n, rows, columns)

        def here(offset):
            at = (self.chip_at(offset), 0, 0)
            own, twin = (lax.dynamic_slice(t, at, (1, rows, columns))[0] for t in (mine, came))
            return own.astype(FLOAT) + twin.astype(FLOAT)

        both = (self.up, self.down)
        split = here(far)
        going_up, going_down = send(1, both, split[:cut], split[cut:])
        for step in range(2, far + 1):
            up_sum, down_sum = here(far + 1 - step), here(step - far - 1)
            going_up, going_down = going_up.astype(FLOAT), going_down.astype(FLOAT)
            if step == 2:
                going_up = jnp.concatenate([up_sum[:cut] + going_up, up_sum[cut:]], axis=0)
                going_down = jnp.concatenate([down_sum[:cut], down_sum[cut:] + going_down], axis=0)
            else:
                going_up, going_down = up_sum + going_up, down_sum + going_down
            going_up, going_down = send(step, both, going_up, going_down)
        return here(0) + going_up.astype(FLOAT) + going_down.astype(FLOAT)

    def all_gather(self, shards, before):
        n = self.n
        fulls = [unwritten((n, 2) + shard.shape, shard.dtype) for shard in shards]

        def put(i, offset, block, row=0):
            chip = self.chip_at(offset)
            for core, part in ((self.core, block), (1 - self.core, self.twin(block))):
                fulls[i] = lax.dynamic_update_slice(
                    fulls[i], part[None, None], (chip, core, row, 0)
                )

        moving = [(shard, shard) for shard in shards]
        for step in range(1, n // 2 + 1):
            if step in before:
                moving = before[step](moving)
            last = step == n // 2
            arrived = []
            for below, above in moving:
                cut = below.shape[0] // 2
                if last:
                    below, above = below[:cut], above[cut:]
                arrived.append((self.up(below), self.down(above)))
            for i, (below, above) in enumerate(moving):
                if step == 1:
                    put(i, 0, shards[i])
                elif step <= n // 2:
                    put(i, 1 - step, below)
                    put(i, step - 1, above)
            moving = arrived
        for i, (below, above) in enumerate(moving):
            put(i, n // 2, below)
            put(i, n // 2, above, below.shape[0])
        return [full.reshape(-1, full.shape[-1]) for full in fulls]


def unwritten(shape, dtype):
    return pl.pallas_call(
        lambda out_ref: None,
        out_specs=pl.BlockSpec(memory_space=pl.ANY),
        out_shape=jax.ShapeDtypeStruct(shape, dtype),
        name="unwritten",
    )()


def tie(value, *others):
    return lax.optimization_barrier((value,) + others)[0]


def swap(x):
    return lax.ppermute(x, "tensor", [(0, 1), (1, 0)])


def gather_rows(part, ways, axis=0):
    if ways != 2:
        return lax.all_gather(part, "tensor", axis=axis, tiled=True)
    came = swap(part)
    first = lax.axis_index("tensor") == 0
    return jnp.concatenate(
        [jnp.where(first, part, came), jnp.where(first, came, part)], axis=axis
    )


def per_device(
    ways, groups,
    tokens, cotangent, lengths,
    qkv_weight, proj_weight, up_weight, down_weight, small_params,
    qkv_first, proj_first, up_first, down_first, small_first,
    qkv_second, proj_second, up_second, down_second, small_second,
):
    ring = Ring(groups)
    tensor_rank = lax.axis_index("tensor")
    in_rows = qkv_weight.shape[0]
    local_width = qkv_weight.shape[2]
    hidden_width = up_weight.shape[1]
    pairs = local_width // PAIR
    own_rows = tokens.shape[0]
    row_count = own_rows * ways
    small_rows = small_params.shape[0]
    qkv_width = 3 * local_width
    att_width = qkv_width + local_width

    def pair_major(t):
        return (
            t.reshape(t.shape[0], 3, pairs, PAIR)
            .transpose(0, 2, 1, 3)
            .reshape(t.shape[0], qkv_width)
        )

    def from_pair_major(t):
        return (
            t.reshape(t.shape[0], pairs, 3, PAIR)
            .transpose(0, 2, 1, 3)
            .reshape(t.shape[0], 3, local_width)
        )

    small_here = gather_rows(small_params, ways, axis=1).T
    small_high = lax.reduce_precision(small_here, 8, 7)
    small_shard = jnp.concatenate(
        [
            small_high.astype(BFLOAT),
            (small_here - small_high).astype(BFLOAT),
            jnp.zeros((in_rows, PAIR - 2 * small_rows), BFLOAT),
        ],
        axis=1,
    )
    up_shard = up_weight.astype(BFLOAT)
    down_shard = jnp.concatenate([down_weight.T.astype(BFLOAT), small_shard], axis=1)
    att_shard = jnp.concatenate(
        [pair_major(qkv_weight.astype(BFLOAT)), proj_weight.T.astype(BFLOAT)], axis=1
    )
    both_in = jnp.stack([tokens, cotangent])
    up_shard, both_in = lax.optimization_barrier((up_shard, both_in))
    both_in = lax.all_gather(both_in, "tensor", axis=1, tiled=True)
    rows_in, dy = both_in[0], both_in[1]
    up_full, down_full = ring.all_gather([up_shard, down_shard], {})
    small = down_full[:, hidden_width:hidden_width + 2 * small_rows].astype(FLOAT).T
    small = small[:small_rows] + small[small_rows:]
    att_shard, up_full, down_full = lax.optimization_barrier((att_shard, up_full, down_full))
    att_full = lax.all_gather(att_shard, "dp", axis=0, tiled=True)

    bias_qkv = pair_major(
        lax.dynamic_slice_in_dim(small[4:7], tensor_rank * local_width, local_width, 1)[None]
    )[0]
    bias_up = lax.dynamic_slice_in_dim(
        small[8:12].reshape(4 * D), tensor_rank * hidden_width, hidden_width, 0
    )

    inputs = rows_in.astype(FLOAT)
    average = jnp.mean(inputs, axis=-1, keepdims=True)
    centred = inputs - average
    variance = jnp.mean(centred * centred, axis=-1, keepdims=True)
    inv_dev = lax.rsqrt(variance + EPS_NORM)
    xhat = centred * inv_dev
    normed_a = (xhat * small[0] + small[1]).astype(BFLOAT)
    normed_m = (xhat * small[2] + small[3]).astype(BFLOAT)

    own_at = tensor_rank * own_rows
    cuts = [(own_rows - own_at, own_rows), (own_at, own_rows)] if ways == 2 else [(0, row_count)]
    rows_of = lambda t, cut: lax.dynamic_slice_in_dim(t, cut[0], cut[1], 0)

    start, position = layout(lengths[0], row_count)
    keep, left, right = rotary_tables(position)
    out_bias_grad = jnp.sum(cotangent, axis=0, dtype=FLOAT)[None]
    normed_m, keep, left, right, out_bias_grad = lax.optimization_barrier(
        (normed_m, keep, left, right, out_bias_grad)
    )

    out_m, d_m, mlp_mine, mlp_theirs, up_bias_grad = mlp(
        normed_m, dy, up_full, down_full, bias_up[None], ring.core[None], ring.n
    )
    up_rows = lax.dynamic_update_slice_in_dim(
        jnp.zeros((4 * D,), FLOAT), up_bias_grad[0], tensor_rank * hidden_width, 0
    ).reshape(4, D)
    normed_a, out_m, up_rows = lax.optimization_barrier((normed_a, out_m, up_rows))
    qkv_full, proj_t = att_full[:, :qkv_width], att_full[:, qkv_width:]
    work = [
        (mm(normed_a, qkv_full) + bias_qkv).astype(BFLOAT),
        mm(dy, proj_t).astype(BFLOAT),
        (),
    ]

    def attend_after(pair, arrived):
        if pair < pairs:
            work[0], arrived = lax.optimization_barrier((work[0], arrived))
            work[2] = attention(
                pair, work[0], work[1], keep, left, right, start[None], tuple(work[2])
            )
        return arrived

    steps = {i: functools.partial(attend_after, i) for i in range(ring.n // 2)}
    mlp_own = ring.reduce_scatter(mlp_mine, mlp_theirs, steps)
    attended, d_qkv = work[2]
    proj_grad = mm_tn(dy, attended).astype(BFLOAT)
    qkv_grad = mm_tn(normed_a, d_qkv).astype(BFLOAT)
    att_mine, att_theirs = ring.split(jnp.concatenate([qkv_grad, proj_grad], axis=1))
    attended, att_theirs = lax.optimization_barrier((attended, att_theirs))
    att_theirs, mlp_own = lax.optimization_barrier((att_theirs, mlp_own))

    out_part = [mm_nt(rows_of(attended, c), proj_t) + rows_of(out_m, c) for c in cuts]
    d_m = [rows_of(d_m, c) for c in cuts]
    held = {}
    if ways == 2:
        held["out"] = lax.all_gather(out_part[0].astype(BFLOAT), "tensor")

    def norm_work(arrived):
        arrived, grad = lax.optimization_barrier((arrived, d_qkv))
        held["d_a"] = [mm_nt(rows_of(grad, c), qkv_full) for c in cuts]
        held["sums"] = [
            sums(ds) for ds in (held["d_a"], d_m) for sums in (with_hat, plain)
        ]
        held["e"] = [a * small[0] + m * small[2] for a, m in zip(held["d_a"], d_m)]
        return arrived

    with_hat = lambda ds: sum(
        jnp.sum(d * rows_of(xhat, c), axis=0)[None] for d, c in zip(ds, cuts)
    )
    plain = lambda ds: sum(jnp.sum(d, axis=0)[None] for d in ds)

    def small_sums(grad, norm_sums):
        qkv_rows = lax.dynamic_update_slice_in_dim(
            jnp.zeros((3, D), FLOAT),
            from_pair_major(jnp.sum(grad, axis=0, dtype=FLOAT)[None])[0],
            tensor_rank * local_width,
            1,
        )
        return jnp.concatenate(
            norm_sums + [qkv_rows, out_bias_grad, up_rows, out_bias_grad],
            axis=0,
        )

    def out_work(arrived):
        if ways == 2:
            arrived, held["out"] = lax.optimization_barrier((arrived, held["out"]))
        arrived, held["late"], held["mlp"] = lax.optimization_barrier(
            (arrived, (d_qkv, held["sums"]), mlp_own)
        )
        return arrived

    def last_send(pair):
        if ways == 2:
            pair, e_other = lax.optimization_barrier((pair, held["e"][0].astype(BFLOAT)))
            held["e_came"] = swap(e_other)
        return pair

    last = ring.n // 2
    att_own = ring.reduce_scatter(
        att_mine, att_theirs, {0: norm_work, last: out_work}, {last: last_send}
    )
    if ways == 2:
        out_came = lax.dynamic_index_in_dim(held["out"], 1 - tensor_rank, 0, keepdims=False)
        summed = out_came.astype(FLOAT) + out_part[1]
        held["e_came"] = tie(held["e_came"], held["late"])
        e_own = held["e_came"].astype(FLOAT) + held["e"][1]
    else:
        summed, e_own = (
            lax.psum_scatter(
                part[0].astype(BFLOAT), "tensor", scatter_dimension=0, tiled=True
            ).astype(FLOAT)
            for part in (out_part, held["e"])
        )
    own_inputs = tokens.astype(FLOAT)
    block_out = (own_inputs + summed + small[7] + small[12]).astype(BFLOAT)
    own_hat = rows_of(xhat, (own_at, own_rows))
    own_inv = rows_of(inv_dev, (own_at, own_rows))
    token_grad = cotangent.astype(FLOAT) + own_inv * (
        e_own
        - jnp.mean(e_own, axis=-1, keepdims=True)
        - own_hat * jnp.mean(e_own * own_hat, axis=-1, keepdims=True)
    )

    held["small"] = small_sums(*held["late"])
    small_both = held["small"] + swap(held["small"]) if ways == 2 else lax.psum(held["small"], "tensor")
    reach = 1
    while reach < groups:
        if reach == 4 and ways == 2:
            small_both = tie(small_both, held["e_came"])
        small_both += lax.ppermute(small_both, "dp", [(i, i ^ reach) for i in range(groups)])
        reach *= 2
    small_width = small_params.shape[1]
    small_grad = lax.dynamic_slice_in_dim(
        small_both,
        (lax.axis_index("dp") * ways + tensor_rank) * small_width,
        small_width,
        1,
    )
    mlp_parts = held["mlp"].reshape(in_rows, -1, 2, mlp_chunk(hidden_width))
    qkv_owned = from_pair_major(att_own[:, :qkv_width])
    proj_owned = att_own[:, qkv_width:att_width].T
    up_owned = mlp_parts[:, :, 0].reshape(in_rows, hidden_width)
    down_owned = mlp_parts[:, :, 1].reshape(in_rows, hidden_width).T
    qkv_new = adamw(qkv_weight, qkv_first, qkv_second, qkv_owned, D ** (-0.5), DECAY)
    proj_new = adamw(proj_weight, proj_first, proj_second, proj_owned, (D // 64) ** (-0.5), DECAY)
    up_new = adamw(up_weight, up_first, up_second, up_owned, D ** (-0.5), DECAY)
    down_new = adamw(down_weight, down_first, down_second, down_owned, FF ** (-0.5), DECAY)
    small_new = adamw(small_params, small_first, small_second, small_grad, SMALL_RATE, 0.0)
    return (block_out, token_grad) + qkv_new + proj_new + up_new + down_new + small_new


def solution(mesh):
    rows = P(("dp", "tensor"), None)
    weights = (P("dp", None, "tensor"), P("tensor", "dp"), P("dp", "tensor"), P("tensor", "dp"))
    small = P(None, ("dp", "tensor"))
    return jax.shard_map(
        functools.partial(per_device, mesh.shape["tensor"], mesh.shape["dp"]),
        mesh=mesh,
        in_specs=(rows, rows, P("dp", None)) + 3 * (weights + (small,)),
        out_specs=(rows, rows) + tuple(w for w in weights + (small,) for _ in range(3)),
        check_vma=False,
    )
```
